128 devices in a mesh: row: 8 (over z, core), col: 16 (over y, x).
Axes of the slice: x: 4, y: 4, z: 4, core: 2. Of those that a mesh axis runs over, the one named last changes fastest.
Arguments:
- vectors: bfloat16 [32768, 2048], P(('row', 'col')), may hold values from -6 to 6
- block_count: int32 [256], P(('row', 'col')), may hold values from 1 to 5, as said below
- block_cols: int32 [256, 5], P(('row', 'col')), may hold values from 0 to 255, as said below
- blocks: bfloat16 [256, 5, 128, 128], P(('row', 'col')), as said below
Outputs:
- hamiltonian_proj: float32 [2048, 2048], P('row', 'col')
- intersection_proj: float32 [2048, 2048], P('row', 'col')
The draws below stay inside these ranges and needn't reach their ends.
Inputs may be any that keep to these rules, and one draw needn't show every extreme that they name: `block_count`: every block row stores its diagonal block; some block row stores all 5 slots. `block_cols`: slots 0 to block_count[i] - 1 of block row i hold distinct block columns, each at most 2 block rows from i in the periodic order modulo 256; the pattern is symmetric; the remaining slots hold i. `blocks`: the matrix H is symmetric; slots beyond block_count hold zeros.
All inputs are finite; a program needn't handle non-finite values.
Results may differ from the reference program's by a relative error of at most 0.0049.
Values may be sent and summed in bfloat16 or wider, within the bound.
A program may use at most 128 MiB of HBM per device.

```python
import math
import jax
import jax.numpy as jnp

BLK = 128
VEC = 2048
REACH = 2
DEGREE = 8
KMAX = 5
NB = 256
NROWS = 32768


def coupling_pattern(key):
    chosen = jax.random.randint(jax.random.fold_in(key, 11), (NB, REACH), 0, 5)
    row_ids = jnp.arange(NB, dtype=jnp.int32)[:, None]
    offset_ids = jnp.arange(1, REACH + 1, dtype=jnp.int32)[None, :]
    forced = jnp.logical_or(row_ids == 0, row_ids + offset_ids == NB)
    return jnp.where(jnp.logical_or(chosen < 3, forced), 1, 0).astype(jnp.int32)


def slot_layout(key):
    present = coupling_pattern(key)
    row_ids = jnp.arange(NB, dtype=jnp.int32)
    flags = []
    columns = []
    for shift in range(-REACH, REACH + 1):
        if shift == 0:
            flags.append(jnp.ones((NB,), jnp.int32))
        elif shift > 0:
            flags.append(present[:, shift - 1])
        else:
            flags.append(jnp.roll(present[:, -shift - 1], -shift))
        columns.append(jnp.mod(row_ids + shift, NB).astype(jnp.int32))
    flags = jnp.stack(flags, 1)
    columns = jnp.stack(columns, 1)
    order = jnp.argsort(1 - flags, axis=1, stable=True)
    counted = jnp.sum(flags, 1).astype(jnp.int32)
    picked = jnp.take_along_axis(columns, order, 1)
    slot_ids = jnp.arange(KMAX, dtype=jnp.int32)[None, :]
    picked = jnp.where(slot_ids < counted[:, None], picked, row_ids[:, None]).astype(jnp.int32)
    return (flags, order, counted, picked)


def draw_block_count(key, part):
    layout = slot_layout(key)
    return layout[2]


def draw_block_cols(key, part):
    layout = slot_layout(key)
    return layout[3]


def draw_blocks(key, part):
    flags, order, counted, picked = slot_layout(key)
    key = jax.random.fold_in(key, 5)
    spread = 1.0 / math.sqrt(BLK * KMAX)
    raw_pairs = jax.random.normal(key, (NB, REACH, BLK, BLK), jnp.float32)
    raw_diag = jax.random.normal(jax.random.fold_in(key, 1), (NB, BLK, BLK), jnp.float32)
    diagonal = (raw_diag + jnp.swapaxes(raw_diag, 1, 2)) * (spread / math.sqrt(2.0))
    stacked = []
    for shift in range(-REACH, REACH + 1):
        if shift == 0:
            stacked.append(diagonal)
        elif shift > 0:
            stacked.append(raw_pairs[:, shift - 1] * spread)
        else:
            stacked.append(jnp.roll(jnp.swapaxes(raw_pairs[:, -shift - 1], 1, 2) * spread, -shift, axis=0))
    stacked = jnp.stack(stacked, 1) * flags[:, :, None, None].astype(jnp.float32)
    ordered = jnp.take_along_axis(stacked, order[:, :, None, None], 1)
    slot_ids = jnp.arange(KMAX, dtype=jnp.int32)[None, :]
    keep = (slot_ids < counted[:, None]).astype(jnp.float32)
    return (ordered * keep[:, :, None, None]).astype(jnp.bfloat16)


def block_scale(stream_key, extent, shards, low, largest):
    gain, own = 1.0, jax.random.fold_in(stream_key, 6)
    for position, shards_of in shards:
        steps = jnp.exp(jax.random.uniform(jax.random.fold_in(own, position), (shards_of,), jnp.float32, low / len(shards), largest / len(shards)))
        gain = gain * jnp.repeat(steps, extent[position] // shards_of).reshape([-1 if axis == position else 1 for axis in range(len(extent))])
    return gain


def gaussian(key, extent, scale, most, cuts=(), kind=jnp.bfloat16):
    values = scale * jax.random.normal(key, extent, jnp.float32)
    if cuts:
        values = values * block_scale(key, extent, cuts, -0.22, 0.18)
    return jnp.clip(values, -most, most).astype(kind)


def setup_inputs(seed: int = 0) -> dict:
    splits = jax.random.split(jax.random.key(seed), 5)
    return {
        "vectors": gaussian(splits[0], (NROWS, VEC), 1.0, 6.0, ((0, 128),)),
        "block_count": draw_block_count(jax.random.fold_in(splits[4], 71), 0),
        "block_cols": draw_block_cols(jax.random.fold_in(splits[4], 71), 0),
        "blocks": draw_blocks(jax.random.fold_in(splits[4], 71), 0),
    }


def apply_operator(source, block_count, block_cols, blocks):
    tile_rows = source.reshape(NB, BLK, VEC)
    slot_ids = jnp.arange(KMAX, dtype=jnp.int32)
    in_use = slot_ids[None, :] < block_count[:, None]
    summed = jnp.zeros((NB, BLK, VEC), jnp.float32)
    for slot in range(KMAX):
        gathered = tile_rows[block_cols[:, slot]].astype(jnp.float32)
        weight = jnp.where(in_use[:, slot][:, None, None], blocks[:, slot].astype(jnp.float32), 0.0)
        summed = summed + jnp.einsum('iab,ibm->iam', weight, gathered)
    return summed.reshape(NROWS, VEC)

def reference(vectors, block_count, block_cols, blocks):
    previous = vectors
    current = ((apply_operator(previous, block_count, block_cols, blocks) - 0.25 * previous.astype(jnp.float32)) / 1.75).astype(jnp.bfloat16)
    for sweep_index in range(DEGREE - 1):
        product = apply_operator(current, block_count, block_cols, blocks)
        following = (2.0 * (product - 0.25 * current.astype(jnp.float32)) / 1.75 - previous.astype(jnp.float32)).astype(jnp.bfloat16)
        previous = current
        current = following
    applied = apply_operator(current, block_count, block_cols, blocks).astype(jnp.bfloat16)
    row_scale = 1.0 / math.sqrt(NROWS)
    hamiltonian_proj = jnp.dot(current.T, applied, preferred_element_type=jnp.float32) * row_scale
    intersection_proj = jnp.dot(current.T, current, preferred_element_type=jnp.float32) * row_scale
    return (hamiltonian_proj, intersection_proj)
```

```python
import functools
import math

import jax
import jax.numpy as jnp
from jax import lax
from jax.experimental import pallas as pl
from jax.experimental.pallas import tpu as pltpu
from jax.sharding import PartitionSpec as P

DEGREE = 8
MESH = pl.DeviceIdType.MESH

filter_center = 0.25
filter_half = 1.75


def band_tiles(blocks, block_cols, block_count, first_block, total_blocks):
    local_blocks = blocks.shape[0]
    slot_count = blocks.shape[1]
    reach_blocks = (slot_count - 1) // 2
    relative = jnp.mod(block_cols - first_block + reach_blocks, total_blocks)
    row_ids = jnp.arange(local_blocks, dtype=jnp.int32)
    slot_ids = jnp.arange(slot_count, dtype=jnp.int32)
    in_use = slot_ids[None, :] < block_count[:, None]
    matches = jnp.logical_and(
        relative[:, :, None] == row_ids[:, None, None] + slot_ids[None, None, :], in_use[:, :, None]
    )
    selector = jnp.where(matches, 1.0, 0.0).astype(jnp.bfloat16)
    return jnp.einsum(
        "iko,ikab->ioab", selector, blocks, preferred_element_type=jnp.float32
    ).astype(jnp.bfloat16)


def filter_kernel(n_row, v_ref, h_ref, f_ref, a_ref, band, ext0, ext1, send_sem, recv_sem):
    rows = v_ref.shape[0]
    blk = h_ref.shape[2]
    edge = 2 * blk
    pairs = rows // edge
    me = lax.axis_index("row")
    up, down = lax.rem(me + 1, n_row), lax.rem(me + n_row - 1, n_row)

    barrier = pltpu.get_barrier_semaphore()
    for neighbour in (up, down):
        pl.semaphore_signal(barrier, inc=1, device_id={"row": neighbour}, device_id_type=MESH)
    pl.semaphore_wait(barrier, 2)

    ext = (ext0, ext1)

    def send(slot):
        copies = (
            pltpu.make_async_remote_copy(
                src_ref=ext[slot].at[pl.ds(rows, edge)],
                dst_ref=ext[slot].at[pl.ds(0, edge)],
                send_sem=send_sem.at[slot, 0],
                recv_sem=recv_sem.at[slot, 0],
                device_id={"row": up},
                device_id_type=MESH,
            ),
            pltpu.make_async_remote_copy(
                src_ref=ext[slot].at[pl.ds(edge, edge)],
                dst_ref=ext[slot].at[pl.ds(rows + edge, edge)],
                send_sem=send_sem.at[slot, 1],
                recv_sem=recv_sem.at[slot, 1],
                device_id={"row": down},
                device_id_type=MESH,
            ),
        )
        for copy in copies:
            copy.start()
        return copies

    ext0[pl.ds(edge, rows), :] = v_ref[...]
    copies = send(0)

    def build(j, carry):
        for half in range(2):
            i = 2 * j + half
            for offset in range(5):
                band[j, pl.ds(half * blk, blk), pl.ds((offset + half) * blk, blk)] = h_ref[i, offset]
            band[j, pl.ds(half * blk, blk), pl.ds((5 - 5 * half) * blk, blk)] = jnp.zeros(
                (blk, blk), jnp.bfloat16
            )
        return carry

    lax.fori_loop(0, pairs, build, 0)

    for step in range(DEGREE + 1):
        now, later = step % 2, (step + 1) % 2
        source, target = ext[now], ext[later]

        def pair(j, carry):
            base = pl.multiple_of(j * edge, edge)
            own = pl.ds(pl.multiple_of(base + edge, edge), edge)
            product = jnp.dot(
                band[j], source[pl.ds(base, 3 * edge), :], preferred_element_type=jnp.float32
            )
            if step == DEGREE:
                a_ref[pl.ds(base, edge), :] = product.astype(jnp.bfloat16)
                return carry
            shifted = product - filter_center * source[own, :].astype(jnp.float32)
            if step == 0:
                result = shifted / filter_half
            else:
                result = 2.0 * shifted / filter_half - target[own, :].astype(jnp.float32)
            result = result.astype(jnp.bfloat16)
            target[own, :] = result
            if step == DEGREE - 1:
                f_ref[pl.ds(base, edge), :] = result
            return carry

        lax.fori_loop(1, pairs - 1, pair, 0, unroll=2)
        for copy in copies:
            copy.wait()
        pair(0, 0)
        pair(pairs - 1, 0)
        if step < DEGREE:
            copies = send(later)


def chebyshev(vectors, tiles, n_row):
    rows, width = vectors.shape
    blk = tiles.shape[2]
    pairs = rows // (2 * blk)
    vmem = pl.BlockSpec(memory_space=pltpu.VMEM)
    return pl.pallas_call(
        functools.partial(filter_kernel, n_row),
        out_shape=[jax.ShapeDtypeStruct((rows, width), jnp.bfloat16)] * 2,
        in_specs=[vmem, vmem],
        out_specs=[vmem, vmem],
        scratch_shapes=[
            pltpu.VMEM((pairs, 2 * blk, 6 * blk), jnp.bfloat16),
            pltpu.VMEM((rows + 4 * blk, width), jnp.bfloat16),
            pltpu.VMEM((rows + 4 * blk, width), jnp.bfloat16),
            pltpu.SemaphoreType.DMA((2, 2)),
            pltpu.SemaphoreType.DMA((2, 2)),
        ],
        compiler_params=pltpu.CompilerParams(
            collective_id=0, has_side_effects=True, vmem_limit_bytes=40 * 1024 * 1024
        ),
    )(vectors, tiles)


def body(vectors, block_count, block_cols, blocks):
    n_row = lax.axis_size("row")
    n_col = lax.axis_size("col")
    local_blocks = blocks.shape[0]
    total_blocks = local_blocks * n_row * n_col
    first_block = lax.axis_index(("row", "col")) * local_blocks
    tiles = band_tiles(blocks, block_cols, block_count, first_block, total_blocks)
    row_scale = 1.0 / math.sqrt(vectors.shape[0] * n_row * n_col)
    width = vectors.shape[1] // n_col
    columns = lax.all_to_all(vectors, "col", split_axis=1, concat_axis=0, tiled=True)
    all_tiles = lax.all_gather(tiles, "col", axis=0, tiled=True)
    filtered, applied = chebyshev(columns, all_tiles, n_row)
    paired = jnp.concatenate([applied, filtered], axis=1)
    partial_terms = lax.dot_general(
        lax.all_gather(filtered, "col", axis=1, tiled=True),
        paired,
        (((0,), (0,)), ((), ())),
        preferred_element_type=jnp.float32,
    )
    summed = lax.psum_scatter(partial_terms, "row", scatter_dimension=0, tiled=True)
    hamiltonian_proj = summed[:, :width] * row_scale
    intersection_proj = summed[:, width:] * row_scale
    return (hamiltonian_proj, intersection_proj)


def solution(mesh):
    in_specs = (
        P(("row", "col"), None),
        P(("row", "col")),
        P(("row", "col"), None),
        P(("row", "col"), None, None, None),
    )
    out_specs = (P("row", "col"), P("row", "col"))
    return jax.shard_map(body, mesh=mesh, in_specs=in_specs, out_specs=out_specs, check_vma=False)
```

```python
import functools
import math

import jax
import jax.numpy as jnp
from jax import lax
from jax.experimental import pallas as pl
from jax.experimental.pallas import tpu as pltpu
from jax.sharding import PartitionSpec as P

DEGREE = 8
MESH = pl.DeviceIdType.MESH

filter_center = 0.25
filter_half = 1.75


def band_tiles(blocks, block_cols, block_count, first_block, total_blocks):
    local_blocks = blocks.shape[0]
    slot_count = blocks.shape[1]
    reach_blocks = (slot_count - 1) // 2
    relative = jnp.mod(block_cols - first_block + reach_blocks, total_blocks)
    row_ids = jnp.arange(local_blocks, dtype=jnp.int32)
    slot_ids = jnp.arange(slot_count, dtype=jnp.int32)
    in_use = slot_ids[None, :] < block_count[:, None]
    matches = jnp.logical_and(
        relative[:, :, None] == row_ids[:, None, None] + slot_ids[None, None, :], in_use[:, :, None]
    )
    selector = jnp.where(matches, 1.0, 0.0).astype(jnp.bfloat16)
    return jnp.einsum(
        "iko,ikab->ioab", selector, blocks, preferred_element_type=jnp.float32
    ).astype(jnp.bfloat16)


def filter_kernel(n_row, v_ref, h_ref, f_ref, a_ref, band, ext0, ext1, send_sem, recv_sem):
    rows = v_ref.shape[0]
    blk = h_ref.shape[2]
    edge = 2 * blk
    pairs = rows // edge
    me = lax.axis_index("row")
    up, down = lax.rem(me + 1, n_row), lax.rem(me + n_row - 1, n_row)

    barrier = pltpu.get_barrier_semaphore()
    for neighbour in (up, down):
        pl.semaphore_signal(barrier, inc=1, device_id={"row": neighbour}, device_id_type=MESH)
    pl.semaphore_wait(barrier, 2)

    ext = (ext0, ext1)

    def send(slot):
        copies = (
            pltpu.make_async_remote_copy(
                src_ref=ext[slot].at[pl.ds(rows, edge)],
                dst_ref=ext[slot].at[pl.ds(0, edge)],
                send_sem=send_sem.at[slot, 0],
                recv_sem=recv_sem.at[slot, 0],
                device_id={"row": up},
                device_id_type=MESH,
            ),
            pltpu.make_async_remote_copy(
                src_ref=ext[slot].at[pl.ds(edge, edge)],
                dst_ref=ext[slot].at[pl.ds(rows + edge, edge)],
                send_sem=send_sem.at[slot, 1],
                recv_sem=recv_sem.at[slot, 1],
                device_id={"row": down},
                device_id_type=MESH,
            ),
        )
        for copy in copies:
            copy.start()
        return copies

    ext0[pl.ds(edge, rows), :] = v_ref[...]
    copies = send(0)

    def build(j, carry):
        for half in range(2):
            i = 2 * j + half
            for offset in range(5):
                band[j, pl.ds(half * blk, blk), pl.ds((offset + half) * blk, blk)] = h_ref[i, offset]
            band[j, pl.ds(half * blk, blk), pl.ds((5 - 5 * half) * blk, blk)] = jnp.zeros(
                (blk, blk), jnp.bfloat16
            )
        return carry

    lax.fori_loop(0, pairs, build, 0)

    for step in range(DEGREE + 1):
        now, later = step % 2, (step + 1) % 2
        source, target = ext[now], ext[later]

        def pair(j, carry):
            base = pl.multiple_of(j * edge, edge)
            own = pl.ds(pl.multiple_of(base + edge, edge), edge)
            product = jnp.dot(
                band[j], source[pl.ds(base, 3 * edge), :], preferred_element_type=jnp.float32
            )
            if step == DEGREE:
                a_ref[pl.ds(base, edge), :] = product.astype(jnp.bfloat16)
                return carry
            shifted = product - filter_center * source[own, :].astype(jnp.float32)
            if step == 0:
                result = shifted / filter_half
            else:
                result = 2.0 * shifted / filter_half - target[own, :].astype(jnp.float32)
            result = result.astype(jnp.bfloat16)
            target[own, :] = result
            if step == DEGREE - 1:
                f_ref[pl.ds(base, edge), :] = result
            return carry

        lax.fori_loop(1, pairs - 1, pair, 0, unroll=7)
        for copy in copies:
            copy.wait()
        pair(0, 0)
        pair(pairs - 1, 0)
        if step < DEGREE:
            copies = send(later)


def chebyshev(vectors, tiles, n_row):
    rows, width = vectors.shape
    blk = tiles.shape[2]
    pairs = rows // (2 * blk)
    vmem = pl.BlockSpec(memory_space=pltpu.VMEM)
    return pl.pallas_call(
        functools.partial(filter_kernel, n_row),
        out_shape=[jax.ShapeDtypeStruct((rows, width), jnp.bfloat16)] * 2,
        in_specs=[vmem, vmem],
        out_specs=[vmem, vmem],
        scratch_shapes=[
            pltpu.VMEM((pairs, 2 * blk, 6 * blk), jnp.bfloat16),
            pltpu.VMEM((rows + 4 * blk, width), jnp.bfloat16),
            pltpu.VMEM((rows + 4 * blk, width), jnp.bfloat16),
            pltpu.SemaphoreType.DMA((2, 2)),
            pltpu.SemaphoreType.DMA((2, 2)),
        ],
        compiler_params=pltpu.CompilerParams(
            collective_id=0, has_side_effects=True, vmem_limit_bytes=40 * 1024 * 1024
        ),
    )(vectors, tiles)


def project_kernel(scale, f_ref, a_ref, h_out, g_out, fown, aown, ft, away, keep, core_in, share, x_in, done, fin,
                   fx_s, fx_r, ax_s, ax_r, up_s, up_r, dn_s, dn_r, core_s, core_r, x_s, x_r, z_s, z_r):
    part = f_ref.shape[0] // 4
    width = f_ref.shape[1]
    half = 2 * width
    row, col = lax.axis_index("row"), lax.axis_index("col")
    z, k, y, x = row // 2, row % 2, col // 4, col % 4

    def on_x(d):
        return {"col": y * 4 + (x + d) % 4}

    def on_y(d):
        return {"col": ((y + d) % 4) * 4 + x}

    def on_z(d):
        return {"row": ((z + d) % 4) * 2 + k}

    partner = {"row": z * 2 + 1 - k}

    def remote(src, dst, send, recv, device):
        return pltpu.make_async_remote_copy(
            src_ref=src, dst_ref=dst, send_sem=send, recv_sem=recv, device_id=device, device_id_type=MESH
        )

    barrier = pltpu.get_barrier_semaphore()
    for device in [on_x(1), on_x(2), on_x(3), on_y(1), on_y(3), on_z(1), on_z(2), on_z(3), partner]:
        pl.semaphore_signal(barrier, inc=1, device_id=device, device_id_type=MESH)
    pl.semaphore_wait(barrier, 9)

    def lanes(i):
        return pl.ds(pl.multiple_of(i * width, width), width)

    def x_copy(src, dst, sems, d):
        rows = pl.ds(pl.multiple_of(((x + d) % 4) * part, part), part)
        return remote(src.at[rows], dst.at[:, lanes(x)], sems[0].at[d - 1], sems[1].at[d - 1], on_x(d))

    f_copies = {d: x_copy(f_ref, fown, (fx_s, fx_r), d) for d in (1, 2, 3)}
    a_copies = {d: x_copy(a_ref, aown, (ax_s, ax_r), d) for d in (1, 2, 3)}

    def y_copy(from_slot, to_slot, d, index, up):
        piece = pl.ds(pl.multiple_of(((x + d) % 4) * width, width), width)
        sems = (up_s, up_r) if up else (dn_s, dn_r)
        return remote(ft.at[from_slot, piece], ft.at[to_slot, piece], sems[0].at[index], sems[1].at[index],
                      on_y(1 if up else 3))

    own_up = [y_copy(0, 1, d, d, True) for d in range(4)]
    own_dn = [y_copy(0, 2, d, d, False) for d in range(4)]
    fwd_up = {0: y_copy(1, 3, 0, 4, True), 1: y_copy(1, 3, 1, 5, True)}
    fwd_dn = {3: y_copy(2, 3, 3, 4, False), 2: y_copy(2, 3, 2, 5, False)}

    def spread(d):
        source = (x + d) % 4
        piece = pl.ds(pl.multiple_of(source * width, width), width)
        ft[0, piece, :] = fown[:, lanes(source)].T
        own_up[d].start()
        own_dn[d].start()

    for d in (1, 3, 2):
        f_copies[d].start()
    mine = pl.ds(pl.multiple_of(x * part, part), part)
    fown[:, lanes(x)] = f_ref[mine, :]
    spread(0)
    aown[:, lanes(x)] = a_ref[mine, :]
    f_copies[1].wait_recv()
    spread(3)
    f_copies[3].wait_recv()
    spread(1)
    for d in (1, 3, 2):
        a_copies[d].start()
    own_up[0].wait_recv()
    fwd_up[0].start()
    f_copies[2].wait_recv()
    spread(2)
    own_up[1].wait_recv()
    fwd_up[1].start()
    own_dn[3].wait_recv()
    fwd_dn[3].start()
    own_dn[2].wait_recv()
    fwd_dn[2].start()

    core_copies = [remote(away.at[j], core_in.at[j], core_s.at[j], core_r.at[j], partner) for j in range(4)]
    x_copies = [
        [
            remote(share.at[j, :, :, lanes((x + d) % 4)], x_in.at[j, d - 1], x_s.at[j, d - 1], x_r.at[j, d - 1], on_x(d))
            for d in (1, 2, 3)
        ]
        for j in range(4)
    ]

    def tile(j):
        for part_k, out in ((1 - k, away), (k, keep)):
            lhs = ft[j, pl.ds(pl.multiple_of(part_k * half, half), half), :]
            for m, rhs in enumerate((aown, fown)):
                out[j, m] = jnp.dot(lhs, rhs[...], preferred_element_type=jnp.float32).astype(out.dtype)
            if out is away:
                core_copies[j].start()

    def over_core(j):
        core_copies[j].wait_recv()
        share[j] = (keep[j] + core_in[j].astype(jnp.float32)).astype(jnp.bfloat16)
        for copy in x_copies[j]:
            copy.start()

    def z_copy(j):
        d = (y + (0, 3, 1, 2)[j] - z + 4) % 4
        return d, remote(done.at[j], fin.at[d], z_s.at[j], z_r.at[d], on_z(d))

    def over_x(j):
        for copy in x_copies[j]:
            copy.wait_recv()
        total = share[j, :, :, lanes(x)].astype(jnp.float32)
        for i in range(3):
            total = total + x_in[j, i].astype(jnp.float32)
        done[j] = total.astype(jnp.bfloat16)
        d, copy = z_copy(j)

        @pl.when(d != 0)
        def _():
            copy.start()

        @pl.when(d == 0)
        def _():
            fin[0] = done[j]

    for d in (1, 3, 2):
        a_copies[d].wait_recv()
    tile(0)
    own_up[2].wait_recv()
    own_up[3].wait_recv()
    tile(1)
    over_core(0)
    own_dn[0].wait_recv()
    own_dn[1].wait_recv()
    tile(2)
    over_core(1)
    over_x(0)
    over_core(2)
    for copy in (*fwd_up.values(), *fwd_dn.values()):
        copy.wait_recv()
    tile(3)
    over_x(1)
    over_core(3)
    over_x(2)
    over_x(3)

    for d in (1, 2, 3):
        remote(done.at[0], fin.at[d], z_s.at[0], z_r.at[d], on_z(d)).wait_recv()
    total = fin[0].astype(jnp.float32)
    for d in (1, 2, 3):
        total = total + fin[d].astype(jnp.float32)
    h_out[...] = total[0] * scale
    g_out[...] = total[1] * scale

    for copy in (*f_copies.values(), *a_copies.values(), *own_up, *own_dn, *fwd_up.values(), *fwd_dn.values(),
                 *core_copies, *(c for cs in x_copies for c in cs)):
        copy.wait_send()
    for j in range(4):
        d, copy = z_copy(j)

        @pl.when(d != 0)
        def _():
            copy.wait_send()


def project(filtered, applied, scale):
    rows, width = filtered.shape
    part = rows // 4
    wide, half = 4 * width, 2 * width
    vmem = pl.BlockSpec(memory_space=pltpu.VMEM)
    bf16 = jnp.bfloat16
    dma = pltpu.SemaphoreType.DMA
    return pl.pallas_call(
        functools.partial(project_kernel, scale),
        out_shape=[jax.ShapeDtypeStruct((half, width), jnp.float32)] * 2,
        in_specs=[vmem, vmem],
        out_specs=[vmem, vmem],
        scratch_shapes=[
            pltpu.VMEM((part, wide), bf16),
            pltpu.VMEM((part, wide), bf16),
            pltpu.VMEM((4, wide, part), bf16),
            pltpu.VMEM((4, 2, half, wide), bf16),
            pltpu.VMEM((4, 2, half, wide), jnp.float32),
            pltpu.VMEM((4, 2, half, wide), bf16),
            pltpu.VMEM((4, 2, half, wide), bf16),
            pltpu.VMEM((4, 3, 2, half, width), bf16),
            pltpu.VMEM((4, 2, half, width), bf16),
            pltpu.VMEM((4, 2, half, width), bf16),
            dma((3,)), dma((3,)), dma((3,)), dma((3,)),
            dma((6,)), dma((6,)), dma((6,)), dma((6,)),
            dma((4,)), dma((4,)), dma((4, 3)), dma((4, 3)), dma((4,)), dma((4,)),
        ],
        compiler_params=pltpu.CompilerParams(
            collective_id=1, has_side_effects=True, vmem_limit_bytes=48 * 1024 * 1024
        ),
    )(filtered, applied)


def body(vectors, block_count, block_cols, blocks):
    n_row = lax.axis_size("row")
    n_col = lax.axis_size("col")
    local_blocks = blocks.shape[0]
    total_blocks = local_blocks * n_row * n_col
    first_block = lax.axis_index(("row", "col")) * local_blocks
    tiles = band_tiles(blocks, block_cols, block_count, first_block, total_blocks)
    row_scale = 1.0 / math.sqrt(vectors.shape[0] * n_row * n_col)
    columns = lax.all_to_all(vectors, "col", split_axis=1, concat_axis=0, tiled=True)
    all_tiles = lax.all_gather(tiles, "col", axis=0, tiled=True)
    filtered, applied = chebyshev(columns, all_tiles, n_row)
    hamiltonian_proj, intersection_proj = project(filtered, applied, row_scale)
    return (hamiltonian_proj, intersection_proj)


def solution(mesh):
    in_specs = (
        P(("row", "col"), None),
        P(("row", "col")),
        P(("row", "col"), None),
        P(("row", "col"), None, None, None),
    )
    out_specs = (P("row", "col"), P("row", "col"))
    return jax.shard_map(body, mesh=mesh, in_specs=in_specs, out_specs=out_specs, check_vma=False)
```

```python
import functools
import math

import jax
import jax.numpy as jnp
from jax import lax
from jax.experimental import pallas as pl
from jax.experimental.pallas import tpu as pltpu
from jax.sharding import PartitionSpec as P

DEGREE = 8
MESH = pl.DeviceIdType.MESH

filter_center = 0.25
filter_half = 1.75


def filter_kernel(n_row, total_blocks, cols_ref, count_ref, blocks_ref, v_ref, f_ref, a_ref,
                  hg, band, ext0, ext1, halo, own_sem, v_s, v_r, h1_s, h1_r, h2_s, h2_r, e_s, e_r, halo_s, halo_r):
    edge = v_ref.shape[0]
    blk = edge // 2
    pairs = 16
    row, col = lax.axis_index("row"), lax.axis_index("col")
    y, x = col // 4, col % 4
    up, down = {"row": (row + 1) % n_row}, {"row": (row + n_row - 1) % n_row}

    def place(dy, dx):
        return ((y + dy) % 4) * 4 + (x + dx) % 4

    def remote(src, dst, send, recv, device):
        return pltpu.make_async_remote_copy(
            src_ref=src, dst_ref=dst, send_sem=send, recv_sem=recv, device_id=device, device_id_type=MESH
        )

    others = [(dy, dx) for dy in range(4) for dx in range(4) if dy or dx]
    barrier = pltpu.get_barrier_semaphore()
    for device in [up, down] + [{"col": place(dy, dx)} for dy, dx in others]:
        pl.semaphore_signal(barrier, inc=1, device_id=device, device_id_type=MESH)

    first = (row * pairs + col) * 2
    for i in range(2):
        for offset in range(3):
            tile = jnp.zeros((blk, blk), jnp.bfloat16)
            for slot in range(5):
                relative = lax.rem(cols_ref[i, slot] - first - i + total_blocks, total_blocks)
                hit = jnp.logical_and(relative == offset, slot < count_ref[i])
                tile = jnp.where(hit, blocks_ref[i, slot], tile)
            hg[col + 2, i, offset] = tile

    pl.semaphore_wait(barrier, 17)

    def lanes(i):
        return pl.ds(pl.multiple_of(i * blk, blk), blk)

    def rows_of(pair, count=1):
        return pl.ds(pl.multiple_of((pair + 2) * edge, edge), count * edge)

    def unit(h, a, b):
        return hg.at[place(b, a) + 2 if h == 0 else place(a, b) + 2, h]

    def tile_copy(h, a, b, to_a, to_b, send, recv):
        target = place(to_b, to_a) if h == 0 else place(to_a, to_b)
        return remote(unit(h, a, b), unit(h, a, b), send, recv, {"col": target})

    stage1, stage2 = [], []
    for h in range(2):
        sign = 1 if h == 0 else 3
        moves = [(0, 1), (0, 3), (4 - sign, sign)]
        stage1.append([tile_copy(h, a, 0, to, 0, h1_s.at[h, n], h1_r.at[h, n]) for n, (a, to) in enumerate(moves)])
        lists = []
        for a in range(4):
            sign = 1 if a < 2 else 3
            moves = [(0, 1), (0, 3), (4 - sign, sign)]
            lists.append([
                tile_copy(h, a, b, 0, to, h2_s.at[h, a, n], h2_r.at[h, a, n]) for n, (b, to) in enumerate(moves)
            ])
        stage2.append(lists)

    v_copies = [
        remote(v_ref.at[:, lanes(place(dy, dx))], ext0.at[rows_of(col)], v_s.at[dy * 4 + dx], v_r.at[dy * 4 + dx],
               {"col": place(dy, dx)})
        for dy, dx in others
    ]
    own = pltpu.make_async_copy(v_ref.at[:, lanes(col)], ext0.at[rows_of(col)], own_sem)

    def scatter(pair, h):
        slot = pair + 2
        for offset in range(3):
            band[slot, pl.ds(h * blk, blk), pl.ds((2 + h + offset) * blk, blk)] = hg[slot, h, offset]
        zero = jnp.zeros((blk, blk), jnp.bfloat16)
        band[slot, pl.ds(h * blk, blk), pl.ds((5 - 5 * h) * blk, blk)] = zero
        if h == 0:
            band[slot, pl.ds(blk, blk), pl.ds(2 * blk, blk)] = hg[slot, 0, 1].T
            band[slot + 1, pl.ds(0, blk), pl.ds(0, blk)] = hg[slot, 0, 2].T
        else:
            band[slot + 1, pl.ds(0, blk), pl.ds(blk, blk)] = hg[slot, 1, 1].T
            band[slot + 1, pl.ds(blk, blk), pl.ds(blk, blk)] = hg[slot, 1, 2].T

    def scatter_unit(h, a, b):
        scatter(place(b, a) if h == 0 else place(a, b), h)

    for h in range(2):
        stage1[h][0].start()
        stage1[h][1].start()
    for h in range(2):
        stage2[h][0][0].start()
        stage2[h][0][1].start()
    own.start()
    for copy in v_copies:
        copy.start()
    for h in range(2):
        scatter(col, h)
    for h in range(2):
        for n, a in ((0, 3), (1, 1)):
            stage1[h][n].wait_recv()
            if n == h:
                stage1[h][2].start()
            stage2[h][a][0].start()
            stage2[h][a][1].start()
    for h in range(2):
        scatter_unit(h, 3, 0)
        scatter_unit(h, 1, 0)
    for h in range(2):
        stage1[h][2].wait_recv()
        stage2[h][2][0].start()
        stage2[h][2][1].start()
    for h in range(2):
        scatter_unit(h, 2, 0)
    for a in (0, 3, 1, 2):
        for h in range(2):
            for n in (0, 1):
                stage2[h][a][n].wait_recv()
                if n == (0 if a < 2 else 1):
                    stage2[h][a][2].start()
        for h in range(2):
            scatter_unit(h, a, 3)
            scatter_unit(h, a, 1)
    for a in (0, 3, 1, 2):
        for h in range(2):
            stage2[h][a][2].wait_recv()
    to_up = remote(hg.at[pl.ds(pairs, 2)], hg.at[pl.ds(0, 2)], e_s.at[0], e_r.at[0], up)
    to_down = remote(hg.at[2], hg.at[pairs + 2], e_s.at[1], e_r.at[1], down)
    to_up.start()
    to_down.start()
    own.wait()
    for copy in v_copies:
        copy.wait_recv()

    def halo_copy(side, parity):
        return remote(ext0.at[rows_of(0 if side == 0 else pairs - 2, 2)], halo.at[parity, side],
                      halo_s.at[parity, side], halo_r.at[parity, side], down if side == 0 else up)

    for side in range(2):
        halo_copy(side, 0).start()
    for a in (0, 3, 1, 2):
        for h in range(2):
            scatter_unit(h, a, 2)

    def product(j, source):
        return jnp.dot(
            band[j + 2], source[pl.ds(pl.multiple_of((j + 1) * edge, edge), 3 * edge), :],
            preferred_element_type=jnp.float32,
        )

    def update(j, source, target, initial):
        shifted = product(j, source) - filter_center * source[rows_of(j), :].astype(jnp.float32)
        if initial:
            result = shifted / filter_half
        else:
            result = 2.0 * shifted / filter_half - target[rows_of(j), :].astype(jnp.float32)
        target[rows_of(j), :] = result.astype(jnp.bfloat16)

    def sweep(low, high, source, target, initial):
        def one(j, carry):
            update(j, source, target, initial)
            return carry

        lax.fori_loop(low, high, one, 0, unroll=high - low)

    def land(side, parity):
        copy = halo_copy(side, parity)
        copy.wait()
        ext0[rows_of(pairs if side == 0 else -2, 2), :] = halo[parity, side]

    def cycle(parity, initial):
        sweep(1, pairs - 1, ext0, ext1, initial)
        sweep(2, pairs - 2, ext1, ext0, False)
        for side in range(2):
            if initial:
                if side == 0:
                    to_up.wait_recv()
                    to_down.wait_recv()
                    for pair in (-2, -1, pairs):
                        for h in range(2):
                            scatter(pair, h)
            land(1 - side, parity)
            low = side == 0
            for j in (-1, 0) if low else (pairs, pairs - 1):
                update(j, ext0, ext1, initial)
        for side in range(2):
            low = side == 0
            for j in (0, 1) if low else (pairs - 1, pairs - 2):
                update(j, ext1, ext0, False)
            halo_copy(side, 1 - parity).start()

    cycle(0, True)

    def loop(c, carry):
        cycle(lax.rem(c, 2), False)
        return carry

    lax.fori_loop(1, DEGREE // 2, loop, 0)
    f_ref[...] = ext0[rows_of(0, pairs), :]

    def apply(j, carry):
        a_ref[pl.ds(pl.multiple_of(j * edge, edge), edge), :] = product(j, ext0).astype(jnp.bfloat16)
        return carry

    lax.fori_loop(1, pairs - 1, apply, 0, unroll=pairs - 2)
    for side in range(2):
        land(1 - side, (DEGREE // 2) % 2)
        apply(0 if side == 0 else pairs - 1, 0)

    to_up.wait_send()
    to_down.wait_send()
    for h in range(2):
        for copy in (*stage1[h], *(c for copies in stage2[h] for c in copies)):
            copy.wait_send()
    for copy in v_copies:
        copy.wait_send()


def chebyshev(vectors, block_count, block_cols, blocks, n_row, n_col):
    edge, columns = vectors.shape
    blk = blocks.shape[2]
    width = columns // n_col
    rows = edge * n_col
    pairs = n_col
    smem = pl.BlockSpec(memory_space=pltpu.SMEM)
    vmem = pl.BlockSpec(memory_space=pltpu.VMEM)
    bf16 = jnp.bfloat16
    dma = pltpu.SemaphoreType.DMA
    return pl.pallas_call(
        functools.partial(filter_kernel, n_row, blocks.shape[0] * n_row * n_col),
        out_shape=[jax.ShapeDtypeStruct((rows, width), bf16)] * 2,
        in_specs=[smem, smem, vmem, pl.BlockSpec(memory_space=pl.ANY)],
        out_specs=[vmem, vmem],
        scratch_shapes=[
            pltpu.VMEM((pairs + 3, 2, 3, blk, blk), bf16),
            pltpu.VMEM((pairs + 4, edge, 6 * blk), bf16),
            pltpu.VMEM((rows + 4 * edge, width), bf16),
            pltpu.VMEM((rows + 4 * edge, width), bf16),
            pltpu.VMEM((2, 2, 2 * edge, width), bf16),
            dma, dma((16,)), dma((16,)), dma((2, 3)), dma((2, 3)), dma((2, 4, 3)), dma((2, 4, 3)),
            dma((2,)), dma((2,)), dma((2, 2)), dma((2, 2)),
        ],
        compiler_params=pltpu.CompilerParams(
            collective_id=0, has_side_effects=True, vmem_limit_bytes=48 * 1024 * 1024
        ),
    )(block_cols, block_count, blocks, vectors)


def project_kernel(scale, f_ref, a_ref, h_out, g_out, fown, aown, ft, away, keep, core_in, share, x_in, done, fin,
                   fx_s, fx_r, ax_s, ax_r, up_s, up_r, dn_s, dn_r, core_s, core_r, x_s, x_r, z_s, z_r):
    part = f_ref.shape[0] // 4
    width = f_ref.shape[1]
    half = 2 * width
    row, col = lax.axis_index("row"), lax.axis_index("col")
    z, k, y, x = row // 2, row % 2, col // 4, col % 4

    def on_x(d):
        return {"col": y * 4 + (x + d) % 4}

    def on_y(d):
        return {"col": ((y + d) % 4) * 4 + x}

    def on_z(d):
        return {"row": ((z + d) % 4) * 2 + k}

    partner = {"row": z * 2 + 1 - k}

    def remote(src, dst, send, recv, device):
        return pltpu.make_async_remote_copy(
            src_ref=src, dst_ref=dst, send_sem=send, recv_sem=recv, device_id=device, device_id_type=MESH
        )

    barrier = pltpu.get_barrier_semaphore()
    for device in [on_x(1), on_x(2), on_x(3), on_y(1), on_y(3), on_z(1), on_z(2), on_z(3), partner]:
        pl.semaphore_signal(barrier, inc=1, device_id=device, device_id_type=MESH)
    pl.semaphore_wait(barrier, 9)

    def lanes(i):
        return pl.ds(pl.multiple_of(i * width, width), width)

    def x_copy(src, dst, sems, d):
        rows = pl.ds(pl.multiple_of(((x + d) % 4) * part, part), part)
        return remote(src.at[rows], dst.at[:, lanes(x)], sems[0].at[d - 1], sems[1].at[d - 1], on_x(d))

    f_copies = {d: x_copy(f_ref, fown, (fx_s, fx_r), d) for d in (1, 2, 3)}
    a_copies = {d: x_copy(a_ref, aown, (ax_s, ax_r), d) for d in (1, 2, 3)}

    def y_copy(from_slot, to_slot, d, index, up):
        piece = pl.ds(pl.multiple_of(((x + d) % 4) * width, width), width)
        sems = (up_s, up_r) if up else (dn_s, dn_r)
        return remote(ft.at[from_slot, piece], ft.at[to_slot, piece], sems[0].at[index], sems[1].at[index],
                      on_y(1 if up else 3))

    own_up = [y_copy(0, 1, d, d, True) for d in range(4)]
    own_dn = [y_copy(0, 2, d, d, False) for d in range(4)]
    fwd_up = {0: y_copy(1, 3, 0, 4, True), 1: y_copy(1, 3, 1, 5, True)}
    fwd_dn = {3: y_copy(2, 3, 3, 4, False), 2: y_copy(2, 3, 2, 5, False)}

    def spread(d):
        source = (x + d) % 4
        piece = pl.ds(pl.multiple_of(source * width, width), width)
        ft[0, piece, :] = fown[:, lanes(source)].T
        own_up[d].start()
        own_dn[d].start()

    for d in (1, 3, 2):
        f_copies[d].start()
    mine = pl.ds(pl.multiple_of(x * part, part), part)
    fown[:, lanes(x)] = f_ref[mine, :]
    spread(0)
    aown[:, lanes(x)] = a_ref[mine, :]
    f_copies[1].wait_recv()
    spread(3)
    f_copies[3].wait_recv()
    spread(1)
    for d in (1, 3, 2):
        a_copies[d].start()
    own_up[0].wait_recv()
    fwd_up[0].start()
    f_copies[2].wait_recv()
    spread(2)
    own_up[1].wait_recv()
    fwd_up[1].start()
    own_dn[3].wait_recv()
    fwd_dn[3].start()
    own_dn[2].wait_recv()
    fwd_dn[2].start()

    core_copies = [remote(away.at[j], core_in.at[j], core_s.at[j], core_r.at[j], partner) for j in range(4)]
    x_copies = [
        [
            remote(share.at[j, :, :, lanes((x + d) % 4)], x_in.at[j, d - 1], x_s.at[j, d - 1], x_r.at[j, d - 1], on_x(d))
            for d in (1, 2, 3)
        ]
        for j in range(4)
    ]

    def tile(j):
        for part_k, out in ((1 - k, away), (k, keep)):
            lhs = ft[j, pl.ds(pl.multiple_of(part_k * half, half), half), :]
            for m, rhs in enumerate((aown, fown)):
                out[j, m] = jnp.dot(lhs, rhs[...], preferred_element_type=jnp.float32).astype(out.dtype)
            if out is away:
                core_copies[j].start()

    def over_core(j):
        core_copies[j].wait_recv()
        share[j] = (keep[j] + core_in[j].astype(jnp.float32)).astype(jnp.bfloat16)
        for copy in x_copies[j]:
            copy.start()

    def z_copy(j):
        d = (y + (0, 3, 1, 2)[j] - z + 4) % 4
        return d, remote(done.at[j], fin.at[d], z_s.at[j], z_r.at[d], on_z(d))

    def over_x(j):
        for copy in x_copies[j]:
            copy.wait_recv()
        total = share[j, :, :, lanes(x)].astype(jnp.float32)
        for i in range(3):
            total = total + x_in[j, i].astype(jnp.float32)
        done[j] = total.astype(jnp.bfloat16)
        d, copy = z_copy(j)

        @pl.when(d != 0)
        def _():
            copy.start()

        @pl.when(d == 0)
        def _():
            fin[0] = done[j]

    for d in (1, 3, 2):
        a_copies[d].wait_recv()
    tile(0)
    own_up[2].wait_recv()
    own_up[3].wait_recv()
    tile(1)
    over_core(0)
    own_dn[0].wait_recv()
    own_dn[1].wait_recv()
    tile(2)
    over_core(1)
    over_x(0)
    over_core(2)
    for copy in (*fwd_up.values(), *fwd_dn.values()):
        copy.wait_recv()
    tile(3)
    over_x(1)
    over_core(3)
    over_x(2)
    over_x(3)

    for d in (1, 2, 3):
        remote(done.at[0], fin.at[d], z_s.at[0], z_r.at[d], on_z(d)).wait_recv()
    total = fin[0].astype(jnp.float32)
    for d in (1, 2, 3):
        total = total + fin[d].astype(jnp.float32)
    h_out[...] = total[0] * scale
    g_out[...] = total[1] * scale

    for copy in (*f_copies.values(), *a_copies.values(), *own_up, *own_dn, *fwd_up.values(), *fwd_dn.values(),
                 *core_copies, *(c for cs in x_copies for c in cs)):
        copy.wait_send()
    for j in range(4):
        d, copy = z_copy(j)

        @pl.when(d != 0)
        def _():
            copy.wait_send()


def project(filtered, applied, scale):
    rows, width = filtered.shape
    part = rows // 4
    wide, half = 4 * width, 2 * width
    vmem = pl.BlockSpec(memory_space=pltpu.VMEM)
    bf16 = jnp.bfloat16
    dma = pltpu.SemaphoreType.DMA
    return pl.pallas_call(
        functools.partial(project_kernel, scale),
        out_shape=[jax.ShapeDtypeStruct((half, width), jnp.float32)] * 2,
        in_specs=[vmem, vmem],
        out_specs=[vmem, vmem],
        scratch_shapes=[
            pltpu.VMEM((part, wide), bf16),
            pltpu.VMEM((part, wide), bf16),
            pltpu.VMEM((4, wide, part), bf16),
            pltpu.VMEM((4, 2, half, wide), bf16),
            pltpu.VMEM((4, 2, half, wide), jnp.float32),
            pltpu.VMEM((4, 2, half, wide), bf16),
            pltpu.VMEM((4, 2, half, wide), bf16),
            pltpu.VMEM((4, 3, 2, half, width), bf16),
            pltpu.VMEM((4, 2, half, width), bf16),
            pltpu.VMEM((4, 2, half, width), bf16),
            dma((3,)), dma((3,)), dma((3,)), dma((3,)),
            dma((6,)), dma((6,)), dma((6,)), dma((6,)),
            dma((4,)), dma((4,)), dma((4, 3)), dma((4, 3)), dma((4,)), dma((4,)),
        ],
        compiler_params=pltpu.CompilerParams(
            collective_id=1, has_side_effects=True, vmem_limit_bytes=48 * 1024 * 1024
        ),
    )(filtered, applied)


def body(vectors, block_count, block_cols, blocks):
    n_row = lax.axis_size("row")
    n_col = lax.axis_size("col")
    row_scale = 1.0 / math.sqrt(vectors.shape[0] * n_row * n_col)
    filtered, applied = chebyshev(vectors, block_count, block_cols, blocks, n_row, n_col)
    hamiltonian_proj, intersection_proj = project(filtered, applied, row_scale)
    return (hamiltonian_proj, intersection_proj)


def solution(mesh):
    in_specs = (
        P(("row", "col"), None),
        P(("row", "col")),
        P(("row", "col"), None),
        P(("row", "col"), None, None, None),
    )
    out_specs = (P("row", "col"), P("row", "col"))
    return jax.shard_map(body, mesh=mesh, in_specs=in_specs, out_specs=out_specs, check_vma=False)
```

```python
import functools
import math

import jax
import jax.numpy as jnp
from jax import lax
from jax.experimental import pallas as pl
from jax.experimental.pallas import tpu as pltpu
from jax.sharding import PartitionSpec as P

DEGREE = 8
REACH_IN = DEGREE + 1
MESH = pl.DeviceIdType.MESH

filter_center = 0.25
filter_half = 1.75


def kernel(n_row, total_blocks, scale, cols_hbm, count_hbm, blocks_hbm, v_ref, h_out, g_out,
           cols_ref, count_ref, blocks_ref, hg, band, vland, ext0, ext1, ftx, ft, aown, fown,
           away, keep, core_in, share, x_in, done, fin,
           in_sem, v_s, v_r, vh_s, vh_r, h1_s, h1_r, h2_s, h2_r, eu_s, eu_r, ed_s, ed_r,
           fx_s, fx_r, lo_s, lo_r, hi_s, hi_r, up_s, up_r, dn_s, dn_r, core_s, core_r, x_s, x_r, z_s, z_r):
    edge = v_ref.shape[0]
    blk = edge // 2
    pairs = 16
    out = REACH_IN
    row, col = lax.axis_index("row"), lax.axis_index("col")
    z, k, y, x = row // 2, row % 2, col // 4, col % 4
    up, down = {"row": (row + 1) % n_row}, {"row": (row + n_row - 1) % n_row}
    partner = {"row": z * 2 + 1 - k}
    across = {"row": (row + n_row - 1 + 2 * k) % n_row}

    def place(dy, dx):
        return ((y + dy) % 4) * 4 + (x + dx) % 4

    def on_x(d):
        return {"col": place(0, d)}

    def on_y(d):
        return {"col": place(d, 0)}

    def on_z(d):
        return {"row": ((z + d) % 4) * 2 + k}

    def remote(src, dst, send, recv, device):
        return pltpu.make_async_remote_copy(
            src_ref=src, dst_ref=dst, send_sem=send, recv_sem=recv, device_id=device, device_id_type=MESH
        )

    def lanes(i, size, count=1):
        return pl.ds(pl.multiple_of(i * size, size), count * size)

    others = [(dy, dx) for dy in range(4) for dx in range(4) if dy or dx]
    barrier = pltpu.get_barrier_semaphore()
    for device in [partner, across, on_z(1), on_z(2), on_z(3)] + [{"col": place(dy, dx)} for dy, dx in others]:
        pl.semaphore_signal(barrier, inc=1, device_id=device, device_id_type=MESH)

    fetch = [
        pltpu.make_async_copy(cols_hbm, cols_ref, in_sem.at[0]),
        pltpu.make_async_copy(count_hbm, count_ref, in_sem.at[1]),
        pltpu.make_async_copy(blocks_hbm, blocks_ref, in_sem.at[2]),
        pltpu.make_async_copy(v_ref.at[:, lanes(col, blk)], vland.at[col + out], in_sem.at[3]),
    ]
    for copy in fetch:
        copy.start()
    for copy in fetch[:3]:
        copy.wait()

    first = (row * pairs + col) * 2
    for i in range(2):
        for offset in range(3):
            tile = jnp.zeros((blk, blk), jnp.bfloat16)
            for slot in range(5):
                relative = lax.rem(cols_ref[i, slot] - first - i + total_blocks, total_blocks)
                hit = jnp.logical_and(relative == offset, slot < count_ref[i])
                tile = jnp.where(hit, blocks_ref[i, slot], tile)
            hg[col + out, i, offset] = tile

    pl.semaphore_wait(barrier, 20)

    def where(h, a, b):
        return place(b, a) if h == 0 else place(a, b)

    def tile_copy(h, a, b, to_a, to_b, send, recv):
        unit = hg.at[where(h, a, b) + out, h]
        return remote(unit, unit, send, recv, {"col": where(h, to_a, to_b)})

    stage1, stage2 = [], []
    for h in range(2):
        sign = 1 if h == 0 else 3
        moves = [(0, 1), (0, 3), (4 - sign, sign)]
        stage1.append([tile_copy(h, a, 0, to, 0, h1_s.at[h, n], h1_r.at[h, n]) for n, (a, to) in enumerate(moves)])
        lists = []
        for a in range(4):
            sign = 1 if a < 2 else 3
            moves = [(0, 1), (0, 3), (4 - sign, sign)]
            lists.append([
                tile_copy(h, a, b, 0, to, h2_s.at[h, a, n], h2_r.at[h, a, n]) for n, (b, to) in enumerate(moves)
            ])
        stage2.append(lists)

    v_copies = [
        remote(v_ref.at[:, lanes(place(dy, dx), blk)], vland.at[col + out], v_s.at[dy * 4 + dx],
               v_r.at[dy * 4 + dx], {"col": place(dy, dx)})
        for dy, dx in others
    ]

    def tile_up(p, h):
        return remote(hg.at[p + out, h], hg.at[p + out - pairs, h], eu_s.at[p + out - pairs, h],
                      eu_r.at[p + out - pairs, h], up)

    def tile_down(p, h):
        return remote(hg.at[p + out, h], hg.at[p + out + pairs, h], ed_s.at[p, h], ed_r.at[p, h], down)

    def pass_on(h, a, b):
        p = where(h, a, b)

        @pl.when(p >= pairs - out)
        def _():
            tile_up(p, h).start()

        @pl.when(p < out - 1)
        def _():
            tile_down(p, h).start()

    v_up = remote(vland.at[pl.ds(pairs, out)], vland.at[pl.ds(0, out)], vh_s.at[0], vh_r.at[0], up)
    v_down = remote(vland.at[pl.ds(out, out)], vland.at[pl.ds(pairs + out, out)], vh_s.at[1], vh_r.at[1], down)

    def scatter(slot, h):
        def put(s, r, c, value):
            band[s, pl.ds(r * blk, blk), pl.ds(c * blk, blk)] = value

        put(slot, 2 + h, h, hg[slot, h, 0])
        put(slot, 3 + h, h, hg[slot, h, 1].T)
        put(slot, 4 + h, h, hg[slot, h, 2].T)
        put(slot, 5 - 5 * h, h, jnp.zeros((blk, blk), jnp.bfloat16))
        if h == 0:
            put(slot, 2, 1, hg[slot, 0, 1])
            put(slot + 1, 0, 0, hg[slot, 0, 2])
        else:
            put(slot + 1, 1, 0, hg[slot, 1, 1])
            put(slot + 1, 1, 1, hg[slot, 1, 2])

    def scatter_unit(h, a, b):
        scatter(where(h, a, b) + out, h)

    for h in range(2):
        stage1[h][0].start()
        stage1[h][1].start()
    for h in range(2):
        stage2[h][0][0].start()
        stage2[h][0][1].start()
    for copy in v_copies:
        copy.start()
    for h in range(2):
        pass_on(h, 0, 0)
        scatter_unit(h, 0, 0)
    for h in range(2):
        for n, a in ((0, 3), (1, 1)):
            stage1[h][n].wait_recv()
            if n == h:
                stage1[h][2].start()
            stage2[h][a][0].start()
            stage2[h][a][1].start()
            pass_on(h, a, 0)
    for h in range(2):
        scatter_unit(h, 3, 0)
        scatter_unit(h, 1, 0)
    for h in range(2):
        stage1[h][2].wait_recv()
        stage2[h][2][0].start()
        stage2[h][2][1].start()
        pass_on(h, 2, 0)
    for h in range(2):
        scatter_unit(h, 2, 0)

    def receive(a):
        for h in range(2):
            for n, b in ((0, 3), (1, 1)):
                stage2[h][a][n].wait_recv()
                if n == (0 if a < 2 else 1):
                    stage2[h][a][2].start()
                pass_on(h, a, b)
        for h in range(2):
            scatter_unit(h, a, 3)
            scatter_unit(h, a, 1)

    def turn(slot):
        ext0[:, lanes(slot, edge)] = vland[slot].T

    for a in (0, 3, 1):
        receive(a)
    fetch[3].wait()
    for copy in v_copies:
        copy.wait_recv()
    v_up.start()
    v_down.start()
    receive(2)
    for a in (0, 3, 1, 2):
        for h in range(2):
            stage2[h][a][2].wait_recv()
            pass_on(h, a, 2)
    for a in (0, 3, 1, 2):
        for h in range(2):
            scatter_unit(h, a, 2)

    def turn_all(low, high):
        def one(slot, carry):
            turn(slot)
            return carry

        lax.fori_loop(low, high, one, 0)

    turn_all(out, out + pairs)

    def sweep(step, low, high):
        source, target = (ext0, ext1) if step % 2 else (ext1, ext0)

        def one(j, carry):
            own = lanes(j + out, edge)
            product = jnp.dot(source[:, lanes(j + out - 1, edge, 3)], band[j + out], preferred_element_type=jnp.float32)
            shifted = product - filter_center * source[:, own].astype(jnp.float32)
            if step == 1:
                result = shifted / filter_half
            else:
                result = 2.0 * shifted / filter_half - target[:, own].astype(jnp.float32)
            target[:, own] = result.astype(jnp.bfloat16)
            return carry

        count = high - low
        lax.fori_loop(low, high, one, 0, unroll=count // 2 if count % 2 == 0 else count)

    sweep(1, 1, pairs - 1)
    sweep(2, 2, pairs - 2)
    v_up.wait_recv()
    v_down.wait_recv()
    turn_all(0, out)
    turn_all(pairs + out, pairs + 2 * out)
    for p in range(out):
        for h in range(2):
            tile_up(p + pairs - out, h).wait_recv()
    for p in range(out - 1):
        for h in range(2):
            tile_down(p, h).wait_recv()

    def scatter_all(low, high):
        def one(slot, carry):
            scatter(slot, 0)
            scatter(slot, 1)
            return carry

        lax.fori_loop(low, high, one, 0)

    scatter_all(0, out)
    scatter_all(pairs + out, pairs + 2 * out - 1)
    sweep(1, 1 - out, 1)
    sweep(1, pairs - 1, pairs + out - 1)
    sweep(2, 2 - out, 2)
    sweep(2, pairs - 2, pairs + out - 2)
    for step in range(3, DEGREE + 1):
        sweep(step, step - out, pairs + out - step)

    part = 4 * edge
    width = blk
    half = 2 * width

    def x_copy(d, first_pair, count, offset, sems):
        pair = 4 * ((x + d) % 4) + first_pair + out
        return remote(ext0.at[:, lanes(pair, edge, count)], ftx.at[lanes(x, width), pl.ds(offset, count * edge)],
                      sems[0].at[d - 1], sems[1].at[d - 1], on_x(d))

    f_copies = {d: x_copy(d, 0, 4, edge, (fx_s, fx_r)) for d in (1, 2, 3)}
    lo_copies = {d: x_copy(d, -1, 1, 0, (lo_s, lo_r)) for d in (1, 2, 3)}
    hi_copies = {d: x_copy(d, 4, 1, 5 * edge, (hi_s, hi_r)) for d in (1, 2, 3)}
    inner = pl.ds(edge, part)

    def y_copy(from_slot, to_slot, d, index, is_up):
        piece = lanes((x + d) % 4, width)
        sems = (up_s, up_r) if is_up else (dn_s, dn_r)
        src = ftx.at[piece, inner] if from_slot == 0 else ft.at[from_slot - 1, piece]
        return remote(src, ft.at[to_slot - 1, piece], sems[0].at[index], sems[1].at[index], on_y(1 if is_up else 3))

    own_up = [y_copy(0, 1, d, d, True) for d in range(4)]
    own_dn = [y_copy(0, 2, d, d, False) for d in range(4)]
    fwd_up = {0: y_copy(1, 3, 0, 4, True), 1: y_copy(1, 3, 1, 5, True)}
    fwd_dn = {3: y_copy(2, 3, 3, 4, False), 2: y_copy(2, 3, 2, 5, False)}

    def spread(d):
        own_up[d].start()
        own_dn[d].start()

    for d in (1, 3, 2):
        f_copies[d].start()
    ftx[lanes(x, width), :] = ext0[:, lanes(4 * x - 1 + out, edge, 6)]
    spread(0)
    for d in (1, 3, 2):
        lo_copies[d].start()
        hi_copies[d].start()
    f_copies[1].wait_recv()
    spread(3)
    f_copies[3].wait_recv()
    spread(1)
    own_up[0].wait_recv()
    fwd_up[0].start()
    f_copies[2].wait_recv()
    spread(2)
    own_dn[3].wait_recv()
    fwd_dn[3].start()
    own_up[1].wait_recv()
    fwd_up[1].start()

    for d in (1, 3, 2):
        lo_copies[d].wait_recv()
        hi_copies[d].wait_recv()
    for q in range(4):
        rows = pl.ds(q * edge, edge)
        applied = jnp.dot(ftx[:, pl.ds(q * edge, 3 * edge)], band[4 * x + q + out], preferred_element_type=jnp.float32)
        aown[rows, :] = applied.astype(jnp.bfloat16).T
        fown[rows, :] = ftx[:, pl.ds((q + 1) * edge, edge)].T

    core_copies = [remote(away.at[j], core_in.at[j], core_s.at[j], core_r.at[j], partner) for j in range(4)]
    x_copies = [
        [
            remote(share.at[j, :, :, lanes((x + d) % 4, width)], x_in.at[j, d - 1], x_s.at[j, d - 1],
                   x_r.at[j, d - 1], on_x(d))
            for d in (1, 2, 3)
        ]
        for j in range(4)
    ]

    def tile(j):
        for part_k, target in ((1 - k, away), (k, keep)):
            rows = lanes(part_k, half)
            lhs = ftx[rows, inner] if j == 0 else ft[j - 1, rows, :]
            for m, rhs in enumerate((aown, fown)):
                target[j, m] = jnp.dot(lhs, rhs[...], preferred_element_type=jnp.float32).astype(target.dtype)
            if target is away:
                core_copies[j].start()

    def over_core(j):
        core_copies[j].wait_recv()
        share[j] = (keep[j] + core_in[j].astype(jnp.float32)).astype(jnp.bfloat16)
        for copy in x_copies[j]:
            copy.start()

    def z_copy(j):
        d = (y + (0, 3, 1, 2)[j] - z + 4) % 4
        return d, remote(done.at[j], fin.at[d], z_s.at[j], z_r.at[d], on_z(d))

    def over_x(j):
        for copy in x_copies[j]:
            copy.wait_recv()
        total = share[j, :, :, lanes(x, width)].astype(jnp.float32)
        for i in range(3):
            total = total + x_in[j, i].astype(jnp.float32)
        done[j] = total.astype(jnp.bfloat16)
        d, copy = z_copy(j)

        @pl.when(d != 0)
        def _():
            copy.start()

        @pl.when(d == 0)
        def _():
            fin[0] = done[j]

    tile(0)
    own_dn[2].wait_recv()
    fwd_dn[2].start()
    own_up[2].wait_recv()
    own_up[3].wait_recv()
    tile(1)
    over_core(0)
    own_dn[0].wait_recv()
    own_dn[1].wait_recv()
    tile(2)
    over_core(1)
    over_x(0)
    over_core(2)
    for copy in (*fwd_up.values(), *fwd_dn.values()):
        copy.wait_recv()
    tile(3)
    over_x(1)
    over_core(3)
    over_x(2)
    over_x(3)

    for d in (1, 2, 3):
        remote(done.at[0], fin.at[d], z_s.at[0], z_r.at[d], on_z(d)).wait_recv()
    total = fin[0].astype(jnp.float32)
    for d in (1, 2, 3):
        total = total + fin[d].astype(jnp.float32)
    h_out[...] = total[0] * scale
    g_out[...] = total[1] * scale

    for h in range(2):
        for copy in (*stage1[h], *(c for copies in stage2[h] for c in copies)):
            copy.wait_send()
        for p in range(out):
            tile_up(p + pairs - out, h).wait_send()
        for p in range(out - 1):
            tile_down(p, h).wait_send()
    for copy in (*v_copies, v_up, v_down, *f_copies.values(), *lo_copies.values(), *hi_copies.values(), *own_up,
                 *own_dn, *fwd_up.values(), *fwd_dn.values(), *core_copies, *(c for cs in x_copies for c in cs)):
        copy.wait_send()
    for j in range(4):
        d, copy = z_copy(j)

        @pl.when(d != 0)
        def _():
            copy.wait_send()


def body(vectors, block_count, block_cols, blocks):
    n_row = lax.axis_size("row")
    n_col = lax.axis_size("col")
    edge, columns = vectors.shape
    local_blocks, slots, blk, _ = blocks.shape
    width = columns // n_col
    scale = 1.0 / math.sqrt(edge * n_row * n_col)
    wide, half, part = 4 * width, 2 * width, 4 * edge
    reach = n_col + 2 * REACH_IN
    anywhere = pl.BlockSpec(memory_space=pl.ANY)
    vmem = pl.BlockSpec(memory_space=pltpu.VMEM)
    bf16 = jnp.bfloat16
    dma = pltpu.SemaphoreType.DMA
    return pl.pallas_call(
        functools.partial(kernel, n_row, local_blocks * n_row * n_col, scale),
        out_shape=[jax.ShapeDtypeStruct((half, width), jnp.float32)] * 2,
        in_specs=[anywhere] * 4,
        out_specs=[vmem, vmem],
        scratch_shapes=[
            pltpu.SMEM(block_cols.shape, jnp.int32),
            pltpu.SMEM(block_count.shape, jnp.int32),
            pltpu.VMEM(blocks.shape, bf16),
            pltpu.VMEM((reach - 1, 2, 3, blk, blk), bf16),
            pltpu.VMEM((reach, 6 * blk, edge), bf16),
            pltpu.VMEM((reach, edge, width), bf16),
            pltpu.VMEM((width, reach * edge), bf16),
            pltpu.VMEM((width, reach * edge), bf16),
            pltpu.VMEM((wide, part + 2 * edge), bf16),
            pltpu.VMEM((3, wide, part), bf16),
            pltpu.VMEM((part, wide), bf16),
            pltpu.VMEM((part, wide), bf16),
            pltpu.VMEM((4, 2, half, wide), bf16),
            pltpu.VMEM((4, 2, half, wide), jnp.float32),
            pltpu.VMEM((4, 2, half, wide), bf16),
            pltpu.VMEM((4, 2, half, wide), bf16),
            pltpu.VMEM((4, 3, 2, half, width), bf16),
            pltpu.VMEM((4, 2, half, width), bf16),
            pltpu.VMEM((4, 2, half, width), bf16),
            dma((4,)),
            dma((16,)), dma((16,)), dma((2,)), dma((2,)),
            dma((2, 3)), dma((2, 3)), dma((2, 4, 3)), dma((2, 4, 3)),
            dma((REACH_IN, 2)), dma((REACH_IN, 2)), dma((REACH_IN - 1, 2)), dma((REACH_IN - 1, 2)),
            dma((3,)), dma((3,)), dma((3,)), dma((3,)), dma((3,)), dma((3,)),
            dma((6,)), dma((6,)), dma((6,)), dma((6,)),
            dma((4,)), dma((4,)), dma((4, 3)), dma((4, 3)), dma((4,)), dma((4,)),
        ],
        compiler_params=pltpu.CompilerParams(
            collective_id=0, has_side_effects=True, vmem_limit_bytes=58 * 1024 * 1024
        ),
    )(block_cols, block_count, blocks, vectors)


def solution(mesh):
    in_specs = (
        P(("row", "col"), None),
        P(("row", "col")),
        P(("row", "col"), None),
        P(("row", "col"), None, None, None),
    )
    out_specs = (P("row", "col"), P("row", "col"))
    return jax.shard_map(body, mesh=mesh, in_specs=in_specs, out_specs=out_specs, check_vma=False)
```

```python
import functools
import math

import jax
import jax.numpy as jnp
from jax import lax
from jax.experimental import pallas as pl
from jax.experimental.pallas import tpu as pltpu
from jax.sharding import PartitionSpec as P

DEGREE = 8
REACH_IN = DEGREE + 1
MESH = pl.DeviceIdType.MESH

filter_center = 0.25
filter_half = 1.75


def kernel(n_row, total_blocks, cols_hbm, count_hbm, blocks_hbm, v_ref, sums,
           cols_ref, count_ref, blocks_ref, hg, band, vland, ext0, ext1, ftx, ft, aown, fown,
           away, keep, core_in, share, x_in, done, fin,
           in_sem, v_s, v_r, vh_s, vh_r, h1_s, h1_r, h2_s, h2_r, eu_s, eu_r, ed_s, ed_r,
           fx_s, fx_r, lo_s, lo_r, hi_s, hi_r, up_s, up_r, dn_s, dn_r, core_s, core_r, x_s, x_r, z_s, z_r):
    edge = v_ref.shape[0]
    blk = edge // 2
    pairs = 16
    out = REACH_IN
    row, col = lax.axis_index("row"), lax.axis_index("col")
    z, k, y, x = row // 2, row % 2, col // 4, col % 4
    up, down = {"row": (row + 1) % n_row}, {"row": (row + n_row - 1) % n_row}
    partner = {"row": z * 2 + 1 - k}
    across = {"row": (row + n_row - 1 + 2 * k) % n_row}

    def place(dy, dx):
        return ((y + dy) % 4) * 4 + (x + dx) % 4

    def on_x(d):
        return {"col": place(0, d)}

    def on_y(d):
        return {"col": place(d, 0)}

    def on_z(d):
        return {"row": ((z + d) % 4) * 2 + k}

    def remote(src, dst, send, recv, device):
        return pltpu.make_async_remote_copy(
            src_ref=src, dst_ref=dst, send_sem=send, recv_sem=recv, device_id=device, device_id_type=MESH
        )

    def lanes(i, size, count=1):
        return pl.ds(pl.multiple_of(i * size, size), count * size)

    others = [(dy, dx) for dy in range(4) for dx in range(4) if dy or dx]
    barrier = pltpu.get_barrier_semaphore()
    for device in [partner, across, on_z(1), on_z(2), on_z(3)] + [{"col": place(dy, dx)} for dy, dx in others]:
        pl.semaphore_signal(barrier, inc=1, device_id=device, device_id_type=MESH)

    fetch = [
        pltpu.make_async_copy(cols_hbm, cols_ref, in_sem.at[0]),
        pltpu.make_async_copy(count_hbm, count_ref, in_sem.at[1]),
        pltpu.make_async_copy(blocks_hbm, blocks_ref, in_sem.at[2]),
        pltpu.make_async_copy(v_ref.at[:, lanes(col, blk)], vland.at[col + out], in_sem.at[3]),
    ]
    for copy in fetch:
        copy.start()
    for copy in fetch[:3]:
        copy.wait()

    first = (row * pairs + col) * 2
    for i in range(2):
        for offset in range(3):
            tile = jnp.zeros((blk, blk), jnp.bfloat16)
            for slot in range(5):
                relative = lax.rem(cols_ref[i, slot] - first - i + total_blocks, total_blocks)
                hit = jnp.logical_and(relative == offset, slot < count_ref[i])
                tile = jnp.where(hit, blocks_ref[i, slot], tile)
            hg[col + out, i, offset] = tile

    pl.semaphore_wait(barrier, 20)

    def where(h, a, b):
        return place(b, a) if h == 0 else place(a, b)

    def tile_copy(h, a, b, to_a, to_b, send, recv):
        unit = hg.at[where(h, a, b) + out, h]
        return remote(unit, unit, send, recv, {"col": where(h, to_a, to_b)})

    stage1, stage2 = [], []
    for h in range(2):
        sign = 1 if h == 0 else 3
        moves = [(0, 1), (0, 3), (4 - sign, sign)]
        stage1.append([tile_copy(h, a, 0, to, 0, h1_s.at[h, n], h1_r.at[h, n]) for n, (a, to) in enumerate(moves)])
        lists = []
        for a in range(4):
            sign = 1 if a < 2 else 3
            moves = [(0, 1), (0, 3), (4 - sign, sign)]
            lists.append([
                tile_copy(h, a, b, 0, to, h2_s.at[h, a, n], h2_r.at[h, a, n]) for n, (b, to) in enumerate(moves)
            ])
        stage2.append(lists)

    v_copies = [
        remote(v_ref.at[:, lanes(place(dy, dx), blk)], vland.at[col + out], v_s.at[dy * 4 + dx],
               v_r.at[dy * 4 + dx], {"col": place(dy, dx)})
        for dy, dx in others
    ]

    def tile_up(p, h):
        return remote(hg.at[p + out, h], hg.at[p + out - pairs, h], eu_s.at[p + out - pairs, h],
                      eu_r.at[p + out - pairs, h], up)

    def tile_down(p, h):
        return remote(hg.at[p + out, h], hg.at[p + out + pairs, h], ed_s.at[p, h], ed_r.at[p, h], down)

    def pass_on(h, a, b):
        p = where(h, a, b)

        @pl.when(p >= pairs - out)
        def _():
            tile_up(p, h).start()

        @pl.when(p < out - 1)
        def _():
            tile_down(p, h).start()

    def vector_up(p):
        return remote(vland.at[p + out], vland.at[p + out - pairs], vh_s.at[0, p + out - pairs],
                      vh_r.at[0, p + out - pairs], up)

    def vector_down(p):
        return remote(vland.at[p + out], vland.at[p + out + pairs], vh_s.at[1, p], vh_r.at[1, p], down)

    def pass_vector(dy, dx):
        if dy or dx:
            v_copies[others.index((dy, dx))].wait_recv()
        else:
            fetch[3].wait()
        p = place(4 - dy, 4 - dx)

        @pl.when(p >= pairs - out)
        def _():
            vector_up(p).start()

        @pl.when(p < out)
        def _():
            vector_down(p).start()

    def scatter(slot, h):
        def put(s, r, c, value):
            band[s, pl.ds(r * blk, blk), pl.ds(c * blk, blk)] = value

        put(slot, 2 + h, h, hg[slot, h, 0])
        put(slot, 3 + h, h, hg[slot, h, 1].T)
        put(slot, 4 + h, h, hg[slot, h, 2].T)
        put(slot, 5 - 5 * h, h, jnp.zeros((blk, blk), jnp.bfloat16))
        if h == 0:
            put(slot, 2, 1, hg[slot, 0, 1])
            put(slot + 1, 0, 0, hg[slot, 0, 2])
        else:
            put(slot + 1, 1, 0, hg[slot, 1, 1])
            put(slot + 1, 1, 1, hg[slot, 1, 2])

    def scatter_unit(h, a, b):
        scatter(where(h, a, b) + out, h)

    for h in range(2):
        stage1[h][0].start()
        stage1[h][1].start()
    for h in range(2):
        stage2[h][0][0].start()
        stage2[h][0][1].start()
    for copy in v_copies:
        copy.start()
    for h in range(2):
        pass_on(h, 0, 0)
        scatter_unit(h, 0, 0)
    for h in range(2):
        for n, a in ((0, 3), (1, 1)):
            stage1[h][n].wait_recv()
            if n == h:
                stage1[h][2].start()
            stage2[h][a][0].start()
            stage2[h][a][1].start()
            pass_on(h, a, 0)
    for h in range(2):
        scatter_unit(h, 3, 0)
        scatter_unit(h, 1, 0)
    for dy, dx in ((0, 0), (0, 1), (0, 3), (1, 0), (3, 0)):
        pass_vector(dy, dx)
    for h in range(2):
        stage1[h][2].wait_recv()
        stage2[h][2][0].start()
        stage2[h][2][1].start()
        pass_on(h, 2, 0)
    for h in range(2):
        scatter_unit(h, 2, 0)

    def receive(a):
        for h in range(2):
            for n, b in ((0, 3), (1, 1)):
                stage2[h][a][n].wait_recv()
                if n == (0 if a < 2 else 1):
                    stage2[h][a][2].start()
                pass_on(h, a, b)
        for h in range(2):
            scatter_unit(h, a, 3)
            scatter_unit(h, a, 1)

    def turn(slot):
        ext0[:, lanes(slot, edge)] = vland[slot].T

    for a, moves in (
        (0, ((1, 1), (1, 3), (3, 1), (3, 3))),
        (3, ((0, 2), (2, 0), (1, 2), (2, 1))),
        (1, ((3, 2), (2, 3), (2, 2))),
        (2, ()),
    ):
        receive(a)
        for dy, dx in moves:
            pass_vector(dy, dx)
    for a in (0, 3, 1, 2):
        for h in range(2):
            stage2[h][a][2].wait_recv()
            pass_on(h, a, 2)
    for a in (0, 3, 1, 2):
        for h in range(2):
            scatter_unit(h, a, 2)

    def turn_all(low, high):
        def one(slot, carry):
            turn(slot)
            return carry

        lax.fori_loop(low, high, one, 0)

    turn_all(out, out + pairs)

    def update(step, j):
        source, target = (ext0, ext1) if step % 2 else (ext1, ext0)
        own = lanes(j + out, edge)
        product = jnp.dot(source[:, lanes(j + out - 1, edge, 3)], band[j + out], preferred_element_type=jnp.float32)
        shifted = product - filter_center * source[:, own].astype(jnp.float32)
        if step == 1:
            result = shifted / filter_half
        else:
            result = 2.0 * shifted / filter_half - target[:, own].astype(jnp.float32)
        target[:, own] = result.astype(jnp.bfloat16)

    for step in range(1, DEGREE):
        def inside(j, carry):
            update(step, j)
            return carry

        lax.fori_loop(step, pairs - step, inside, 0, unroll=pairs // 2 - step)

    for p in range(out):
        vector_up(p + pairs - out).wait_recv()
        turn(p)
        vector_down(p).wait_recv()
        turn(p + pairs + out)
    for p in range(out):
        for h in range(2):
            tile_up(p + pairs - out, h).wait_recv()
            scatter(p, h)
            if p < out - 1:
                tile_down(p, h).wait_recv()
                scatter(p + pairs + out, h)

    for step in range(1, DEGREE + 1):
        def outside(i, carry):
            update(step, step - out + i)
            update(step, pairs - step + i)
            return carry

        lax.fori_loop(0, out, outside, 0, unroll=3)

    part = 4 * edge
    width = blk
    half = 2 * width

    def mate(e):
        return (x, x + 1 - 2 * (x % 2), (x + 2) % 4, 3 - x)[e]

    def x_copy(e, first_pair, count, offset, sems):
        pair = 4 * mate(e) + first_pair + out
        return remote(ext0.at[:, lanes(pair, edge, count)], ftx.at[lanes(x, width), pl.ds(offset, count * edge)],
                      sems[0].at[e - 1], sems[1].at[e - 1], {"col": y * 4 + mate(e)})

    f_copies = {e: x_copy(e, 0, 4, edge, (fx_s, fx_r)) for e in (1, 2, 3)}
    lo_copies = {e: x_copy(e, -1, 1, 0, (lo_s, lo_r)) for e in (1, 2, 3)}
    hi_copies = {e: x_copy(e, 4, 1, 5 * edge, (hi_s, hi_r)) for e in (1, 2, 3)}
    inner = pl.ds(edge, part)

    def y_copy(from_slot, to_slot, e, index, is_up):
        piece = lanes(mate(e), width)
        sems = (up_s, up_r) if is_up else (dn_s, dn_r)
        src = ftx.at[piece, inner] if from_slot == 0 else ft.at[from_slot - 1, piece]
        return remote(src, ft.at[to_slot - 1, piece], sems[0].at[index], sems[1].at[index], on_y(1 if is_up else 3))

    own_up = [y_copy(0, 1, e, e, True) for e in range(4)]
    own_dn = [y_copy(0, 2, e, e, False) for e in range(4)]
    fwd_up = {0: y_copy(1, 3, 0, 4, True), 3: y_copy(1, 3, 3, 5, True)}
    fwd_dn = {1: y_copy(2, 3, 1, 4, False), 2: y_copy(2, 3, 2, 5, False)}

    def spread(e):
        own_up[e].start()
        own_dn[e].start()

    for e in (1, 3, 2):
        f_copies[e].start()
    ftx[lanes(x, width), :] = ext0[:, lanes(4 * x - 1 + out, edge, 6)]
    spread(0)
    f_copies[1].wait_recv()
    spread(1)
    f_copies[3].wait_recv()
    spread(3)
    own_up[0].wait_recv()
    fwd_up[0].start()
    f_copies[2].wait_recv()
    spread(2)
    for e in (1, 3, 2):
        lo_copies[e].start()
        hi_copies[e].start()
    own_dn[1].wait_recv()
    fwd_dn[1].start()

    def apply(q):
        rows = pl.ds(q * edge, edge)
        applied = jnp.dot(ftx[:, pl.ds(q * edge, 3 * edge)], band[4 * x + q + out], preferred_element_type=jnp.float32)
        aown[rows, :] = applied.astype(jnp.bfloat16).T
        fown[rows, :] = ftx[:, pl.ds((q + 1) * edge, edge)].T

    apply(1)
    apply(2)
    own_up[3].wait_recv()
    fwd_up[3].start()
    for e in (1, 3, 2):
        lo_copies[e].wait_recv()
        hi_copies[e].wait_recv()
    apply(0)
    apply(3)

    core_copies = [remote(away.at[j], core_in.at[j], core_s.at[j], core_r.at[j], partner) for j in range(4)]
    x_copies = [
        [
            remote(share.at[j, :, :, lanes((x + d) % 4, width)], x_in.at[j, d - 1], x_s.at[j, d - 1],
                   x_r.at[j, d - 1], on_x(d))
            for d in (1, 2, 3)
        ]
        for j in range(4)
    ]

    def half_tile(j, g):
        target_k = x // 2 if g == 0 else 1 - x // 2
        rows = lanes(target_k, half)
        lhs = ftx[rows, inner] if j == 0 else ft[j - 1, rows, :]
        parts = [jnp.dot(lhs, rhs[...], preferred_element_type=jnp.float32) for rhs in (aown, fown)]

        @pl.when(target_k == k)
        def _():
            for m in range(2):
                keep[j, m] = parts[m]

        @pl.when(target_k != k)
        def _():
            for m in range(2):
                away[j, m] = parts[m].astype(jnp.bfloat16)
            core_copies[j].start()

    def tile(j):
        half_tile(j, 0)
        half_tile(j, 1)

    def over_core(j):
        core_copies[j].wait_recv()
        share[j] = (keep[j] + core_in[j].astype(jnp.float32)).astype(jnp.bfloat16)
        for copy in x_copies[j]:
            copy.start()

    def z_copy(j):
        d = (y + (0, 3, 1, 2)[j] - z + 4) % 4
        return d, remote(done.at[j], fin.at[d], z_s.at[j], z_r.at[d], on_z(d))

    def over_x(j):
        for copy in x_copies[j]:
            copy.wait_recv()
        total = share[j, :, :, lanes(x, width)].astype(jnp.float32)
        for i in range(3):
            total = total + x_in[j, i].astype(jnp.float32)
        done[j] = total.astype(jnp.bfloat16)
        d, copy = z_copy(j)

        @pl.when(d != 0)
        def _():
            copy.start()

        @pl.when(d == 0)
        def _():
            fin[0] = done[j]

    tile(0)
    own_dn[2].wait_recv()
    fwd_dn[2].start()
    own_up[1].wait_recv()
    own_up[2].wait_recv()
    tile(1)
    over_core(0)
    own_dn[0].wait_recv()
    own_dn[3].wait_recv()
    tile(2)
    over_core(1)
    over_x(0)
    over_core(2)
    fwd_up[0].wait_recv()
    fwd_dn[1].wait_recv()
    half_tile(3, 0)

    @pl.when(x // 2 == k)
    def _():
        over_core(3)

    over_x(1)
    fwd_up[3].wait_recv()
    fwd_dn[2].wait_recv()
    half_tile(3, 1)

    @pl.when(x // 2 != k)
    def _():
        over_core(3)

    over_x(2)
    over_x(3)

    for d in (1, 2, 3):
        remote(done.at[0], fin.at[d], z_s.at[0], z_r.at[d], on_z(d)).wait_recv()
    total = fin[0].astype(jnp.float32)
    for d in (1, 2, 3):
        total = total + fin[d].astype(jnp.float32)
    sums[...] = total

    for h in range(2):
        for copy in (*stage1[h], *(c for copies in stage2[h] for c in copies)):
            copy.wait_send()
        for p in range(out):
            tile_up(p + pairs - out, h).wait_send()
        for p in range(out - 1):
            tile_down(p, h).wait_send()
    for p in range(out):
        vector_up(p + pairs - out).wait_send()
        vector_down(p).wait_send()
    for copy in (*v_copies, *f_copies.values(), *lo_copies.values(), *hi_copies.values(), *own_up,
                 *own_dn, *fwd_up.values(), *fwd_dn.values(), *core_copies, *(c for cs in x_copies for c in cs)):
        copy.wait_send()
    for j in range(4):
        d, copy = z_copy(j)

        @pl.when(d != 0)
        def _():
            copy.wait_send()


def body(vectors, block_count, block_cols, blocks):
    n_row = lax.axis_size("row")
    n_col = lax.axis_size("col")
    edge, columns = vectors.shape
    local_blocks, slots, blk, _ = blocks.shape
    width = columns // n_col
    scale = 1.0 / math.sqrt(edge * n_row * n_col)
    wide, half, part = 4 * width, 2 * width, 4 * edge
    reach = n_col + 2 * REACH_IN
    anywhere = pl.BlockSpec(memory_space=pl.ANY)
    vmem = pl.BlockSpec(memory_space=pltpu.VMEM)
    bf16 = jnp.bfloat16
    dma = pltpu.SemaphoreType.DMA
    sums = pl.pallas_call(
        functools.partial(kernel, n_row, local_blocks * n_row * n_col),
        out_shape=jax.ShapeDtypeStruct((2, half, width), jnp.float32),
        in_specs=[anywhere] * 4,
        out_specs=vmem,
        scratch_shapes=[
            pltpu.SMEM(block_cols.shape, jnp.int32),
            pltpu.SMEM(block_count.shape, jnp.int32),
            pltpu.VMEM(blocks.shape, bf16),
            pltpu.VMEM((reach - 1, 2, 3, blk, blk), bf16),
            pltpu.VMEM((reach, 6 * blk, edge), bf16),
            pltpu.VMEM((reach, edge, width), bf16),
            pltpu.VMEM((width, reach * edge), bf16),
            pltpu.VMEM((width, reach * edge), bf16),
            pltpu.VMEM((wide, part + 2 * edge), bf16),
            pltpu.VMEM((3, wide, part), bf16),
            pltpu.VMEM((part, wide), bf16),
            pltpu.VMEM((part, wide), bf16),
            pltpu.VMEM((4, 2, half, wide), bf16),
            pltpu.VMEM((4, 2, half, wide), jnp.float32),
            pltpu.VMEM((4, 2, half, wide), bf16),
            pltpu.VMEM((4, 2, half, wide), bf16),
            pltpu.VMEM((4, 3, 2, half, width), bf16),
            pltpu.VMEM((4, 2, half, width), bf16),
            pltpu.VMEM((4, 2, half, width), bf16),
            dma((4,)),
            dma((16,)), dma((16,)), dma((2, REACH_IN)), dma((2, REACH_IN)),
            dma((2, 3)), dma((2, 3)), dma((2, 4, 3)), dma((2, 4, 3)),
            dma((REACH_IN, 2)), dma((REACH_IN, 2)), dma((REACH_IN - 1, 2)), dma((REACH_IN - 1, 2)),
            dma((3,)), dma((3,)), dma((3,)), dma((3,)), dma((3,)), dma((3,)),
            dma((6,)), dma((6,)), dma((6,)), dma((6,)),
            dma((4,)), dma((4,)), dma((4, 3)), dma((4, 3)), dma((4,)), dma((4,)),
        ],
        compiler_params=pltpu.CompilerParams(
            collective_id=0, has_side_effects=True, vmem_limit_bytes=58 * 1024 * 1024
        ),
    )(block_cols, block_count, blocks, vectors)
    return (sums[0] * scale, sums[1] * scale)


def solution(mesh):
    in_specs = (
        P(("row", "col"), None),
        P(("row", "col")),
        P(("row", "col"), None),
        P(("row", "col"), None, None, None),
    )
    out_specs = (P("row", "col"), P("row", "col"))
    return jax.shard_map(body, mesh=mesh, in_specs=in_specs, out_specs=out_specs, check_vma=False)
```

```python
import functools
import math

import jax
import jax.numpy as jnp
from jax import lax
from jax.experimental import pallas as pl
from jax.experimental.pallas import tpu as pltpu
from jax.sharding import PartitionSpec as P

DEGREE = 8
REACH_IN = DEGREE + 1
MESH = pl.DeviceIdType.MESH

filter_center = 0.25
filter_half = 1.75


def kernel(n_row, total_blocks, cols_hbm, count_hbm, blocks_hbm, v_ref, sums,
           cols_ref, count_ref, blocks_ref, hg, band, vland, ext0, ext1, ftx, ft, aown, fown,
           away, keep, core_in, share, x_in, done, fin, zin, ksum, kx_in,
           in_sem, v_s, v_r, vh_s, vh_r, h1_s, h1_r, h2_s, h2_r, eu_s, eu_r, ed_s, ed_r,
           fx_s, fx_r, lo_s, lo_r, hi_s, hi_r, up_s, up_r, dn_s, dn_r, core_s, core_r, x_s, x_r, z_s, z_r,
           zk_s, zk_r, kx_s, kx_r):
    edge = v_ref.shape[0]
    blk = edge // 2
    pairs = 16
    out = REACH_IN
    row, col = lax.axis_index("row"), lax.axis_index("col")
    z, k, y, x = row // 2, row % 2, col // 4, col % 4
    up, down = {"row": (row + 1) % n_row}, {"row": (row + n_row - 1) % n_row}
    partner = {"row": z * 2 + 1 - k}
    across = {"row": (row + n_row - 1 + 2 * k) % n_row}

    def place(dy, dx):
        return ((y + dy) % 4) * 4 + (x + dx) % 4

    def on_x(d):
        return {"col": place(0, d)}

    def on_y(d):
        return {"col": place(d, 0)}

    def on_z(d):
        return {"row": ((z + d) % 4) * 2 + k}

    def remote(src, dst, send, recv, device):
        return pltpu.make_async_remote_copy(
            src_ref=src, dst_ref=dst, send_sem=send, recv_sem=recv, device_id=device, device_id_type=MESH
        )

    def lanes(i, size, count=1):
        return pl.ds(pl.multiple_of(i * size, size), count * size)

    others = [(dy, dx) for dy in range(4) for dx in range(4) if dy or dx]
    barrier = pltpu.get_barrier_semaphore()
    for device in [partner, across, on_z(1), on_z(2), on_z(3)] + [{"col": place(dy, dx)} for dy, dx in others]:
        pl.semaphore_signal(barrier, inc=1, device_id=device, device_id_type=MESH)

    fetch = [
        pltpu.make_async_copy(cols_hbm, cols_ref, in_sem.at[0]),
        pltpu.make_async_copy(count_hbm, count_ref, in_sem.at[1]),
        pltpu.make_async_copy(blocks_hbm, blocks_ref, in_sem.at[2]),
        pltpu.make_async_copy(v_ref.at[:, lanes(col, blk)], vland.at[col + out], in_sem.at[3]),
    ]
    for copy in fetch:
        copy.start()
    for copy in fetch[:3]:
        copy.wait()

    first = (row * pairs + col) * 2
    for i in range(2):
        for offset in range(3):
            tile = jnp.zeros((blk, blk), jnp.bfloat16)
            for slot in range(5):
                relative = lax.rem(cols_ref[i, slot] - first - i + total_blocks, total_blocks)
                hit = jnp.logical_and(relative == offset, slot < count_ref[i])
                tile = jnp.where(hit, blocks_ref[i, slot], tile)
            hg[col + out, i, offset] = tile

    pl.semaphore_wait(barrier, 20)

    def where(h, a, b):
        return place(b, a) if h == 0 else place(a, b)

    def tile_copy(h, a, b, to_a, to_b, send, recv):
        unit = hg.at[where(h, a, b) + out, h]
        return remote(unit, unit, send, recv, {"col": where(h, to_a, to_b)})

    stage1, stage2 = [], []
    for h in range(2):
        sign = 1 if h == 0 else 3
        moves = [(0, 1), (0, 3), (4 - sign, sign)]
        stage1.append([tile_copy(h, a, 0, to, 0, h1_s.at[h, n], h1_r.at[h, n]) for n, (a, to) in enumerate(moves)])
        lists = []
        for a in range(4):
            sign = 1 if a < 2 else 3
            moves = [(0, 1), (0, 3), (4 - sign, sign)]
            lists.append([
                tile_copy(h, a, b, 0, to, h2_s.at[h, a, n], h2_r.at[h, a, n]) for n, (b, to) in enumerate(moves)
            ])
        stage2.append(lists)

    v_copies = [
        remote(v_ref.at[:, lanes(place(dy, dx), blk)], vland.at[col + out], v_s.at[dy * 4 + dx],
               v_r.at[dy * 4 + dx], {"col": place(dy, dx)})
        for dy, dx in others
    ]

    def tile_up(p, h):
        return remote(hg.at[p + out, h], hg.at[p + out - pairs, h], eu_s.at[p + out - pairs, h],
                      eu_r.at[p + out - pairs, h], up)

    def tile_down(p, h):
        return remote(hg.at[p + out, h], hg.at[p + out + pairs, h], ed_s.at[p, h], ed_r.at[p, h], down)

    def pass_on(h, a, b):
        p = where(h, a, b)

        @pl.when(p >= pairs - out)
        def _():
            tile_up(p, h).start()

        @pl.when(p < out - 1)
        def _():
            tile_down(p, h).start()

    def vector_up(p):
        return remote(vland.at[p + out], vland.at[p + out - pairs], vh_s.at[0, p + out - pairs],
                      vh_r.at[0, p + out - pairs], up)

    def vector_down(p):
        return remote(vland.at[p + out], vland.at[p + out + pairs], vh_s.at[1, p], vh_r.at[1, p], down)

    def pass_vector(dy, dx):
        if dy or dx:
            v_copies[others.index((dy, dx))].wait_recv()
        else:
            fetch[3].wait()
        p = place(4 - dy, 4 - dx)

        @pl.when(p >= pairs - out)
        def _():
            vector_up(p).start()

        @pl.when(p < out)
        def _():
            vector_down(p).start()

    def scatter(slot, h):
        def put(s, r, c, value):
            band[s, pl.ds(r * blk, blk), pl.ds(c * blk, blk)] = value

        put(slot, 2 + h, h, hg[slot, h, 0])
        put(slot, 3 + h, h, hg[slot, h, 1].T)
        put(slot, 4 + h, h, hg[slot, h, 2].T)
        put(slot, 5 - 5 * h, h, jnp.zeros((blk, blk), jnp.bfloat16))
        if h == 0:
            put(slot, 2, 1, hg[slot, 0, 1])
            put(slot + 1, 0, 0, hg[slot, 0, 2])
        else:
            put(slot + 1, 1, 0, hg[slot, 1, 1])
            put(slot + 1, 1, 1, hg[slot, 1, 2])

    def scatter_unit(h, a, b):
        scatter(where(h, a, b) + out, h)

    def start_first():
        for h in range(2):
            stage1[h][0].start()
            stage1[h][1].start()

    def start_own():
        for h in range(2):
            stage2[h][0][0].start()
            stage2[h][0][1].start()

    def start_vectors(moves):
        for move in moves:
            v_copies[others.index(move)].start()

    def pass_vectors(moves):
        for dy, dx in moves:
            pass_vector(dy, dx)

    def pass_own():
        for h in range(2):
            pass_on(h, 0, 0)
            scatter_unit(h, 0, 0)

    def take_first():
        for h in range(2):
            for n, a in ((0, 3), (1, 1)):
                stage1[h][n].wait_recv()
                if n == h:
                    stage1[h][2].start()
                stage2[h][a][0].start()
                stage2[h][a][1].start()
                pass_on(h, a, 0)
        for h in range(2):
            scatter_unit(h, 3, 0)
            scatter_unit(h, 1, 0)

    def take_far():
        for h in range(2):
            stage1[h][2].wait_recv()
            stage2[h][2][0].start()
            stage2[h][2][1].start()
            pass_on(h, 2, 0)
        for h in range(2):
            scatter_unit(h, 2, 0)

    def receive(a):
        for h in range(2):
            for n, b in ((0, 3), (1, 1)):
                stage2[h][a][n].wait_recv()
                if n == (0 if a < 2 else 1):
                    stage2[h][a][2].start()
                pass_on(h, a, b)
        for h in range(2):
            scatter_unit(h, a, 3)
            scatter_unit(h, a, 1)

    def receive_far(a):
        for h in range(2):
            stage2[h][a][2].wait_recv()
            pass_on(h, a, 2)
        for h in range(2):
            scatter_unit(h, a, 2)

    def turn(slot):
        ext0[:, lanes(slot, edge)] = vland[slot].T

    near = [(0, 1), (0, 3), (1, 0), (3, 0)]
    middle = [(1, 1), (1, 3), (3, 1), (3, 3), (0, 2), (2, 0)]
    distant = [(1, 2), (3, 2), (2, 1), (2, 3), (2, 2)]

    start_first()
    start_own()
    start_vectors(near)
    pass_own()
    take_first()
    pass_vectors([(0, 0)] + near)
    start_vectors(middle)
    take_far()
    receive(0)
    pass_vectors(middle)
    start_vectors(distant)
    receive(3)
    receive_far(0)
    receive(1)
    receive_far(3)
    pass_vectors(distant)
    receive(2)
    receive_far(1)
    receive_far(2)

    def turn_all(low, high):
        def one(slot, carry):
            turn(slot)
            return carry

        lax.fori_loop(low, high, one, 0)

    turn_all(out, out + pairs)

    def update(step, j):
        source, target = (ext0, ext1) if step % 2 else (ext1, ext0)
        own = lanes(j + out, edge)
        product = jnp.dot(source[:, lanes(j + out - 1, edge, 3)], band[j + out], preferred_element_type=jnp.float32)
        shifted = product - filter_center * source[:, own].astype(jnp.float32)
        if step == 1:
            result = shifted / filter_half
        else:
            result = 2.0 * shifted / filter_half - target[:, own].astype(jnp.float32)
        target[:, own] = result.astype(jnp.bfloat16)

    for step in range(1, DEGREE):
        def inside(j, carry):
            update(step, j)
            return carry

        lax.fori_loop(step, pairs - step, inside, 0, unroll=pairs // 2 - step)

    for p in range(out):
        vector_up(p + pairs - out).wait_recv()
        turn(p)
        vector_down(p).wait_recv()
        turn(p + pairs + out)
    for p in range(out):
        for h in range(2):
            tile_up(p + pairs - out, h).wait_recv()
            scatter(p, h)
            if p < out - 1:
                tile_down(p, h).wait_recv()
                scatter(p + pairs + out, h)

    for step in range(1, DEGREE + 1):
        def outside(i, carry):
            update(step, step - out + i)
            update(step, pairs - step + i)
            return carry

        lax.fori_loop(0, out, outside, 0, unroll=3)

    part = 4 * edge
    width = blk
    half = 2 * width

    def mate(e):
        return (x, x + 1 - 2 * (x % 2), (x + 2) % 4, 3 - x)[e]

    def x_copy(e, first_pair, count, offset, sems):
        pair = 4 * mate(e) + first_pair + out
        return remote(ext0.at[:, lanes(pair, edge, count)], ftx.at[lanes(x, width), pl.ds(offset, count * edge)],
                      sems[0].at[e - 1], sems[1].at[e - 1], {"col": y * 4 + mate(e)})

    f_copies = {e: x_copy(e, 0, 4, edge, (fx_s, fx_r)) for e in (1, 2, 3)}
    lo_copies = {e: x_copy(e, -1, 1, 0, (lo_s, lo_r)) for e in (1, 2, 3)}
    hi_copies = {e: x_copy(e, 4, 1, 5 * edge, (hi_s, hi_r)) for e in (1, 2, 3)}
    inner = pl.ds(edge, part)

    def y_copy(from_slot, to_slot, e, index, is_up):
        piece = lanes(mate(e), width)
        sems = (up_s, up_r) if is_up else (dn_s, dn_r)
        src = ftx.at[piece, inner] if from_slot == 0 else ft.at[from_slot - 1, piece]
        return remote(src, ft.at[to_slot - 1, piece], sems[0].at[index], sems[1].at[index], on_y(1 if is_up else 3))

    own_up = [y_copy(0, 1, e, e, True) for e in range(4)]
    own_dn = [y_copy(0, 2, e, e, False) for e in range(4)]
    fwd_up = {0: y_copy(1, 3, 0, 4, True), 3: y_copy(1, 3, 3, 5, True)}
    fwd_dn = {1: y_copy(2, 3, 1, 4, False), 2: y_copy(2, 3, 2, 5, False)}

    def spread(e):
        own_up[e].start()
        own_dn[e].start()

    for e in (1, 3, 2):
        f_copies[e].start()
    ftx[lanes(x, width), :] = ext0[:, lanes(4 * x - 1 + out, edge, 6)]
    spread(0)
    f_copies[1].wait_recv()
    spread(1)
    f_copies[3].wait_recv()
    spread(3)
    own_up[0].wait_recv()
    fwd_up[0].start()
    f_copies[2].wait_recv()
    spread(2)
    for e in (1, 3, 2):
        lo_copies[e].start()
        hi_copies[e].start()
    own_dn[1].wait_recv()
    fwd_dn[1].start()

    def apply(q):
        rows = pl.ds(q * edge, edge)
        applied = jnp.dot(ftx[:, pl.ds(q * edge, 3 * edge)], band[4 * x + q + out], preferred_element_type=jnp.float32)
        aown[rows, :] = applied.astype(jnp.bfloat16).T
        fown[rows, :] = ftx[:, pl.ds((q + 1) * edge, edge)].T

    apply(1)
    apply(2)
    own_up[3].wait_recv()
    fwd_up[3].start()
    for e in (1, 3, 2):
        lo_copies[e].wait_recv()
        hi_copies[e].wait_recv()
    apply(0)
    apply(3)

    core_copies = [remote(away.at[j], core_in.at[j], core_s.at[j], core_r.at[j], partner) for j in range(4)]
    far = (y - z + 4) % 4 == 2

    def sum_copy(j, d):
        src, dst = share.at[j, :, :, lanes((x + d) % 4, width)], x_in.at[j, d - 1]
        if j < 3:
            src, dst = share.at[j, 1, :, lanes((x + d) % 4, width)], x_in.at[j, d - 1, 1]
        return remote(src, dst, x_s.at[j, d - 1], x_r.at[j, d - 1], on_x(d))

    x_copies = [[sum_copy(j, d) for d in (1, 2, 3)] for j in range(4)]
    kx_copies = [
        remote(ksum.at[:, lanes((x + d) % 4, width)], kx_in.at[d - 1], kx_s.at[d - 1], kx_r.at[d - 1], on_x(d))
        for d in (1, 2, 3)
    ]

    def to_owner(j):
        return (y + (0, 3, 1, 2)[j] - z + 4) % 4

    def z_copy(j):
        d = to_owner(j)
        src, dst = (done.at[j], fin.at[d]) if j == 3 else (done.at[j, 1], fin.at[d, 1])
        return d, remote(src, dst, z_s.at[j], z_r.at[d], on_z(d))

    def zk_copy(j):
        d = to_owner(j)
        return d, remote(share.at[j, 0], zin.at[d], zk_s.at[j], zk_r.at[d], on_z(d))

    def half_tile(j, g):
        target_k = x // 2 if g == 0 else 1 - x // 2
        rows = lanes(target_k, half)
        lhs = ftx[rows, inner] if j == 0 else ft[j - 1, rows, :]
        parts = [jnp.dot(lhs, rhs[...], preferred_element_type=jnp.float32) for rhs in (aown, fown)]

        @pl.when(target_k == k)
        def _():
            for m in range(2):
                keep[j, m] = parts[m]

        @pl.when(target_k != k)
        def _():
            for m in range(2):
                away[j, m] = parts[m].astype(jnp.bfloat16)
            core_copies[j].start()

    def tile(j):
        half_tile(j, 0)
        half_tile(j, 1)

    def over_core(j):
        core_copies[j].wait_recv()
        share[j] = (keep[j] + core_in[j].astype(jnp.float32)).astype(jnp.bfloat16)
        for copy in x_copies[j]:
            copy.start()
        if j < 3:
            d, copy = zk_copy(j)

            @pl.when(d != 0)
            def _():
                copy.start()

            @pl.when(d == 0)
            def _():
                zin[0] = share[j, 0]

    def over_x(j):
        for copy in x_copies[j]:
            copy.wait_recv()
        for m in (0, 1) if j == 3 else (1,):
            total = share[j, m, :, lanes(x, width)].astype(jnp.float32)
            for i in range(3):
                total = total + x_in[j, i, m].astype(jnp.float32)
            done[j, m] = total.astype(jnp.bfloat16)
        d, copy = z_copy(j)

        @pl.when(d != 0)
        def _():
            copy.start()

        @pl.when(d == 0)
        def _():
            for m in (0, 1) if j == 3 else (1,):
                fin[0, m] = done[j, m]

    tile(0)
    own_dn[2].wait_recv()
    fwd_dn[2].start()
    own_up[1].wait_recv()
    own_up[2].wait_recv()
    tile(1)
    over_core(0)
    own_dn[0].wait_recv()
    own_dn[3].wait_recv()
    tile(2)
    over_core(1)
    over_x(0)
    over_core(2)
    fwd_up[0].wait_recv()
    fwd_dn[1].wait_recv()
    half_tile(3, 0)

    @pl.when(x // 2 == k)
    def _():
        over_core(3)

    over_x(1)
    fwd_up[3].wait_recv()
    fwd_dn[2].wait_recv()
    half_tile(3, 1)

    @pl.when(x // 2 != k)
    def _():
        over_core(3)

    over_x(2)

    @pl.when(jnp.logical_not(far))
    def _():
        for d in (1, 2, 3):
            remote(share.at[0, 0], zin.at[d], zk_s.at[0], zk_r.at[d], on_z(d)).wait_recv()
        total = zin[0].astype(jnp.float32)
        for d in (1, 2, 3):
            total = total + zin[d].astype(jnp.float32)
        ksum[...] = total.astype(jnp.bfloat16)
        for copy in kx_copies:
            copy.start()

    over_x(3)

    def add_up(first, rest):
        total = first.astype(jnp.float32)
        for term in rest:
            total = total + term.astype(jnp.float32)
        return total

    @pl.when(jnp.logical_not(far))
    def _():
        for d in (1, 2, 3):
            remote(done.at[0, 1], fin.at[d, 1], z_s.at[0], z_r.at[d], on_z(d)).wait_recv()
        for copy in kx_copies:
            copy.wait_recv()
        sums[0] = add_up(ksum[:, lanes(x, width)], [kx_in[i] for i in range(3)])

    @pl.when(far)
    def _():
        for d in (1, 2, 3):
            remote(done.at[3], fin.at[d], z_s.at[3], z_r.at[d], on_z(d)).wait_recv()
        sums[0] = add_up(fin[0, 0], [fin[d, 0] for d in (1, 2, 3)])

    sums[1] = add_up(fin[0, 1], [fin[d, 1] for d in (1, 2, 3)])

    for h in range(2):
        for copy in (*stage1[h], *(c for copies in stage2[h] for c in copies)):
            copy.wait_send()
        for p in range(out):
            tile_up(p + pairs - out, h).wait_send()
        for p in range(out - 1):
            tile_down(p, h).wait_send()
    for p in range(out):
        vector_up(p + pairs - out).wait_send()
        vector_down(p).wait_send()
    for copy in (*v_copies, *f_copies.values(), *lo_copies.values(), *hi_copies.values(), *own_up,
                 *own_dn, *fwd_up.values(), *fwd_dn.values(), *core_copies, *(c for cs in x_copies for c in cs)):
        copy.wait_send()
    for j in range(4):
        for d, copy in [z_copy(j)] + ([zk_copy(j)] if j < 3 else []):
            @pl.when(d != 0)
            def _():
                copy.wait_send()

    @pl.when(jnp.logical_not(far))
    def _():
        for copy in kx_copies:
            copy.wait_send()


def body(vectors, block_count, block_cols, blocks):
    n_row = lax.axis_size("row")
    n_col = lax.axis_size("col")
    edge, columns = vectors.shape
    local_blocks, slots, blk, _ = blocks.shape
    width = columns // n_col
    scale = 1.0 / math.sqrt(edge * n_row * n_col)
    wide, half, part = 4 * width, 2 * width, 4 * edge
    reach = n_col + 2 * REACH_IN
    anywhere = pl.BlockSpec(memory_space=pl.ANY)
    vmem = pl.BlockSpec(memory_space=pltpu.VMEM)
    bf16 = jnp.bfloat16
    dma = pltpu.SemaphoreType.DMA
    sums = pl.pallas_call(
        functools.partial(kernel, n_row, local_blocks * n_row * n_col),
        out_shape=jax.ShapeDtypeStruct((2, half, width), jnp.float32),
        in_specs=[anywhere] * 4,
        out_specs=vmem,
        scratch_shapes=[
            pltpu.SMEM(block_cols.shape, jnp.int32),
            pltpu.SMEM(block_count.shape, jnp.int32),
            pltpu.VMEM(blocks.shape, bf16),
            pltpu.VMEM((reach - 1, 2, 3, blk, blk), bf16),
            pltpu.VMEM((reach, 6 * blk, edge), bf16),
            pltpu.VMEM((reach, edge, width), bf16),
            pltpu.VMEM((width, reach * edge), bf16),
            pltpu.VMEM((width, reach * edge), bf16),
            pltpu.VMEM((wide, part + 2 * edge), bf16),
            pltpu.VMEM((3, wide, part), bf16),
            pltpu.VMEM((part, wide), bf16),
            pltpu.VMEM((part, wide), bf16),
            pltpu.VMEM((4, 2, half, wide), bf16),
            pltpu.VMEM((4, 2, half, wide), jnp.float32),
            pltpu.VMEM((4, 2, half, wide), bf16),
            pltpu.VMEM((4, 2, half, wide), bf16),
            pltpu.VMEM((4, 3, 2, half, width), bf16),
            pltpu.VMEM((4, 2, half, width), bf16),
            pltpu.VMEM((4, 2, half, width), bf16),
            pltpu.VMEM((4, half, wide), bf16),
            pltpu.VMEM((half, wide), bf16),
            pltpu.VMEM((3, half, width), bf16),
            dma((4,)),
            dma((16,)), dma((16,)), dma((2, REACH_IN)), dma((2, REACH_IN)),
            dma((2, 3)), dma((2, 3)), dma((2, 4, 3)), dma((2, 4, 3)),
            dma((REACH_IN, 2)), dma((REACH_IN, 2)), dma((REACH_IN - 1, 2)), dma((REACH_IN - 1, 2)),
            dma((3,)), dma((3,)), dma((3,)), dma((3,)), dma((3,)), dma((3,)),
            dma((6,)), dma((6,)), dma((6,)), dma((6,)),
            dma((4,)), dma((4,)), dma((4, 3)), dma((4, 3)), dma((4,)), dma((4,)),
            dma((3,)), dma((4,)), dma((3,)), dma((3,)),
        ],
        compiler_params=pltpu.CompilerParams(
            collective_id=0, has_side_effects=True, vmem_limit_bytes=58 * 1024 * 1024
        ),
    )(block_cols, block_count, blocks, vectors)
    return (sums[0] * scale, sums[1] * scale)


def solution(mesh):
    in_specs = (
        P(("row", "col"), None),
        P(("row", "col")),
        P(("row", "col"), None),
        P(("row", "col"), None, None, None),
    )
    out_specs = (P("row", "col"), P("row", "col"))
    return jax.shard_map(body, mesh=mesh, in_specs=in_specs, out_specs=out_specs, check_vma=False)
```

```python
import functools
import math

import jax
import jax.numpy as jnp
from jax import lax
from jax.experimental import pallas as pl
from jax.experimental.pallas import tpu as pltpu
from jax.sharding import PartitionSpec as P

DEGREE = 8
REACH_IN = DEGREE + 1
MESH = pl.DeviceIdType.MESH

filter_center = 0.25
filter_half = 1.75


def kernel(n_row, total_blocks, cols_hbm, count_hbm, blocks_hbm, v_ref, sums,
           cols_ref, count_ref, blocks_ref, hg, band, vland, ext0, ext1, ftx, ft, aown, fown,
           away, keep, core_in, share, x_in, done, fin, zin, ksum, kx_in,
           in_sem, v_s, v_r, vh_s, vh_r, h1_s, h1_r, h2_s, h2_r, eu_s, eu_r, ed_s, ed_r,
           fx_s, fx_r, lo_s, lo_r, hi_s, hi_r, up_s, up_r, dn_s, dn_r, core_s, core_r, x_s, x_r, z_s, z_r,
           zk_s, zk_r, kx_s, kx_r):
    edge = v_ref.shape[0]
    blk = edge // 2
    pairs = 16
    out = REACH_IN
    row, col = lax.axis_index("row"), lax.axis_index("col")
    z, k, y, x = row // 2, row % 2, col // 4, col % 4
    up, down = {"row": (row + 1) % n_row}, {"row": (row + n_row - 1) % n_row}
    partner = {"row": z * 2 + 1 - k}
    across = {"row": (row + n_row - 1 + 2 * k) % n_row}

    def place(dy, dx):
        return ((y + dy) % 4) * 4 + (x + dx) % 4

    def on_x(d):
        return {"col": place(0, d)}

    def on_y(d):
        return {"col": place(d, 0)}

    def on_z(d):
        return {"row": ((z + d) % 4) * 2 + k}

    def remote(src, dst, send, recv, device):
        return pltpu.make_async_remote_copy(
            src_ref=src, dst_ref=dst, send_sem=send, recv_sem=recv, device_id=device, device_id_type=MESH
        )

    def lanes(i, size, count=1):
        return pl.ds(pl.multiple_of(i * size, size), count * size)

    others = [(dy, dx) for dy in range(4) for dx in range(4) if dy or dx]
    barrier = pltpu.get_barrier_semaphore()
    for device in [partner, across, on_z(1), on_z(2), on_z(3)] + [{"col": place(dy, dx)} for dy, dx in others]:
        pl.semaphore_signal(barrier, inc=1, device_id=device, device_id_type=MESH)

    fetch = [
        pltpu.make_async_copy(cols_hbm, cols_ref, in_sem.at[0]),
        pltpu.make_async_copy(count_hbm, count_ref, in_sem.at[1]),
        pltpu.make_async_copy(blocks_hbm, blocks_ref, in_sem.at[2]),
        pltpu.make_async_copy(v_ref.at[:, lanes(col, blk)], vland.at[col + out], in_sem.at[3]),
    ]
    for copy in fetch:
        copy.start()
    for copy in fetch[:3]:
        copy.wait()

    first = (row * pairs + col) * 2
    for i in range(2):
        for offset in range(3):
            tile = jnp.zeros((blk, blk), jnp.bfloat16)
            for slot in range(5):
                relative = lax.rem(cols_ref[i, slot] - first - i + total_blocks, total_blocks)
                hit = jnp.logical_and(relative == offset, slot < count_ref[i])
                tile = jnp.where(hit, blocks_ref[i, slot], tile)
            hg[col + out, i, offset] = tile

    pl.semaphore_wait(barrier, 20)

    def where(h, a, b):
        return place(b, a) if h == 0 else place(a, b)

    def tile_copy(h, a, b, to_a, to_b, send, recv):
        unit = hg.at[where(h, a, b) + out, h]
        return remote(unit, unit, send, recv, {"col": where(h, to_a, to_b)})

    stage1, stage2 = [], []
    for h in range(2):
        sign = 1 if h == 0 else 3
        moves = [(0, 1), (0, 3), (4 - sign, sign)]
        stage1.append([tile_copy(h, a, 0, to, 0, h1_s.at[h, n], h1_r.at[h, n]) for n, (a, to) in enumerate(moves)])
        lists = []
        for a in range(4):
            sign = 1 if a < 2 else 3
            moves = [(0, 1), (0, 3), (4 - sign, sign)]
            lists.append([
                tile_copy(h, a, b, 0, to, h2_s.at[h, a, n], h2_r.at[h, a, n]) for n, (b, to) in enumerate(moves)
            ])
        stage2.append(lists)

    v_copies = [
        remote(v_ref.at[:, lanes(place(dy, dx), blk)], vland.at[col + out], v_s.at[dy * 4 + dx],
               v_r.at[dy * 4 + dx], {"col": place(dy, dx)})
        for dy, dx in others
    ]

    def tile_up(p, h):
        return remote(hg.at[p + out, h], hg.at[p + out - pairs, h], eu_s.at[p + out - pairs, h],
                      eu_r.at[p + out - pairs, h], up)

    def tile_down(p, h):
        return remote(hg.at[p + out, h], hg.at[p + out + pairs, h], ed_s.at[p, h], ed_r.at[p, h], down)

    def pass_on(h, a, b):
        p = where(h, a, b)

        @pl.when(p >= pairs - out)
        def _():
            tile_up(p, h).start()

        @pl.when(p < out - 1)
        def _():
            tile_down(p, h).start()

    def vector_up(p):
        return remote(vland.at[p + out], vland.at[p + out - pairs], vh_s.at[0, p + out - pairs],
                      vh_r.at[0, p + out - pairs], up)

    def vector_down(p):
        return remote(vland.at[p + out], vland.at[p + out + pairs], vh_s.at[1, p], vh_r.at[1, p], down)

    def pass_vector(dy, dx):
        if dy or dx:
            v_copies[others.index((dy, dx))].wait_recv()
        else:
            fetch[3].wait()
        p = place(4 - dy, 4 - dx)

        @pl.when(p >= pairs - out)
        def _():
            vector_up(p).start()

        @pl.when(p < out)
        def _():
            vector_down(p).start()

    def scatter(slot, h):
        def put(s, r, c, value):
            band[s, pl.ds(r * blk, blk), pl.ds(c * blk, blk)] = value

        put(slot, 2 + h, h, hg[slot, h, 0])
        put(slot, 3 + h, h, hg[slot, h, 1].T)
        put(slot, 4 + h, h, hg[slot, h, 2].T)
        put(slot, 5 - 5 * h, h, jnp.zeros((blk, blk), jnp.bfloat16))
        if h == 0:
            put(slot, 2, 1, hg[slot, 0, 1])
            put(slot + 1, 0, 0, hg[slot, 0, 2])
        else:
            put(slot + 1, 1, 0, hg[slot, 1, 1])
            put(slot + 1, 1, 1, hg[slot, 1, 2])

    def scatter_unit(h, a, b):
        scatter(where(h, a, b) + out, h)

    def start_first():
        for h in range(2):
            stage1[h][0].start()
            stage1[h][1].start()

    def start_own():
        for h in range(2):
            stage2[h][0][0].start()
            stage2[h][0][1].start()

    def start_vectors(moves):
        for move in moves:
            v_copies[others.index(move)].start()

    def pass_vectors(moves):
        for dy, dx in moves:
            pass_vector(dy, dx)

    def pass_own():
        for h in range(2):
            pass_on(h, 0, 0)
            scatter_unit(h, 0, 0)

    def take_first():
        for h in range(2):
            for n, a in ((0, 3), (1, 1)):
                stage1[h][n].wait_recv()
                if n == h:
                    stage1[h][2].start()
                stage2[h][a][0].start()
                stage2[h][a][1].start()
                pass_on(h, a, 0)
        for h in range(2):
            scatter_unit(h, 3, 0)
            scatter_unit(h, 1, 0)

    def take_far():
        for h in range(2):
            stage1[h][2].wait_recv()
            stage2[h][2][0].start()
            stage2[h][2][1].start()
            pass_on(h, 2, 0)
        for h in range(2):
            scatter_unit(h, 2, 0)

    def receive(a):
        for h in range(2):
            for n, b in ((0, 3), (1, 1)):
                stage2[h][a][n].wait_recv()
                if n == (0 if a < 2 else 1):
                    stage2[h][a][2].start()
                pass_on(h, a, b)
        for h in range(2):
            scatter_unit(h, a, 3)
            scatter_unit(h, a, 1)

    def receive_far(a):
        for h in range(2):
            stage2[h][a][2].wait_recv()
            pass_on(h, a, 2)
        for h in range(2):
            scatter_unit(h, a, 2)

    def turn(slot):
        ext0[:, lanes(slot, edge)] = vland[slot].T

    near = [(0, 1), (0, 3), (1, 0), (3, 0)]
    middle = [(1, 1), (1, 3), (3, 1), (3, 3), (0, 2), (2, 0)]
    distant = [(1, 2), (3, 2), (2, 1), (2, 3), (2, 2)]

    start_first()
    start_own()
    start_vectors(near)
    pass_own()
    take_first()
    pass_vectors([(0, 0)] + near)
    start_vectors(middle)
    take_far()
    receive(0)
    pass_vectors(middle)
    start_vectors(distant)
    receive(3)
    receive_far(0)
    receive(1)
    receive_far(3)
    pass_vectors(distant)
    receive(2)
    receive_far(1)
    receive_far(2)

    def turn_all(low, high):
        def one(slot, carry):
            turn(slot)
            return carry

        lax.fori_loop(low, high, one, 0)

    turn_all(out, out + pairs)

    def update(step, j):
        source, target = (ext0, ext1) if step % 2 else (ext1, ext0)
        own = lanes(j + out, edge)
        product = jnp.dot(source[:, lanes(j + out - 1, edge, 3)], band[j + out], preferred_element_type=jnp.float32)
        shifted = product - filter_center * source[:, own].astype(jnp.float32)
        if step == 1:
            result = shifted / filter_half
        else:
            result = 2.0 * shifted / filter_half - target[:, own].astype(jnp.float32)
        target[:, own] = result.astype(jnp.bfloat16)

    for step in range(1, DEGREE):
        def inside(j, carry):
            update(step, j)
            return carry

        lax.fori_loop(step, pairs - step, inside, 0, unroll=pairs // 2 - step)

    for p in range(out):
        vector_up(p + pairs - out).wait_recv()
        turn(p)
        vector_down(p).wait_recv()
        turn(p + pairs + out)
    for p in range(out):
        for h in range(2):
            tile_up(p + pairs - out, h).wait_recv()
            scatter(p, h)
            if p < out - 1:
                tile_down(p, h).wait_recv()
                scatter(p + pairs + out, h)

    for step in range(1, DEGREE + 1):
        def outside(i, carry):
            update(step, step - out + i)
            update(step, pairs - step + i)
            return carry

        lax.fori_loop(0, out, outside, 0, unroll=out)

    part = 4 * edge
    width = blk
    half = 2 * width

    def mate(e):
        return (x, x + 1 - 2 * (x % 2), (x + 2) % 4, 3 - x)[e]

    def x_copy(e, first_pair, count, offset, sems):
        pair = 4 * mate(e) + first_pair + out
        return remote(ext0.at[:, lanes(pair, edge, count)], ftx.at[lanes(x, width), pl.ds(offset, count * edge)],
                      sems[0].at[e - 1], sems[1].at[e - 1], {"col": y * 4 + mate(e)})

    f_copies = {e: x_copy(e, 0, 4, edge, (fx_s, fx_r)) for e in (1, 2, 3)}
    lo_copies = {e: x_copy(e, -1, 1, 0, (lo_s, lo_r)) for e in (1, 2, 3)}
    hi_copies = {e: x_copy(e, 4, 1, 5 * edge, (hi_s, hi_r)) for e in (1, 2, 3)}
    inner = pl.ds(edge, part)

    def y_copy(from_slot, to_slot, e, index, is_up):
        piece = lanes(mate(e), width)
        sems = (up_s, up_r) if is_up else (dn_s, dn_r)
        src = ftx.at[piece, inner] if from_slot == 0 else ft.at[from_slot - 1, piece]
        return remote(src, ft.at[to_slot - 1, piece], sems[0].at[index], sems[1].at[index], on_y(1 if is_up else 3))

    own_up = [y_copy(0, 1, e, e, True) for e in range(4)]
    own_dn = [y_copy(0, 2, e, e, False) for e in range(4)]
    fwd_up = {0: y_copy(1, 3, 0, 4, True), 3: y_copy(1, 3, 3, 5, True)}
    fwd_dn = {1: y_copy(2, 3, 1, 4, False), 2: y_copy(2, 3, 2, 5, False)}

    def spread(e):
        own_up[e].start()
        own_dn[e].start()

    for e in (1, 3, 2):
        f_copies[e].start()
    ftx[lanes(x, width), :] = ext0[:, lanes(4 * x - 1 + out, edge, 6)]
    spread(0)
    f_copies[1].wait_recv()
    spread(1)
    f_copies[3].wait_recv()
    spread(3)
    f_copies[2].wait_recv()
    spread(2)
    for e in (1, 3, 2):
        lo_copies[e].start()
        hi_copies[e].start()

    def apply(q):
        rows = pl.ds(q * edge, edge)
        applied = jnp.dot(ftx[:, pl.ds(q * edge, 3 * edge)], band[4 * x + q + out], preferred_element_type=jnp.float32)
        aown[rows, :] = applied.astype(jnp.bfloat16).T
        fown[rows, :] = ftx[:, pl.ds((q + 1) * edge, edge)].T

    for e in (0, 1, 3):
        own_up[e].wait_recv()
        own_dn[e].wait_recv()
    fwd_up[0].start()
    fwd_dn[1].start()
    apply(1)
    apply(2)
    own_up[2].wait_recv()
    own_dn[2].wait_recv()
    fwd_up[3].start()
    fwd_dn[2].start()
    for e in (1, 3, 2):
        lo_copies[e].wait_recv()
        hi_copies[e].wait_recv()
    apply(0)
    apply(3)

    core_copies = [
        [remote(away.at[j, m], core_in.at[j, m], core_s.at[j, m], core_r.at[j, m], partner) for m in range(2)]
        for j in range(4)
    ]
    far = (y - z + 4) % 4 >= 2

    over_z_first = [(0, 0), (1, 0)]
    x_copies = {
        (j, m): [
            remote(share.at[j, m, :, lanes((x + d) % 4, width)], x_in.at[j, d - 1, m], x_s.at[j, m, d - 1],
                   x_r.at[j, m, d - 1], on_x(d))
            for d in (1, 2, 3)
        ]
        for j in range(4) for m in range(2) if (j, m) not in over_z_first
    }
    kx_copies = [
        remote(ksum.at[:, lanes((x + d) % 4, width)], kx_in.at[d - 1], kx_s.at[d - 1], kx_r.at[d - 1], on_x(d))
        for d in (1, 2, 3)
    ]

    def to_owner(j):
        return (y + (0, 3, 1, 2)[j] - z + 4) % 4

    def z_copy(j, m):
        d = to_owner(j)
        if (j, m) in over_z_first:
            return d, remote(share.at[j, 0], zin.at[d], zk_s.at[j], zk_r.at[d], on_z(d))
        return d, remote(done.at[j, m], fin.at[d, m], z_s.at[j, m], z_r.at[d, m], on_z(d))

    def send_over_z(j, m):
        d, copy = z_copy(j, m)

        @pl.when(d != 0)
        def _():
            copy.start()

        @pl.when(d == 0)
        def _():
            if (j, m) in over_z_first:
                zin[0] = share[j, 0]
            else:
                fin[0, m] = done[j, m]

    def half_tile(j, g):
        target_k = x // 2 if g == 0 else 1 - x // 2
        rows = lanes(target_k, half)
        lhs = ftx[rows, inner] if j == 0 else ft[j - 1, rows, :]
        for m, rhs in enumerate((aown, fown)):
            product = jnp.dot(lhs, rhs[...], preferred_element_type=jnp.float32)

            @pl.when(target_k == k)
            def _():
                keep[j, m] = product

            @pl.when(target_k != k)
            def _():
                away[j, m] = product.astype(jnp.bfloat16)
                core_copies[j][m].start()

    def tile(j):
        half_tile(j, 0)
        half_tile(j, 1)

    def over_core(j):
        for m in range(2):
            core_copies[j][m].wait_recv()
            share[j, m] = (keep[j, m] + core_in[j, m].astype(jnp.float32)).astype(jnp.bfloat16)
            if (j, m) in over_z_first:
                send_over_z(j, m)
            else:
                for copy in x_copies[j, m]:
                    copy.start()

    def add_up(first, rest):
        total = first.astype(jnp.float32)
        for term in rest:
            total = total + term.astype(jnp.float32)
        return total

    def over_x(j):
        for m in range(2):
            if (j, m) in over_z_first:
                continue
            for copy in x_copies[j, m]:
                copy.wait_recv()
            total = add_up(share[j, m, :, lanes(x, width)], [x_in[j, i, m] for i in range(3)])
            done[j, m] = total.astype(jnp.bfloat16)
            send_over_z(j, m)

    tile(0)
    tile(1)
    over_core(0)
    tile(2)
    over_core(1)
    over_x(0)
    over_core(2)
    fwd_up[0].wait_recv()
    fwd_dn[1].wait_recv()
    half_tile(3, 0)

    @pl.when(x // 2 == k)
    def _():
        over_core(3)

    over_x(1)
    fwd_up[3].wait_recv()
    fwd_dn[2].wait_recv()
    half_tile(3, 1)

    @pl.when(x // 2 != k)
    def _():
        over_core(3)

    over_x(2)

    @pl.when(jnp.logical_not(far))
    def _():
        for d in (1, 2, 3):
            remote(share.at[0, 0], zin.at[d], zk_s.at[0], zk_r.at[d], on_z(d)).wait_recv()
        ksum[...] = add_up(zin[0], [zin[d] for d in (1, 2, 3)]).astype(jnp.bfloat16)
        for copy in kx_copies:
            copy.start()

    over_x(3)

    def owned(m):
        for d in (1, 2, 3):
            remote(done.at[0, m], fin.at[d, m], z_s.at[0, m], z_r.at[d, m], on_z(d)).wait_recv()
        return add_up(fin[0, m], [fin[d, m] for d in (1, 2, 3)])

    @pl.when(jnp.logical_not(far))
    def _():
        for copy in kx_copies:
            copy.wait_recv()
        sums[0] = add_up(ksum[:, lanes(x, width)], [kx_in[i] for i in range(3)])

    @pl.when(far)
    def _():
        sums[0] = owned(0)

    sums[1] = owned(1)

    for h in range(2):
        for copy in (*stage1[h], *(c for copies in stage2[h] for c in copies)):
            copy.wait_send()
        for p in range(out):
            tile_up(p + pairs - out, h).wait_send()
        for p in range(out - 1):
            tile_down(p, h).wait_send()
    for p in range(out):
        vector_up(p + pairs - out).wait_send()
        vector_down(p).wait_send()
    for copy in (*v_copies, *f_copies.values(), *lo_copies.values(), *hi_copies.values(), *own_up,
                 *own_dn, *fwd_up.values(), *fwd_dn.values(), *(c for cs in core_copies for c in cs),
                 *(c for cs in x_copies.values() for c in cs)):
        copy.wait_send()
    for j in range(4):
        for m in range(2):
            d, copy = z_copy(j, m)

            @pl.when(d != 0)
            def _():
                copy.wait_send()

    @pl.when(jnp.logical_not(far))
    def _():
        for copy in kx_copies:
            copy.wait_send()


def body(vectors, block_count, block_cols, blocks):
    n_row = lax.axis_size("row")
    n_col = lax.axis_size("col")
    edge, columns = vectors.shape
    local_blocks, slots, blk, _ = blocks.shape
    width = columns // n_col
    scale = 1.0 / math.sqrt(edge * n_row * n_col)
    wide, half, part = 4 * width, 2 * width, 4 * edge
    reach = n_col + 2 * REACH_IN
    anywhere = pl.BlockSpec(memory_space=pl.ANY)
    vmem = pl.BlockSpec(memory_space=pltpu.VMEM)
    bf16 = jnp.bfloat16
    dma = pltpu.SemaphoreType.DMA
    sums = pl.pallas_call(
        functools.partial(kernel, n_row, local_blocks * n_row * n_col),
        out_shape=jax.ShapeDtypeStruct((2, half, width), jnp.float32),
        in_specs=[anywhere] * 4,
        out_specs=vmem,
        scratch_shapes=[
            pltpu.SMEM(block_cols.shape, jnp.int32),
            pltpu.SMEM(block_count.shape, jnp.int32),
            pltpu.VMEM(blocks.shape, bf16),
            pltpu.VMEM((reach - 1, 2, 3, blk, blk), bf16),
            pltpu.VMEM((reach, 6 * blk, edge), bf16),
            pltpu.VMEM((reach, edge, width), bf16),
            pltpu.VMEM((width, reach * edge), bf16),
            pltpu.VMEM((width, reach * edge), bf16),
            pltpu.VMEM((wide, part + 2 * edge), bf16),
            pltpu.VMEM((3, wide, part), bf16),
            pltpu.VMEM((part, wide), bf16),
            pltpu.VMEM((part, wide), bf16),
            pltpu.VMEM((4, 2, half, wide), bf16),
            pltpu.VMEM((4, 2, half, wide), jnp.float32),
            pltpu.VMEM((4, 2, half, wide), bf16),
            pltpu.VMEM((4, 2, half, wide), bf16),
            pltpu.VMEM((4, 3, 2, half, width), bf16),
            pltpu.VMEM((4, 2, half, width), bf16),
            pltpu.VMEM((4, 2, half, width), bf16),
            pltpu.VMEM((4, half, wide), bf16),
            pltpu.VMEM((half, wide), bf16),
            pltpu.VMEM((3, half, width), bf16),
            dma((4,)),
            dma((16,)), dma((16,)), dma((2, REACH_IN)), dma((2, REACH_IN)),
            dma((2, 3)), dma((2, 3)), dma((2, 4, 3)), dma((2, 4, 3)),
            dma((REACH_IN, 2)), dma((REACH_IN, 2)), dma((REACH_IN - 1, 2)), dma((REACH_IN - 1, 2)),
            dma((3,)), dma((3,)), dma((3,)), dma((3,)), dma((3,)), dma((3,)),
            dma((6,)), dma((6,)), dma((6,)), dma((6,)),
            dma((4, 2)), dma((4, 2)), dma((4, 2, 3)), dma((4, 2, 3)), dma((4, 2)), dma((4, 2)),
            dma((2,)), dma((4,)), dma((3,)), dma((3,)),
        ],
        compiler_params=pltpu.CompilerParams(
            collective_id=0, has_side_effects=True, vmem_limit_bytes=58 * 1024 * 1024
        ),
    )(block_cols, block_count, blocks, vectors)
    return (sums[0] * scale, sums[1] * scale)


def solution(mesh):
    in_specs = (
        P(("row", "col"), None),
        P(("row", "col")),
        P(("row", "col"), None),
        P(("row", "col"), None, None, None),
    )
    out_specs = (P("row", "col"), P("row", "col"))
    return jax.shard_map(body, mesh=mesh, in_specs=in_specs, out_specs=out_specs, check_vma=False)
```

```python
import functools
import math

import jax
import jax.numpy as jnp
from jax import lax
from jax.experimental import pallas as pl
from jax.experimental.pallas import tpu as pltpu
from jax.sharding import PartitionSpec as P

DEGREE = 8
REACH_IN = DEGREE + 1
MESH = pl.DeviceIdType.MESH

filter_center = 0.25
filter_half = 1.75


def kernel(n_row, total_blocks, cols_hbm, count_hbm, blocks_hbm, v_ref, sums,
           cols_ref, count_ref, blocks_ref, hg, band, vland, ext0, ext1, ftx, ft, aown, fown,
           away, keep, core_in, share, x_in, done, fin, zin, ksum, kx_in,
           in_sem, v_s, v_r, vh_s, vh_r, h1_s, h1_r, h2_s, h2_r, eu_s, eu_r, ed_s, ed_r,
           fx_s, fx_r, lo_s, lo_r, hi_s, hi_r, up_s, up_r, dn_s, dn_r, core_s, core_r, x_s, x_r, z_s, z_r,
           zk_s, zk_r, kx_s, kx_r):
    edge = v_ref.shape[0]
    blk = edge // 2
    pairs = 16
    out = REACH_IN
    row, col = lax.axis_index("row"), lax.axis_index("col")
    z, k, y, x = row // 2, row % 2, col // 4, col % 4
    up, down = {"row": (row + 1) % n_row}, {"row": (row + n_row - 1) % n_row}
    partner = {"row": z * 2 + 1 - k}
    across = {"row": (row + n_row - 1 + 2 * k) % n_row}

    def place(dy, dx):
        return ((y + dy) % 4) * 4 + (x + dx) % 4

    def on_x(d):
        return {"col": place(0, d)}

    def on_y(d):
        return {"col": place(d, 0)}

    def on_z(d):
        return {"row": ((z + d) % 4) * 2 + k}

    def remote(src, dst, send, recv, device):
        return pltpu.make_async_remote_copy(
            src_ref=src, dst_ref=dst, send_sem=send, recv_sem=recv, device_id=device, device_id_type=MESH
        )

    def lanes(i, size, count=1):
        return pl.ds(pl.multiple_of(i * size, size), count * size)

    others = [(dy, dx) for dy in range(4) for dx in range(4) if dy or dx]
    barrier = pltpu.get_barrier_semaphore()
    for device in [partner, across, on_z(1), on_z(2), on_z(3)] + [{"col": place(dy, dx)} for dy, dx in others]:
        pl.semaphore_signal(barrier, inc=1, device_id=device, device_id_type=MESH)

    fetch = [
        pltpu.make_async_copy(cols_hbm, cols_ref, in_sem.at[0]),
        pltpu.make_async_copy(count_hbm, count_ref, in_sem.at[1]),
        pltpu.make_async_copy(blocks_hbm, blocks_ref, in_sem.at[2]),
        pltpu.make_async_copy(v_ref.at[:, lanes(col, blk)], vland.at[col + out], in_sem.at[3]),
    ]
    for copy in fetch:
        copy.start()
    for copy in fetch[:3]:
        copy.wait()

    first = (row * pairs + col) * 2
    for i in range(2):
        for offset in range(3):
            tile = jnp.zeros((blk, blk), jnp.bfloat16)
            for slot in range(5):
                relative = lax.rem(cols_ref[i, slot] - first - i + total_blocks, total_blocks)
                hit = jnp.logical_and(relative == offset, slot < count_ref[i])
                tile = jnp.where(hit, blocks_ref[i, slot], tile)
            hg[col + out, i, offset] = tile

    pl.semaphore_wait(barrier, 20)

    def where(h, a, b):
        return place(b, a) if h == 0 else place(a, b)

    def tile_copy(h, a, b, to_a, to_b, send, recv):
        unit = hg.at[where(h, a, b) + out, h]
        return remote(unit, unit, send, recv, {"col": where(h, to_a, to_b)})

    stage1, stage2 = [], []
    for h in range(2):
        sign = 1 if h == 0 else 3
        moves = [(0, 1), (0, 3), (4 - sign, sign)]
        stage1.append([tile_copy(h, a, 0, to, 0, h1_s.at[h, n], h1_r.at[h, n]) for n, (a, to) in enumerate(moves)])
        lists = []
        for a in range(4):
            sign = 1 if a < 2 else 3
            moves = [(0, 1), (0, 3), (4 - sign, sign)]
            lists.append([
                tile_copy(h, a, b, 0, to, h2_s.at[h, a, n], h2_r.at[h, a, n]) for n, (b, to) in enumerate(moves)
            ])
        stage2.append(lists)

    v_copies = [
        remote(v_ref.at[:, lanes(place(dy, dx), blk)], vland.at[col + out], v_s.at[dy * 4 + dx],
               v_r.at[dy * 4 + dx], {"col": place(dy, dx)})
        for dy, dx in others
    ]

    def tile_up(p, h):
        return remote(hg.at[p + out, h], hg.at[p + out - pairs, h], eu_s.at[p + out - pairs, h],
                      eu_r.at[p + out - pairs, h], up)

    def tile_down(p, h):
        return remote(hg.at[p + out, h], hg.at[p + out + pairs, h], ed_s.at[p, h], ed_r.at[p, h], down)

    def pass_on(h, a, b):
        p = where(h, a, b)

        @pl.when(p >= pairs - out)
        def _():
            tile_up(p, h).start()

        @pl.when(p < out - 1)
        def _():
            tile_down(p, h).start()

    def vector_up(p):
        return remote(vland.at[p + out], vland.at[p + out - pairs], vh_s.at[0, p + out - pairs],
                      vh_r.at[0, p + out - pairs], up)

    def vector_down(p):
        return remote(vland.at[p + out], vland.at[p + out + pairs], vh_s.at[1, p], vh_r.at[1, p], down)

    def pass_vector(dy, dx):
        if dy or dx:
            v_copies[others.index((dy, dx))].wait_recv()
        else:
            fetch[3].wait()
        p = place(4 - dy, 4 - dx)

        @pl.when(p >= pairs - out)
        def _():
            vector_up(p).start()

        @pl.when(p < out)
        def _():
            vector_down(p).start()

    def scatter(slot, h):
        def put(s, r, c, value):
            band[s, pl.ds(r * blk, blk), pl.ds(c * blk, blk)] = value

        put(slot, 2 + h, h, hg[slot, h, 0])
        put(slot, 3 + h, h, hg[slot, h, 1].T)
        put(slot, 4 + h, h, hg[slot, h, 2].T)
        put(slot, 5 - 5 * h, h, jnp.zeros((blk, blk), jnp.bfloat16))
        if h == 0:
            put(slot, 2, 1, hg[slot, 0, 1])
            put(slot + 1, 0, 0, hg[slot, 0, 2])
        else:
            put(slot + 1, 1, 0, hg[slot, 1, 1])
            put(slot + 1, 1, 1, hg[slot, 1, 2])

    def scatter_unit(h, a, b):
        scatter(where(h, a, b) + out, h)

    def start_first():
        for h in range(2):
            stage1[h][0].start()
            stage1[h][1].start()

    def start_own():
        for h in range(2):
            stage2[h][0][0].start()
            stage2[h][0][1].start()

    def start_vectors(moves):
        for move in moves:
            v_copies[others.index(move)].start()

    def pass_vectors(moves):
        for dy, dx in moves:
            pass_vector(dy, dx)

    def pass_own():
        for h in range(2):
            pass_on(h, 0, 0)
            scatter_unit(h, 0, 0)

    def take_first():
        for h in range(2):
            for n, a in ((0, 3), (1, 1)):
                stage1[h][n].wait_recv()
                if n == h:
                    stage1[h][2].start()
                stage2[h][a][0].start()
                stage2[h][a][1].start()
                pass_on(h, a, 0)
        for h in range(2):
            scatter_unit(h, 3, 0)
            scatter_unit(h, 1, 0)

    def take_far():
        for h in range(2):
            stage1[h][2].wait_recv()
            stage2[h][2][0].start()
            stage2[h][2][1].start()
            pass_on(h, 2, 0)
        for h in range(2):
            scatter_unit(h, 2, 0)

    def receive(a):
        for h in range(2):
            for n, b in ((0, 3), (1, 1)):
                stage2[h][a][n].wait_recv()
                if n == (0 if a < 2 else 1):
                    stage2[h][a][2].start()
                pass_on(h, a, b)
        for h in range(2):
            scatter_unit(h, a, 3)
            scatter_unit(h, a, 1)

    def receive_far(a):
        for h in range(2):
            stage2[h][a][2].wait_recv()
            pass_on(h, a, 2)
        for h in range(2):
            scatter_unit(h, a, 2)

    def turn(slot):
        ext0[:, lanes(slot, edge)] = vland[slot].T

    near = [(0, 1), (0, 3), (1, 0), (3, 0)]
    middle = [(1, 1), (1, 3), (3, 1), (3, 3), (0, 2), (2, 0)]
    distant = [(1, 2), (3, 2), (2, 1), (2, 3), (2, 2)]

    start_first()
    start_own()
    start_vectors(near)
    pass_own()
    take_first()
    pass_vectors([(0, 0)] + near)
    start_vectors(middle)
    take_far()
    receive(0)
    pass_vectors(middle)
    start_vectors(distant)
    receive(3)
    receive_far(0)
    receive(1)
    receive_far(3)
    pass_vectors(distant)
    receive(2)
    receive_far(1)
    receive_far(2)

    def turn_all(low, high):
        def one(slot, carry):
            turn(slot)
            return carry

        lax.fori_loop(low, high, one, 0)

    turn_all(out, out + pairs)

    def update(step, j):
        source, target = (ext0, ext1) if step % 2 else (ext1, ext0)
        own = lanes(j + out, edge)
        product = jnp.dot(source[:, lanes(j + out - 1, edge, 3)], band[j + out], preferred_element_type=jnp.float32)
        shifted = product - filter_center * source[:, own].astype(jnp.float32)
        if step == 1:
            result = shifted / filter_half
        else:
            result = 2.0 * shifted / filter_half - target[:, own].astype(jnp.float32)
        target[:, own] = result.astype(jnp.bfloat16)

    for step in range(1, DEGREE):
        def inside(j, carry):
            update(step, j)
            return carry

        lax.fori_loop(step, pairs - step, inside, 0, unroll=pairs // 2 - step)

    for p in range(out):
        vector_up(p + pairs - out).wait_recv()
        turn(p)
        vector_down(p).wait_recv()
        turn(p + pairs + out)
    for p in range(out):
        for h in range(2):
            tile_up(p + pairs - out, h).wait_recv()
            scatter(p, h)
            if p < out - 1:
                tile_down(p, h).wait_recv()
                scatter(p + pairs + out, h)

    for step in range(1, DEGREE + 1):
        def outside(i, carry):
            update(step, step - out + i)
            update(step, pairs - step + i)
            return carry

        lax.fori_loop(0, out, outside, 0, unroll=out)

    part = 4 * edge
    width = blk
    half = 2 * width

    def mate(e):
        return (x, x + 1 - 2 * (x % 2), (x + 2) % 4, 3 - x)[e]

    def x_copy(e, first_pair, count, offset, sems):
        pair = 4 * mate(e) + first_pair + out
        return remote(ext0.at[:, lanes(pair, edge, count)], ftx.at[lanes(x, width), pl.ds(offset, count * edge)],
                      sems[0].at[e - 1], sems[1].at[e - 1], {"col": y * 4 + mate(e)})

    f_copies = {e: x_copy(e, 0, 4, edge, (fx_s, fx_r)) for e in (1, 2, 3)}
    lo_copies = {e: x_copy(e, -1, 1, 0, (lo_s, lo_r)) for e in (1, 2, 3)}
    hi_copies = {e: x_copy(e, 4, 1, 5 * edge, (hi_s, hi_r)) for e in (1, 2, 3)}
    inner = pl.ds(edge, part)

    def y_copy(from_slot, to_slot, e, index, is_up):
        piece = lanes(mate(e), width)
        sems = (up_s, up_r) if is_up else (dn_s, dn_r)
        src = ftx.at[piece, inner] if from_slot == 0 else ft.at[from_slot - 1, piece]
        return remote(src, ft.at[to_slot - 1, piece], sems[0].at[index], sems[1].at[index], on_y(1 if is_up else 3))

    own_up = [y_copy(0, 1, e, e, True) for e in range(4)]
    own_dn = [y_copy(0, 2, e, e, False) for e in range(4)]
    fwd_up, fwd_dn = y_copy(1, 3, 0, 4, True), y_copy(2, 3, 1, 4, False)

    def late_rows(i):
        return lanes(2 * (1 - x // 2) + i, width)

    def late_copy(i, is_up):
        sems = (up_s, up_r) if is_up else (dn_s, dn_r)
        depth = pl.ds(0 if is_up else part // 2, part // 2)
        return remote(ft.at[0 if is_up else 1, late_rows(i), depth], ft.at[2, late_rows(i), depth],
                      sems[0].at[5 + i], sems[1].at[5 + i], on_y(1 if is_up else 3))

    late = [[late_copy(i, is_up) for is_up in (True, False)] for i in range(2)]

    def spread(e):
        own_up[e].start()
        own_dn[e].start()

    for e in (1, 3, 2):
        f_copies[e].start()
    ftx[lanes(x, width), :] = ext0[:, lanes(4 * x - 1 + out, edge, 6)]
    spread(0)
    f_copies[1].wait_recv()
    spread(1)
    f_copies[3].wait_recv()
    spread(3)
    f_copies[2].wait_recv()
    spread(2)
    for e in (1, 3, 2):
        lo_copies[e].start()
        hi_copies[e].start()

    def apply(q):
        rows = pl.ds(q * edge, edge)
        applied = jnp.dot(ftx[:, pl.ds(q * edge, 3 * edge)], band[4 * x + q + out], preferred_element_type=jnp.float32)
        aown[rows, :] = applied.astype(jnp.bfloat16).T
        fown[rows, :] = ftx[:, pl.ds((q + 1) * edge, edge)].T

    for e in (0, 1, 3):
        own_up[e].wait_recv()
        own_dn[e].wait_recv()
    fwd_up.start()
    fwd_dn.start()
    apply(1)
    apply(2)
    own_up[2].wait_recv()
    own_dn[2].wait_recv()
    for i in range(2):
        for copy in late[i]:
            copy.start()
    for e in (1, 3, 2):
        lo_copies[e].wait_recv()
        hi_copies[e].wait_recv()
    apply(0)
    apply(3)

    def parts(j):
        return range(2 if j == 3 else 1)

    def part_rows(j, i):
        return pl.ds(i * width, width) if j == 3 else pl.ds(0, half)

    core_copies = {
        (j, m, i): remote(away.at[j, m, part_rows(j, i)], core_in.at[j, m, part_rows(j, i)], core_s.at[j, m, i],
                          core_r.at[j, m, i], partner)
        for j in range(4) for m in range(2) for i in parts(j)
    }
    owner = (y - z + 4) % 4
    far = owner >= 2

    over_z_first = [(0, 0), (1, 0)]
    x_copies = {
        (j, m, i): [
            remote(share.at[j, m, part_rows(j, i), lanes((x + d) % 4, width)], x_in.at[j, d - 1, m, part_rows(j, i)],
                   x_s.at[j, m, i, d - 1], x_r.at[j, m, i, d - 1], on_x(d))
            for d in (1, 2, 3)
        ]
        for j in range(4) for m in range(2) for i in parts(j) if (j, m) not in over_z_first
    }
    kx_copies = [
        remote(ksum.at[:, lanes((x + d) % 4, width)], kx_in.at[d - 1], kx_s.at[d - 1], kx_r.at[d - 1], on_x(d))
        for d in (1, 2, 3)
    ]

    def to_owner(j):
        return (y + (0, 3, 1, 2)[j] - z + 4) % 4

    def z_copy(j, m, i):
        d = to_owner(j)
        if (j, m) in over_z_first:
            return d, remote(share.at[j, 0], zin.at[d], zk_s.at[j], zk_r.at[d], on_z(d))
        rows = part_rows(j, i)
        return d, remote(done.at[j, m, rows], fin.at[d, m, rows], z_s.at[j, m, i], z_r.at[d, m, i], on_z(d))

    def send_over_z(j, m, i):
        d, copy = z_copy(j, m, i)

        @pl.when(d != 0)
        def _():
            copy.start()

        @pl.when(d == 0)
        def _():
            if (j, m) in over_z_first:
                zin[0] = share[j, 0]
            else:
                fin[0, m, part_rows(j, i), :] = done[j, m, part_rows(j, i), :]

    def place_product(j, m, target_k, product, rows, sent):
        @pl.when(target_k == k)
        def _():
            keep[j, m, rows, :] = product

        @pl.when(target_k != k)
        def _():
            away[j, m, rows, :] = product.astype(jnp.bfloat16)
            for i in sent:
                core_copies[j, m, i].start()

    def half_tile(j, g):
        target_k = x // 2 if g == 0 else 1 - x // 2
        rows = lanes(target_k, half)
        lhs = ftx[rows, inner] if j == 0 else ft[j - 1, rows, :]
        for m, rhs in enumerate((aown, fown)):
            product = jnp.dot(lhs, rhs[...], preferred_element_type=jnp.float32)

            place_product(j, m, target_k, product, pl.ds(0, half), parts(j))

    def late_quarter(i):
        lhs = ft[2, late_rows(i), :]
        for m, rhs in enumerate((aown, fown)):
            product = jnp.dot(lhs, rhs[...], preferred_element_type=jnp.float32)
            place_product(3, m, 1 - x // 2, product, part_rows(3, i), [i])

    def tile(j):
        half_tile(j, 0)
        half_tile(j, 1)

    def over_core(j, i=0):
        rows = part_rows(j, i)
        for m in range(2):
            core_copies[j, m, i].wait_recv()
            share[j, m, rows, :] = (keep[j, m, rows, :] + core_in[j, m, rows, :].astype(jnp.float32)).astype(jnp.bfloat16)
            if (j, m) in over_z_first:
                send_over_z(j, m, i)
            else:
                for copy in x_copies[j, m, i]:
                    copy.start()

    def add_up(first, rest):
        total = first.astype(jnp.float32)
        for term in rest:
            total = total + term.astype(jnp.float32)
        return total

    def over_x(j, i=0):
        rows = part_rows(j, i)
        for m in range(2):
            if (j, m) in over_z_first:
                continue
            for copy in x_copies[j, m, i]:
                copy.wait_recv()
            total = add_up(share[j, m, rows, lanes(x, width)], [x_in[j, n, m, rows, :] for n in range(3)])
            done[j, m, rows, :] = total.astype(jnp.bfloat16)
            send_over_z(j, m, i)

    tile(0)
    tile(1)
    over_core(0)
    tile(2)
    over_core(1)
    over_x(0)
    over_core(2)
    fwd_up.wait_recv()
    fwd_dn.wait_recv()
    half_tile(3, 0)

    @pl.when(x // 2 == k)
    def _():
        over_core(3, 0)
        over_core(3, 1)

    over_x(1)
    for i in range(2):
        for copy in late[i]:
            copy.wait_recv()
        late_quarter(i)

        @pl.when(x // 2 != k)
        def _():
            over_core(3, i)

    over_x(2)

    @pl.when(jnp.logical_not(far))
    def _():
        for d in (1, 2, 3):
            remote(share.at[0, 0], zin.at[d], zk_s.at[0], zk_r.at[d], on_z(d)).wait_recv()
        ksum[...] = add_up(zin[0], [zin[d] for d in (1, 2, 3)]).astype(jnp.bfloat16)
        for copy in kx_copies:
            copy.start()

    over_x(3, 0)
    over_x(3, 1)

    def owned(m):
        @pl.when(owner == 2)
        def _():
            for d in (1, 2, 3):
                for i in range(2):
                    rows = part_rows(3, i)
                    remote(done.at[3, m, rows], fin.at[d, m, rows], z_s.at[3, m, i], z_r.at[d, m, i], on_z(d)).wait_recv()

        @pl.when(owner != 2)
        def _():
            for d in (1, 2, 3):
                remote(done.at[0, m], fin.at[d, m], z_s.at[0, m, 0], z_r.at[d, m, 0], on_z(d)).wait_recv()

        return add_up(fin[0, m], [fin[d, m] for d in (1, 2, 3)])

    @pl.when(jnp.logical_not(far))
    def _():
        for copy in kx_copies:
            copy.wait_recv()
        sums[0] = add_up(ksum[:, lanes(x, width)], [kx_in[i] for i in range(3)])

    @pl.when(far)
    def _():
        sums[0] = owned(0)

    sums[1] = owned(1)

    for h in range(2):
        for copy in (*stage1[h], *(c for copies in stage2[h] for c in copies)):
            copy.wait_send()
        for p in range(out):
            tile_up(p + pairs - out, h).wait_send()
        for p in range(out - 1):
            tile_down(p, h).wait_send()
    for p in range(out):
        vector_up(p + pairs - out).wait_send()
        vector_down(p).wait_send()
    for copy in (*v_copies, *f_copies.values(), *lo_copies.values(), *hi_copies.values(), *own_up,
                 *own_dn, fwd_up, fwd_dn, *late[0], *late[1], *core_copies.values(),
                 *(c for cs in x_copies.values() for c in cs)):
        copy.wait_send()
    for j in range(4):
        for m, i in [(m, i) for m in range(2) for i in parts(j)]:
            d, copy = z_copy(j, m, i)

            @pl.when(d != 0)
            def _():
                copy.wait_send()

    @pl.when(jnp.logical_not(far))
    def _():
        for copy in kx_copies:
            copy.wait_send()


def body(vectors, block_count, block_cols, blocks):
    n_row = lax.axis_size("row")
    n_col = lax.axis_size("col")
    edge, columns = vectors.shape
    local_blocks, slots, blk, _ = blocks.shape
    width = columns // n_col
    scale = 1.0 / math.sqrt(edge * n_row * n_col)
    wide, half, part = 4 * width, 2 * width, 4 * edge
    reach = n_col + 2 * REACH_IN
    anywhere = pl.BlockSpec(memory_space=pl.ANY)
    vmem = pl.BlockSpec(memory_space=pltpu.VMEM)
    bf16 = jnp.bfloat16
    dma = pltpu.SemaphoreType.DMA
    sums = pl.pallas_call(
        functools.partial(kernel, n_row, local_blocks * n_row * n_col),
        out_shape=jax.ShapeDtypeStruct((2, half, width), jnp.float32),
        in_specs=[anywhere] * 4,
        out_specs=vmem,
        scratch_shapes=[
            pltpu.SMEM(block_cols.shape, jnp.int32),
            pltpu.SMEM(block_count.shape, jnp.int32),
            pltpu.VMEM(blocks.shape, bf16),
            pltpu.VMEM((reach - 1, 2, 3, blk, blk), bf16),
            pltpu.VMEM((reach, 6 * blk, edge), bf16),
            pltpu.VMEM((reach, edge, width), bf16),
            pltpu.VMEM((width, reach * edge), bf16),
            pltpu.VMEM((width, reach * edge), bf16),
            pltpu.VMEM((wide, part + 2 * edge), bf16),
            pltpu.VMEM((3, wide, part), bf16),
            pltpu.VMEM((part, wide), bf16),
            pltpu.VMEM((part, wide), bf16),
            pltpu.VMEM((4, 2, half, wide), bf16),
            pltpu.VMEM((4, 2, half, wide), jnp.float32),
            pltpu.VMEM((4, 2, half, wide), bf16),
            pltpu.VMEM((4, 2, half, wide), bf16),
            pltpu.VMEM((4, 3, 2, half, width), bf16),
            pltpu.VMEM((4, 2, half, width), bf16),
            pltpu.VMEM((4, 2, half, width), bf16),
            pltpu.VMEM((4, half, wide), bf16),
            pltpu.VMEM((half, wide), bf16),
            pltpu.VMEM((3, half, width), bf16),
            dma((4,)),
            dma((16,)), dma((16,)), dma((2, REACH_IN)), dma((2, REACH_IN)),
            dma((2, 3)), dma((2, 3)), dma((2, 4, 3)), dma((2, 4, 3)),
            dma((REACH_IN, 2)), dma((REACH_IN, 2)), dma((REACH_IN - 1, 2)), dma((REACH_IN - 1, 2)),
            dma((3,)), dma((3,)), dma((3,)), dma((3,)), dma((3,)), dma((3,)),
            dma((7,)), dma((7,)), dma((7,)), dma((7,)),
            dma((4, 2, 2)), dma((4, 2, 2)), dma((4, 2, 2, 3)), dma((4, 2, 2, 3)), dma((4, 2, 2)), dma((4, 2, 2)),
            dma((2,)), dma((4,)), dma((3,)), dma((3,)),
        ],
        compiler_params=pltpu.CompilerParams(
            collective_id=0, has_side_effects=True, vmem_limit_bytes=58 * 1024 * 1024
        ),
    )(block_cols, block_count, blocks, vectors)
    return (sums[0] * scale, sums[1] * scale)


def solution(mesh):
    in_specs = (
        P(("row", "col"), None),
        P(("row", "col")),
        P(("row", "col"), None),
        P(("row", "col"), None, None, None),
    )
    out_specs = (P("row", "col"), P("row", "col"))
    return jax.shard_map(body, mesh=mesh, in_specs=in_specs, out_specs=out_specs, check_vma=False)
```

```python
import functools
import math

import jax
import jax.numpy as jnp
from jax import lax
from jax.experimental import pallas as pl
from jax.experimental.pallas import tpu as pltpu
from jax.sharding import PartitionSpec as P

DEGREE = 8
REACH_IN = DEGREE
MESH = pl.DeviceIdType.MESH

filter_center = 0.25
filter_half = 1.75


def kernel(n_row, total_blocks, cols_hbm, count_hbm, blocks_hbm, v_ref, sums,
           cols_ref, count_ref, blocks_ref, hg, band, vland, ext0, ext1, ftx, ft, aown, fown,
           away, keep, core_in, share, x_in, done, fin, zin, ksum, kx_in, fedge,
           in_sem, v_s, v_r, vh_s, vh_r, h1_s, h1_r, h2_s, h2_r, eu_s, eu_r, ed_s, ed_r,
           fx_s, fx_r, lo_s, lo_r, hi_s, hi_r, up_s, up_r, dn_s, dn_r, core_s, core_r, x_s, x_r, z_s, z_r,
           zk_s, zk_r, kx_s, kx_r, fe_s, fe_r):
    edge = v_ref.shape[0]
    blk = edge // 2
    pairs = 16
    out = REACH_IN
    row, col = lax.axis_index("row"), lax.axis_index("col")
    z, k, y, x = row // 2, row % 2, col // 4, col % 4
    up, down = {"row": (row + 1) % n_row}, {"row": (row + n_row - 1) % n_row}
    partner = {"row": z * 2 + 1 - k}
    across = {"row": (row + n_row - 1 + 2 * k) % n_row}

    def place(dy, dx):
        return ((y + dy) % 4) * 4 + (x + dx) % 4

    def on_x(d):
        return {"col": place(0, d)}

    def on_y(d):
        return {"col": place(d, 0)}

    def on_z(d):
        return {"row": ((z + d) % 4) * 2 + k}

    def remote(src, dst, send, recv, device):
        return pltpu.make_async_remote_copy(
            src_ref=src, dst_ref=dst, send_sem=send, recv_sem=recv, device_id=device, device_id_type=MESH
        )

    def lanes(i, size, count=1):
        return pl.ds(pl.multiple_of(i * size, size), count * size)

    others = [(dy, dx) for dy in range(4) for dx in range(4) if dy or dx]
    barrier = pltpu.get_barrier_semaphore()
    for device in [partner, across, on_z(1), on_z(2), on_z(3)] + [{"col": place(dy, dx)} for dy, dx in others]:
        pl.semaphore_signal(barrier, inc=1, device_id=device, device_id_type=MESH)

    fetch = [
        pltpu.make_async_copy(cols_hbm, cols_ref, in_sem.at[0]),
        pltpu.make_async_copy(count_hbm, count_ref, in_sem.at[1]),
        pltpu.make_async_copy(blocks_hbm, blocks_ref, in_sem.at[2]),
        pltpu.make_async_copy(v_ref.at[:, lanes(col, blk)], vland.at[col + out], in_sem.at[3]),
    ]
    for copy in fetch:
        copy.start()
    for copy in fetch[:3]:
        copy.wait()

    first = (row * pairs + col) * 2
    for i in range(2):
        for offset in range(3):
            tile = jnp.zeros((blk, blk), jnp.bfloat16)
            for slot in range(5):
                relative = lax.rem(cols_ref[i, slot] - first - i + total_blocks, total_blocks)
                hit = jnp.logical_and(relative == offset, slot < count_ref[i])
                tile = jnp.where(hit, blocks_ref[i, slot], tile)
            hg[col + out, i, offset] = tile

    pl.semaphore_wait(barrier, 20)

    def where(h, a, b):
        return place(b, a) if h == 0 else place(a, b)

    def tile_copy(h, a, b, to_a, to_b, send, recv):
        unit = hg.at[where(h, a, b) + out, h]
        return remote(unit, unit, send, recv, {"col": where(h, to_a, to_b)})

    stage1, stage2 = [], []
    for h in range(2):
        sign = 1 if h == 0 else 3
        moves = [(0, 1), (0, 3), (4 - sign, sign)]
        stage1.append([tile_copy(h, a, 0, to, 0, h1_s.at[h, n], h1_r.at[h, n]) for n, (a, to) in enumerate(moves)])
        lists = []
        for a in range(4):
            sign = 1 if a < 2 else 3
            moves = [(0, 1), (0, 3), (4 - sign, sign)]
            lists.append([
                tile_copy(h, a, b, 0, to, h2_s.at[h, a, n], h2_r.at[h, a, n]) for n, (b, to) in enumerate(moves)
            ])
        stage2.append(lists)

    v_copies = [
        remote(v_ref.at[:, lanes(place(dy, dx), blk)], vland.at[col + out], v_s.at[dy * 4 + dx],
               v_r.at[dy * 4 + dx], {"col": place(dy, dx)})
        for dy, dx in others
    ]

    def tile_up(p, h):
        return remote(hg.at[p + out, h], hg.at[p + out - pairs, h], eu_s.at[p + out - pairs, h],
                      eu_r.at[p + out - pairs, h], up)

    def tile_down(p, h):
        return remote(hg.at[p + out, h], hg.at[p + out + pairs, h], ed_s.at[p, h], ed_r.at[p, h], down)

    def pass_on(h, a, b):
        p = where(h, a, b)

        @pl.when(p >= pairs - out)
        def _():
            tile_up(p, h).start()

        @pl.when(p < out - 1)
        def _():
            tile_down(p, h).start()

    def vector_up(p):
        return remote(vland.at[p + out], vland.at[p + out - pairs], vh_s.at[0, p + out - pairs],
                      vh_r.at[0, p + out - pairs], up)

    def vector_down(p):
        return remote(vland.at[p + out], vland.at[p + out + pairs], vh_s.at[1, p], vh_r.at[1, p], down)

    def pass_vector(dy, dx):
        if dy or dx:
            v_copies[others.index((dy, dx))].wait_recv()
        else:
            fetch[3].wait()
        p = place(4 - dy, 4 - dx)

        @pl.when(p >= pairs - out)
        def _():
            vector_up(p).start()

        @pl.when(p < out)
        def _():
            vector_down(p).start()

    def scatter(slot, h):
        def put(s, r, c, value):
            band[s, pl.ds(r * blk, blk), pl.ds(c * blk, blk)] = value

        put(slot, 2 + h, h, hg[slot, h, 0])
        put(slot, 3 + h, h, hg[slot, h, 1].T)
        put(slot, 4 + h, h, hg[slot, h, 2].T)
        put(slot, 5 - 5 * h, h, jnp.zeros((blk, blk), jnp.bfloat16))
        if h == 0:
            put(slot, 2, 1, hg[slot, 0, 1])
            put(slot + 1, 0, 0, hg[slot, 0, 2])
        else:
            put(slot + 1, 1, 0, hg[slot, 1, 1])
            put(slot + 1, 1, 1, hg[slot, 1, 2])

    def scatter_unit(h, a, b):
        scatter(where(h, a, b) + out, h)

    def start_first():
        for h in range(2):
            stage1[h][0].start()
            stage1[h][1].start()

    def start_own():
        for h in range(2):
            stage2[h][0][0].start()
            stage2[h][0][1].start()

    def start_vectors(moves):
        for move in moves:
            v_copies[others.index(move)].start()

    def pass_vectors(moves):
        for dy, dx in moves:
            pass_vector(dy, dx)

    def pass_own():
        for h in range(2):
            pass_on(h, 0, 0)
            scatter_unit(h, 0, 0)

    def take_first():
        for h in range(2):
            for n, a in ((0, 3), (1, 1)):
                stage1[h][n].wait_recv()
                if n == h:
                    stage1[h][2].start()
                stage2[h][a][0].start()
                stage2[h][a][1].start()
                pass_on(h, a, 0)
        for h in range(2):
            scatter_unit(h, 3, 0)
            scatter_unit(h, 1, 0)

    def take_far():
        for h in range(2):
            stage1[h][2].wait_recv()
            stage2[h][2][0].start()
            stage2[h][2][1].start()
            pass_on(h, 2, 0)
        for h in range(2):
            scatter_unit(h, 2, 0)

    def receive(a):
        for h in range(2):
            for n, b in ((0, 3), (1, 1)):
                stage2[h][a][n].wait_recv()
                if n == (0 if a < 2 else 1):
                    stage2[h][a][2].start()
                pass_on(h, a, b)
        for h in range(2):
            scatter_unit(h, a, 3)
            scatter_unit(h, a, 1)

    def receive_far(a):
        for h in range(2):
            stage2[h][a][2].wait_recv()
            pass_on(h, a, 2)
        for h in range(2):
            scatter_unit(h, a, 2)

    def turn(slot):
        ext0[:, lanes(slot, edge)] = vland[slot].T

    near = [(0, 1), (0, 3), (1, 0), (3, 0)]
    middle = [(1, 1), (1, 3), (3, 1), (3, 3), (0, 2), (2, 0)]
    distant = [(1, 2), (3, 2), (2, 1), (2, 3), (2, 2)]

    start_first()
    start_own()
    start_vectors(near)
    pass_own()
    take_first()
    pass_vectors([(0, 0)] + near)
    start_vectors(middle)
    take_far()
    receive(0)
    pass_vectors(middle)
    start_vectors(distant)
    receive(3)
    receive_far(0)
    receive(1)
    receive_far(3)
    pass_vectors(distant)
    receive(2)
    receive_far(1)
    receive_far(2)

    def turn_all(low, high):
        def one(slot, carry):
            turn(slot)
            return carry

        lax.fori_loop(low, high, one, 0)

    turn_all(out, out + pairs)

    def update(step, j):
        source, target = (ext0, ext1) if step % 2 else (ext1, ext0)
        own = lanes(j + out, edge)
        product = jnp.dot(source[:, lanes(j + out - 1, edge, 3)], band[j + out], preferred_element_type=jnp.float32)
        shifted = product - filter_center * source[:, own].astype(jnp.float32)
        if step == 1:
            result = shifted / filter_half
        else:
            result = 2.0 * shifted / filter_half - target[:, own].astype(jnp.float32)
        target[:, own] = result.astype(jnp.bfloat16)

    for step in range(1, DEGREE):
        def inside(j, carry):
            update(step, j)
            return carry

        lax.fori_loop(step, pairs - step, inside, 0, unroll=pairs // 2 - step)

    for p in range(out):
        vector_up(p + pairs - out).wait_recv()
        turn(p)
        vector_down(p).wait_recv()
        turn(p + pairs + out)
    for p in range(out):
        for h in range(2):
            tile_up(p + pairs - out, h).wait_recv()
            scatter(p, h)
            if p < out - 1:
                tile_down(p, h).wait_recv()
                scatter(p + pairs + out, h)

    for step in range(1, DEGREE + 1):
        def outside(i, carry):
            update(step, step - out + i)
            update(step, pairs - step + i)
            return carry

        lax.fori_loop(0, out, outside, 0, unroll=out)

    f_up = remote(ext0.at[:, lanes(pairs - 1 + out, edge)], fedge.at[0], fe_s.at[0], fe_r.at[0], up)
    f_down = remote(ext0.at[:, lanes(out, edge)], fedge.at[1], fe_s.at[1], fe_r.at[1], down)

    part = 4 * edge
    width = blk
    half = 2 * width

    def mate(e):
        return (x, x + 1 - 2 * (x % 2), (x + 2) % 4, 3 - x)[e]

    def x_copy(e, first_pair, count, offset, sems):
        pair = 4 * mate(e) + first_pair + out
        return remote(ext0.at[:, lanes(pair, edge, count)], ftx.at[lanes(x, width), pl.ds(offset, count * edge)],
                      sems[0].at[e - 1], sems[1].at[e - 1], {"col": y * 4 + mate(e)})

    f_copies = {
        (e, b): x_copy(e, 2 * b, 2, edge + 2 * b * edge, (fx_s.at[b], fx_r.at[b])) for e in (1, 2, 3) for b in range(2)
    }
    lo_copies = {e: x_copy(e, -1, 1, 0, (lo_s, lo_r)) for e in (1, 2, 3)}
    hi_copies = {e: x_copy(e, 4, 1, 5 * edge, (hi_s, hi_r)) for e in (1, 2, 3)}
    inner = pl.ds(edge, part)

    def y_copy(from_slot, to_slot, e, b, count, index, is_up):
        piece = lanes(mate(e), width)
        sems = (up_s, up_r) if is_up else (dn_s, dn_r)
        depth = 2 * b * edge, 2 * count * edge
        if from_slot == 0:
            src = ftx.at[piece, pl.ds(edge + depth[0], depth[1])]
        else:
            src = ft.at[from_slot - 1, piece, pl.ds(*depth)]
        return remote(src, ft.at[to_slot - 1, piece, pl.ds(*depth)], sems[0].at[index], sems[1].at[index],
                      on_y(1 if is_up else 3))

    own_up = {(e, b): y_copy(0, 1, e, b, 1, 2 * e + b, True) for e in range(4) for b in range(2)}
    own_dn = {(e, b): y_copy(0, 2, e, b, 1, 2 * e + b, False) for e in range(4) for b in range(2)}
    fwd_up, fwd_dn = y_copy(1, 3, 0, 0, 2, 8, True), y_copy(2, 3, 1, 0, 2, 8, False)

    def late_rows(i):
        return lanes(2 * (1 - x // 2) + i, width)

    def late_copy(i, is_up):
        sems = (up_s, up_r) if is_up else (dn_s, dn_r)
        depth = pl.ds(0 if is_up else part // 2, part // 2)
        return remote(ft.at[0 if is_up else 1, late_rows(i), depth], ft.at[2, late_rows(i), depth],
                      sems[0].at[9 + i], sems[1].at[9 + i], on_y(1 if is_up else 3))

    late = [[late_copy(i, is_up) for is_up in (True, False)] for i in range(2)]

    def spread(e, b):
        own_up[e, b].start()
        own_dn[e, b].start()

    order = [(1, 0), (3, 0), (1, 1), (3, 1), (2, 0), (2, 1)]
    for key in order:
        f_copies[key].start()
    ftx[lanes(x, width), inner] = ext0[:, lanes(4 * x + out, edge, 4)]
    spread(0, 0)
    spread(0, 1)
    f_up.start()
    f_down.start()
    for key in order:
        f_copies[key].wait_recv()
        spread(*key)
    f_up.wait()
    f_down.wait()
    ext0[:, lanes(out - 1, edge)] = fedge[0]
    ext0[:, lanes(pairs + out, edge)] = fedge[1]
    for e in (1, 3, 2):
        lo_copies[e].start()
        hi_copies[e].start()
    ftx[lanes(x, width), pl.ds(0, edge)] = ext0[:, lanes(4 * x - 1 + out, edge)]
    ftx[lanes(x, width), pl.ds(5 * edge, edge)] = ext0[:, lanes(4 * x + 4 + out, edge)]

    def apply(q):
        rows = pl.ds(q * edge, edge)
        applied = jnp.dot(ftx[:, pl.ds(q * edge, 3 * edge)], band[4 * x + q + out], preferred_element_type=jnp.float32)
        aown[rows, :] = applied.astype(jnp.bfloat16).T
        fown[rows, :] = ftx[:, pl.ds((q + 1) * edge, edge)].T

    for e in (0, 1, 3):
        for b in range(2):
            own_up[e, b].wait_recv()
            own_dn[e, b].wait_recv()
    fwd_up.start()
    fwd_dn.start()
    apply(1)
    apply(2)
    for b in range(2):
        own_up[2, b].wait_recv()
        own_dn[2, b].wait_recv()
    for i in range(2):
        for copy in late[i]:
            copy.start()
    for e in (1, 3, 2):
        lo_copies[e].wait_recv()
        hi_copies[e].wait_recv()
    apply(0)
    apply(3)

    def parts(j):
        return range(2 if j == 3 else 1)

    def part_rows(j, i):
        return pl.ds(i * width, width) if j == 3 else pl.ds(0, half)

    core_copies = {
        (j, m, i): remote(away.at[j, m, part_rows(j, i)], core_in.at[j, m, part_rows(j, i)], core_s.at[j, m, i],
                          core_r.at[j, m, i], partner)
        for j in range(4) for m in range(2) for i in parts(j)
    }
    owner = (y - z + 4) % 4
    far = owner >= 2

    over_z_first = [(0, 0), (1, 0)]
    x_copies = {
        (j, m, i): [
            remote(share.at[j, m, part_rows(j, i), lanes((x + d) % 4, width)], x_in.at[j, d - 1, m, part_rows(j, i)],
                   x_s.at[j, m, i, d - 1], x_r.at[j, m, i, d - 1], on_x(d))
            for d in (1, 2, 3)
        ]
        for j in range(4) for m in range(2) for i in parts(j) if (j, m) not in over_z_first
    }
    kx_copies = [
        remote(ksum.at[:, lanes((x + d) % 4, width)], kx_in.at[d - 1], kx_s.at[d - 1], kx_r.at[d - 1], on_x(d))
        for d in (1, 2, 3)
    ]

    def to_owner(j):
        return (y + (0, 3, 1, 2)[j] - z + 4) % 4

    def z_copy(j, m, i):
        d = to_owner(j)
        if (j, m) in over_z_first:
            return d, remote(share.at[j, 0], zin.at[d], zk_s.at[j], zk_r.at[d], on_z(d))
        rows = part_rows(j, i)
        return d, remote(done.at[j, m, rows], fin.at[d, m, rows], z_s.at[j, m, i], z_r.at[d, m, i], on_z(d))

    def send_over_z(j, m, i):
        d, copy = z_copy(j, m, i)

        @pl.when(d != 0)
        def _():
            copy.start()

        @pl.when(d == 0)
        def _():
            if (j, m) in over_z_first:
                zin[0] = share[j, 0]
            else:
                fin[0, m, part_rows(j, i), :] = done[j, m, part_rows(j, i), :]

    def place_product(j, m, target_k, product, rows, sent):
        @pl.when(target_k == k)
        def _():
            keep[j, m, rows, :] = product

        @pl.when(target_k != k)
        def _():
            away[j, m, rows, :] = product.astype(jnp.bfloat16)
            for i in sent:
                core_copies[j, m, i].start()

    def half_tile(j, g):
        target_k = x // 2 if g == 0 else 1 - x // 2
        rows = lanes(target_k, half)
        lhs = ftx[rows, inner] if j == 0 else ft[j - 1, rows, :]
        for m, rhs in enumerate((aown, fown)):
            product = jnp.dot(lhs, rhs[...], preferred_element_type=jnp.float32)

            place_product(j, m, target_k, product, pl.ds(0, half), parts(j))

    def late_quarter(i):
        lhs = ft[2, late_rows(i), :]
        for m, rhs in enumerate((aown, fown)):
            product = jnp.dot(lhs, rhs[...], preferred_element_type=jnp.float32)
            place_product(3, m, 1 - x // 2, product, part_rows(3, i), [i])

    def tile(j):
        half_tile(j, 0)
        half_tile(j, 1)

    def over_core(j, i=0):
        rows = part_rows(j, i)
        for m in range(2):
            core_copies[j, m, i].wait_recv()
            share[j, m, rows, :] = (keep[j, m, rows, :] + core_in[j, m, rows, :].astype(jnp.float32)).astype(jnp.bfloat16)
            if (j, m) in over_z_first:
                send_over_z(j, m, i)
            else:
                for copy in x_copies[j, m, i]:
                    copy.start()

    def add_up(first, rest):
        total = first.astype(jnp.float32)
        for term in rest:
            total = total + term.astype(jnp.float32)
        return total

    def over_x(j, i=0):
        rows = part_rows(j, i)
        for m in range(2):
            if (j, m) in over_z_first:
                continue
            for copy in x_copies[j, m, i]:
                copy.wait_recv()
            total = add_up(share[j, m, rows, lanes(x, width)], [x_in[j, n, m, rows, :] for n in range(3)])
            done[j, m, rows, :] = total.astype(jnp.bfloat16)
            send_over_z(j, m, i)

    tile(0)
    tile(1)
    over_core(0)
    tile(2)
    over_core(1)
    over_x(0)
    over_core(2)
    fwd_up.wait_recv()
    fwd_dn.wait_recv()
    half_tile(3, 0)

    @pl.when(x // 2 == k)
    def _():
        over_core(3, 0)
        over_core(3, 1)

    over_x(1)
    for i in range(2):
        for copy in late[i]:
            copy.wait_recv()
        late_quarter(i)

        @pl.when(x // 2 != k)
        def _():
            over_core(3, i)

    over_x(2)

    @pl.when(jnp.logical_not(far))
    def _():
        for d in (1, 2, 3):
            remote(share.at[0, 0], zin.at[d], zk_s.at[0], zk_r.at[d], on_z(d)).wait_recv()
        ksum[...] = add_up(zin[0], [zin[d] for d in (1, 2, 3)]).astype(jnp.bfloat16)
        for copy in kx_copies:
            copy.start()

    over_x(3, 0)
    over_x(3, 1)

    def owned(m):
        @pl.when(owner == 2)
        def _():
            for d in (1, 2, 3):
                for i in range(2):
                    rows = part_rows(3, i)
                    remote(done.at[3, m, rows], fin.at[d, m, rows], z_s.at[3, m, i], z_r.at[d, m, i], on_z(d)).wait_recv()

        @pl.when(owner != 2)
        def _():
            for d in (1, 2, 3):
                remote(done.at[0, m], fin.at[d, m], z_s.at[0, m, 0], z_r.at[d, m, 0], on_z(d)).wait_recv()

        return add_up(fin[0, m], [fin[d, m] for d in (1, 2, 3)])

    @pl.when(jnp.logical_not(far))
    def _():
        for copy in kx_copies:
            copy.wait_recv()
        sums[0] = add_up(ksum[:, lanes(x, width)], [kx_in[i] for i in range(3)])

    @pl.when(far)
    def _():
        sums[0] = owned(0)

    sums[1] = owned(1)

    for h in range(2):
        for copy in (*stage1[h], *(c for copies in stage2[h] for c in copies)):
            copy.wait_send()
        for p in range(out):
            tile_up(p + pairs - out, h).wait_send()
        for p in range(out - 1):
            tile_down(p, h).wait_send()
    for p in range(out):
        vector_up(p + pairs - out).wait_send()
        vector_down(p).wait_send()
    for copy in (*v_copies, *f_copies.values(), *lo_copies.values(), *hi_copies.values(), *own_up.values(),
                 *own_dn.values(), fwd_up, fwd_dn, *late[0], *late[1], *core_copies.values(),
                 *(c for cs in x_copies.values() for c in cs)):
        copy.wait_send()
    for j in range(4):
        for m, i in [(m, i) for m in range(2) for i in parts(j)]:
            d, copy = z_copy(j, m, i)

            @pl.when(d != 0)
            def _():
                copy.wait_send()

    @pl.when(jnp.logical_not(far))
    def _():
        for copy in kx_copies:
            copy.wait_send()


def body(vectors, block_count, block_cols, blocks):
    n_row = lax.axis_size("row")
    n_col = lax.axis_size("col")
    edge, columns = vectors.shape
    local_blocks, slots, blk, _ = blocks.shape
    width = columns // n_col
    scale = 1.0 / math.sqrt(edge * n_row * n_col)
    wide, half, part = 4 * width, 2 * width, 4 * edge
    reach = n_col + 2 * REACH_IN
    anywhere = pl.BlockSpec(memory_space=pl.ANY)
    vmem = pl.BlockSpec(memory_space=pltpu.VMEM)
    bf16 = jnp.bfloat16
    dma = pltpu.SemaphoreType.DMA
    sums = pl.pallas_call(
        functools.partial(kernel, n_row, local_blocks * n_row * n_col),
        out_shape=jax.ShapeDtypeStruct((2, half, width), jnp.float32),
        in_specs=[anywhere] * 4,
        out_specs=vmem,
        scratch_shapes=[
            pltpu.SMEM(block_cols.shape, jnp.int32),
            pltpu.SMEM(block_count.shape, jnp.int32),
            pltpu.VMEM(blocks.shape, bf16),
            pltpu.VMEM((reach - 1, 2, 3, blk, blk), bf16),
            pltpu.VMEM((reach, 6 * blk, edge), bf16),
            pltpu.VMEM((reach, edge, width), bf16),
            pltpu.VMEM((width, reach * edge), bf16),
            pltpu.VMEM((width, reach * edge), bf16),
            pltpu.VMEM((wide, part + 2 * edge), bf16),
            pltpu.VMEM((3, wide, part), bf16),
            pltpu.VMEM((part, wide), bf16),
            pltpu.VMEM((part, wide), bf16),
            pltpu.VMEM((4, 2, half, wide), bf16),
            pltpu.VMEM((4, 2, half, wide), jnp.float32),
            pltpu.VMEM((4, 2, half, wide), bf16),
            pltpu.VMEM((4, 2, half, wide), bf16),
            pltpu.VMEM((4, 3, 2, half, width), bf16),
            pltpu.VMEM((4, 2, half, width), bf16),
            pltpu.VMEM((4, 2, half, width), bf16),
            pltpu.VMEM((4, half, wide), bf16),
            pltpu.VMEM((half, wide), bf16),
            pltpu.VMEM((3, half, width), bf16),
            pltpu.VMEM((2, width, edge), bf16),
            dma((4,)),
            dma((16,)), dma((16,)), dma((2, REACH_IN)), dma((2, REACH_IN)),
            dma((2, 3)), dma((2, 3)), dma((2, 4, 3)), dma((2, 4, 3)),
            dma((REACH_IN, 2)), dma((REACH_IN, 2)), dma((REACH_IN - 1, 2)), dma((REACH_IN - 1, 2)),
            dma((2, 3)), dma((2, 3)), dma((3,)), dma((3,)), dma((3,)), dma((3,)),
            dma((11,)), dma((11,)), dma((11,)), dma((11,)),
            dma((4, 2, 2)), dma((4, 2, 2)), dma((4, 2, 2, 3)), dma((4, 2, 2, 3)), dma((4, 2, 2)), dma((4, 2, 2)),
            dma((2,)), dma((4,)), dma((3,)), dma((3,)), dma((2,)), dma((2,)),
        ],
        compiler_params=pltpu.CompilerParams(
            collective_id=0, has_side_effects=True, vmem_limit_bytes=58 * 1024 * 1024
        ),
    )(block_cols, block_count, blocks, vectors)
    return (sums[0] * scale, sums[1] * scale)


def solution(mesh):
    in_specs = (
        P(("row", "col"), None),
        P(("row", "col")),
        P(("row", "col"), None),
        P(("row", "col"), None, None, None),
    )
    out_specs = (P("row", "col"), P("row", "col"))
    return jax.shard_map(body, mesh=mesh, in_specs=in_specs, out_specs=out_specs, check_vma=False)
```

```python
import functools
import math

import jax
import jax.numpy as jnp
from jax import lax
from jax.experimental import pallas as pl
from jax.experimental.pallas import tpu as pltpu
from jax.sharding import PartitionSpec as P

DEGREE = 8
REACH_IN = DEGREE
MESH = pl.DeviceIdType.MESH

filter_center = 0.25
filter_half = 1.75


def kernel(n_row, total_blocks, cols_hbm, count_hbm, blocks_hbm, v_ref, sums,
           cols_ref, count_ref, blocks_ref, hg, band, vland, ext0, ext1, ftx, ft, aown, fown,
           away, keep, core_in, share, x_in, done, fin, zin, ksum, kx_in, fedge,
           in_sem, v_s, v_r, vh_s, vh_r, h1_s, h1_r, h2_s, h2_r, eu_s, eu_r, ed_s, ed_r,
           fx_s, fx_r, lo_s, lo_r, hi_s, hi_r, up_s, up_r, dn_s, dn_r, core_s, core_r, x_s, x_r, z_s, z_r,
           zk_s, zk_r, kx_s, kx_r, fe_s, fe_r):
    edge = v_ref.shape[0]
    blk = edge // 2
    pairs = 16
    out = REACH_IN
    row, col = lax.axis_index("row"), lax.axis_index("col")
    z, k, y, x = row // 2, row % 2, col // 4, col % 4
    up, down = {"row": (row + 1) % n_row}, {"row": (row + n_row - 1) % n_row}
    partner = {"row": z * 2 + 1 - k}
    across = {"row": (row + n_row - 1 + 2 * k) % n_row}

    def place(dy, dx):
        return ((y + dy) % 4) * 4 + (x + dx) % 4

    def on_x(d):
        return {"col": place(0, d)}

    def on_y(d):
        return {"col": place(d, 0)}

    def on_z(d):
        return {"row": ((z + d) % 4) * 2 + k}

    def remote(src, dst, send, recv, device):
        return pltpu.make_async_remote_copy(
            src_ref=src, dst_ref=dst, send_sem=send, recv_sem=recv, device_id=device, device_id_type=MESH
        )

    def lanes(i, size, count=1):
        return pl.ds(pl.multiple_of(i * size, size), count * size)

    others = [(dy, dx) for dy in range(4) for dx in range(4) if dy or dx]
    barrier = pltpu.get_barrier_semaphore()
    for device in [partner, across, on_z(1), on_z(2), on_z(3)] + [{"col": place(dy, dx)} for dy, dx in others]:
        pl.semaphore_signal(barrier, inc=1, device_id=device, device_id_type=MESH)

    fetch = [
        pltpu.make_async_copy(cols_hbm, cols_ref, in_sem.at[0]),
        pltpu.make_async_copy(count_hbm, count_ref, in_sem.at[1]),
        pltpu.make_async_copy(blocks_hbm, blocks_ref, in_sem.at[2]),
        pltpu.make_async_copy(v_ref.at[:, lanes(col, blk)], vland.at[col + out], in_sem.at[3]),
    ]
    for copy in fetch:
        copy.start()
    for copy in fetch[:3]:
        copy.wait()

    first = (row * pairs + col) * 2
    for i in range(2):
        for offset in range(3):
            tile = jnp.zeros((blk, blk), jnp.bfloat16)
            for slot in range(5):
                relative = lax.rem(cols_ref[i, slot] - first - i + total_blocks, total_blocks)
                hit = jnp.logical_and(relative == offset, slot < count_ref[i])
                tile = jnp.where(hit, blocks_ref[i, slot], tile)
            hg[col + out, i, offset] = tile

    pl.semaphore_wait(barrier, 20)

    def where(h, a, b):
        return place(b, a) if h == 0 else place(a, b)

    def tile_copy(h, a, b, to_a, to_b, send, recv):
        unit = hg.at[where(h, a, b) + out, h]
        return remote(unit, unit, send, recv, {"col": where(h, to_a, to_b)})

    stage1, stage2 = [], []
    for h in range(2):
        sign = 1 if h == 0 else 3
        moves = [(0, 1), (0, 3), (4 - sign, sign)]
        stage1.append([tile_copy(h, a, 0, to, 0, h1_s.at[h, n], h1_r.at[h, n]) for n, (a, to) in enumerate(moves)])
        lists = []
        for a in range(4):
            sign = 1 if a < 2 else 3
            moves = [(0, 1), (0, 3), (4 - sign, sign)]
            lists.append([
                tile_copy(h, a, b, 0, to, h2_s.at[h, a, n], h2_r.at[h, a, n]) for n, (b, to) in enumerate(moves)
            ])
        stage2.append(lists)

    v_copies = [
        remote(v_ref.at[:, lanes(place(dy, dx), blk)], vland.at[col + out], v_s.at[dy * 4 + dx],
               v_r.at[dy * 4 + dx], {"col": place(dy, dx)})
        for dy, dx in others
    ]

    def tile_up(p, h):
        return remote(hg.at[p + out, h], hg.at[p + out - pairs, h], eu_s.at[p + out - pairs, h],
                      eu_r.at[p + out - pairs, h], up)

    def tile_down(p, h):
        return remote(hg.at[p + out, h], hg.at[p + out + pairs, h], ed_s.at[p, h], ed_r.at[p, h], down)

    def pass_on(h, a, b):
        p = where(h, a, b)

        @pl.when(p >= pairs - out)
        def _():
            tile_up(p, h).start()

        @pl.when(p < out - 1)
        def _():
            tile_down(p, h).start()

    def vector_up(p):
        return remote(vland.at[p + out], vland.at[p + out - pairs], vh_s.at[0, p + out - pairs],
                      vh_r.at[0, p + out - pairs], up)

    def vector_down(p):
        return remote(vland.at[p + out], vland.at[p + out + pairs], vh_s.at[1, p], vh_r.at[1, p], down)

    def pass_vector(dy, dx):
        if dy or dx:
            v_copies[others.index((dy, dx))].wait_recv()
        else:
            fetch[3].wait()
        p = place(4 - dy, 4 - dx)

        @pl.when(p >= pairs - out)
        def _():
            vector_up(p).start()

        @pl.when(p < out)
        def _():
            vector_down(p).start()

    def scatter(slot, h):
        def put(s, r, c, value):
            band[s, pl.ds(r * blk, blk), pl.ds(c * blk, blk)] = value

        put(slot, 2 + h, h, hg[slot, h, 0])
        put(slot, 3 + h, h, hg[slot, h, 1].T)
        put(slot, 4 + h, h, hg[slot, h, 2].T)
        put(slot, 5 - 5 * h, h, jnp.zeros((blk, blk), jnp.bfloat16))
        if h == 0:
            put(slot, 2, 1, hg[slot, 0, 1])
            put(slot + 1, 0, 0, hg[slot, 0, 2])
        else:
            put(slot + 1, 1, 0, hg[slot, 1, 1])
            put(slot + 1, 1, 1, hg[slot, 1, 2])

    def scatter_unit(h, a, b):
        scatter(where(h, a, b) + out, h)

    def start_first():
        for h in range(2):
            stage1[h][0].start()
            stage1[h][1].start()

    def start_own():
        for h in range(2):
            stage2[h][0][0].start()
            stage2[h][0][1].start()

    def start_vectors(moves):
        for move in moves:
            v_copies[others.index(move)].start()

    def pass_vectors(moves):
        for dy, dx in moves:
            pass_vector(dy, dx)

    def pass_own():
        for h in range(2):
            pass_on(h, 0, 0)
            scatter_unit(h, 0, 0)

    def take_first():
        for h in range(2):
            for n, a in ((0, 3), (1, 1)):
                stage1[h][n].wait_recv()
                if n == h:
                    stage1[h][2].start()
                stage2[h][a][0].start()
                stage2[h][a][1].start()
                pass_on(h, a, 0)
        for h in range(2):
            scatter_unit(h, 3, 0)
            scatter_unit(h, 1, 0)

    def take_far():
        for h in range(2):
            stage1[h][2].wait_recv()
            stage2[h][2][0].start()
            stage2[h][2][1].start()
            pass_on(h, 2, 0)
        for h in range(2):
            scatter_unit(h, 2, 0)

    def receive(a):
        for h in range(2):
            for n, b in ((0, 3), (1, 1)):
                stage2[h][a][n].wait_recv()
                if n == (0 if a < 2 else 1):
                    stage2[h][a][2].start()
                pass_on(h, a, b)
        for h in range(2):
            scatter_unit(h, a, 3)
            scatter_unit(h, a, 1)

    def receive_far(a):
        for h in range(2):
            stage2[h][a][2].wait_recv()
            pass_on(h, a, 2)
        for h in range(2):
            scatter_unit(h, a, 2)

    def turn(slot):
        ext0[:, lanes(slot, edge)] = vland[slot].T

    near = [(0, 1), (0, 3), (1, 0), (3, 0)]
    middle = [(1, 1), (1, 3), (3, 1), (3, 3), (0, 2), (2, 0)]
    distant = [(1, 2), (3, 2), (2, 1), (2, 3), (2, 2)]

    start_first()
    start_own()
    start_vectors(near)
    pass_own()
    take_first()
    pass_vectors([(0, 0)] + near)
    start_vectors(middle)
    take_far()
    receive(0)
    pass_vectors(middle)
    start_vectors(distant)
    receive(3)
    receive_far(0)
    receive(1)
    receive_far(3)
    pass_vectors(distant)
    receive(2)
    receive_far(1)
    receive_far(2)

    def turn_all(low, high):
        def one(slot, carry):
            turn(slot)
            return carry

        lax.fori_loop(low, high, one, 0)

    turn_all(out, out + pairs)

    def update(step, j):
        source, target = (ext0, ext1) if step % 2 else (ext1, ext0)
        own = lanes(j + out, edge)
        product = jnp.dot(source[:, lanes(j + out - 1, edge, 3)], band[j + out], preferred_element_type=jnp.float32)
        shifted = product - filter_center * source[:, own].astype(jnp.float32)
        if step == 1:
            result = shifted / filter_half
        else:
            result = 2.0 * shifted / filter_half - target[:, own].astype(jnp.float32)
        target[:, own] = result.astype(jnp.bfloat16)

    for step in range(1, DEGREE):
        def inside(j, carry):
            update(step, j)
            return carry

        lax.fori_loop(step, pairs - step, inside, 0, unroll=pairs // 2 - step)

    for p in range(out):
        vector_up(p + pairs - out).wait_recv()
        turn(p)
        vector_down(p).wait_recv()
        turn(p + pairs + out)
    for p in range(out):
        for h in range(2):
            tile_up(p + pairs - out, h).wait_recv()
            scatter(p, h)
            if p < out - 1:
                tile_down(p, h).wait_recv()
                scatter(p + pairs + out, h)

    for step in range(1, DEGREE + 1):
        def outside(i, carry):
            update(step, step - out + i)
            update(step, pairs - step + i)
            return carry

        lax.fori_loop(0, out, outside, 0, unroll=out)

    f_up = remote(ext0.at[:, lanes(pairs - 1 + out, edge)], fedge.at[0], fe_s.at[0], fe_r.at[0], up)
    f_down = remote(ext0.at[:, lanes(out, edge)], fedge.at[1], fe_s.at[1], fe_r.at[1], down)

    part = 4 * edge
    width = blk
    half = 2 * width

    def mate(e):
        return (x, x + 1 - 2 * (x % 2), (x + 2) % 4, 3 - x)[e]

    def x_copy(e, first_pair, count, offset, sems):
        pair = 4 * mate(e) + first_pair + out
        return remote(ext0.at[:, lanes(pair, edge, count)], ftx.at[lanes(x, width), pl.ds(offset, count * edge)],
                      sems[0].at[e - 1], sems[1].at[e - 1], {"col": y * 4 + mate(e)})

    f_copies = {
        (e, b): x_copy(e, 2 * b, 2, edge + 2 * b * edge, (fx_s.at[b], fx_r.at[b])) for e in (1, 2, 3) for b in range(2)
    }
    lo_copies = {e: x_copy(e, -1, 1, 0, (lo_s, lo_r)) for e in (1, 2, 3)}
    hi_copies = {e: x_copy(e, 4, 1, 5 * edge, (hi_s, hi_r)) for e in (1, 2, 3)}
    inner = pl.ds(edge, part)

    def y_copy(from_slot, to_slot, e, b, count, index, is_up):
        piece = lanes(mate(e), width)
        sems = (up_s, up_r) if is_up else (dn_s, dn_r)
        depth = 2 * b * edge, 2 * count * edge
        if from_slot == 0:
            src = ftx.at[piece, pl.ds(edge + depth[0], depth[1])]
        else:
            src = ft.at[from_slot - 1, piece, pl.ds(*depth)]
        return remote(src, ft.at[to_slot - 1, piece, pl.ds(*depth)], sems[0].at[index], sems[1].at[index],
                      on_y(1 if is_up else 3))

    own_up = {(e, b): y_copy(0, 1, e, b, 1, 2 * e + b, True) for e in range(4) for b in range(2)}
    own_dn = {(e, b): y_copy(0, 2, e, b, 1, 2 * e + b, False) for e in range(4) for b in range(2)}
    fwd_up, fwd_dn = y_copy(1, 3, 0, 0, 2, 8, True), y_copy(2, 3, 1, 0, 2, 8, False)

    def late_rows(i):
        return lanes(2 * (1 - x // 2) + i, width)

    def late_copy(i, is_up):
        sems = (up_s, up_r) if is_up else (dn_s, dn_r)
        depth = pl.ds(0 if is_up else part // 2, part // 2)
        return remote(ft.at[0 if is_up else 1, late_rows(i), depth], ft.at[2, late_rows(i), depth],
                      sems[0].at[9 + i], sems[1].at[9 + i], on_y(1 if is_up else 3))

    late = [[late_copy(i, is_up) for is_up in (True, False)] for i in range(2)]

    def spread(e, b):
        own_up[e, b].start()
        own_dn[e, b].start()

    order = [(1, 0), (3, 0), (1, 1), (3, 1), (2, 0), (2, 1)]
    for key in order:
        f_copies[key].start()
    ftx[lanes(x, width), inner] = ext0[:, lanes(4 * x + out, edge, 4)]
    spread(0, 0)
    spread(0, 1)
    f_up.start()
    f_down.start()
    for key in order:
        f_copies[key].wait_recv()
        spread(*key)
    f_up.wait()
    f_down.wait()
    ext0[:, lanes(out - 1, edge)] = fedge[0]
    ext0[:, lanes(pairs + out, edge)] = fedge[1]
    for e in (1, 3, 2):
        lo_copies[e].start()
        hi_copies[e].start()
    ftx[lanes(x, width), pl.ds(0, edge)] = ext0[:, lanes(4 * x - 1 + out, edge)]
    ftx[lanes(x, width), pl.ds(5 * edge, edge)] = ext0[:, lanes(4 * x + 4 + out, edge)]

    def apply(q):
        rows = pl.ds(q * edge, edge)
        applied = jnp.dot(ftx[:, pl.ds(q * edge, 3 * edge)], band[4 * x + q + out], preferred_element_type=jnp.float32)
        aown[rows, :] = applied.astype(jnp.bfloat16).T

    def parts(j):
        return range(2 if j == 3 else 1)

    def part_rows(j, i):
        return pl.ds(i * width, width) if j == 3 else pl.ds(0, half)

    core_copies = {
        (j, m, i): remote(away.at[j, m, part_rows(j, i)], core_in.at[j, m, part_rows(j, i)], core_s.at[j, m, i],
                          core_r.at[j, m, i], partner)
        for j in range(4) for m in range(2) for i in parts(j)
    }
    owner = (y - z + 4) % 4
    far = owner >= 2

    over_z_first = [(0, 0), (1, 0)]
    x_copies = {
        (j, m, i): [
            remote(share.at[j, m, part_rows(j, i), lanes((x + d) % 4, width)], x_in.at[j, d - 1, m, part_rows(j, i)],
                   x_s.at[j, m, i, d - 1], x_r.at[j, m, i, d - 1], on_x(d))
            for d in (1, 2, 3)
        ]
        for j in range(4) for m in range(2) for i in parts(j) if (j, m) not in over_z_first
    }
    kx_copies = [
        remote(ksum.at[:, lanes((x + d) % 4, width)], kx_in.at[d - 1], kx_s.at[d - 1], kx_r.at[d - 1], on_x(d))
        for d in (1, 2, 3)
    ]

    def to_owner(j):
        return (y + (0, 3, 1, 2)[j] - z + 4) % 4

    def z_copy(j, m, i):
        d = to_owner(j)
        if (j, m) in over_z_first:
            return d, remote(share.at[j, 0], zin.at[d], zk_s.at[j], zk_r.at[d], on_z(d))
        rows = part_rows(j, i)
        return d, remote(done.at[j, m, rows], fin.at[d, m, rows], z_s.at[j, m, i], z_r.at[d, m, i], on_z(d))

    def send_over_z(j, m, i):
        d, copy = z_copy(j, m, i)

        @pl.when(d != 0)
        def _():
            copy.start()

        @pl.when(d == 0)
        def _():
            if (j, m) in over_z_first:
                zin[0] = share[j, 0]
            else:
                fin[0, m, part_rows(j, i), :] = done[j, m, part_rows(j, i), :]

    def place_product(j, m, target_k, product, rows, sent):
        @pl.when(target_k == k)
        def _():
            keep[j, m, rows, :] = product

        @pl.when(target_k != k)
        def _():
            away[j, m, rows, :] = product.astype(jnp.bfloat16)
            for i in sent:
                core_copies[j, m, i].start()

    def half_tile(j, g, products=(0, 1)):
        target_k = x // 2 if g == 0 else 1 - x // 2
        rows = lanes(target_k, half)
        lhs = ftx[rows, inner] if j == 0 else ft[j - 1, rows, :]
        for m in products:
            product = jnp.dot(lhs, (aown, fown)[m][...], preferred_element_type=jnp.float32)
            place_product(j, m, target_k, product, pl.ds(0, half), parts(j))

    def late_quarter(i):
        lhs = ft[2, late_rows(i), :]
        for m, rhs in enumerate((aown, fown)):
            product = jnp.dot(lhs, rhs[...], preferred_element_type=jnp.float32)
            place_product(3, m, 1 - x // 2, product, part_rows(3, i), [i])

    def tile(j, products=(0, 1)):
        half_tile(j, 0, products)
        half_tile(j, 1, products)

    def over_core(j, i=0, products=(0, 1)):
        rows = part_rows(j, i)
        for m in products:
            core_copies[j, m, i].wait_recv()
            share[j, m, rows, :] = (keep[j, m, rows, :] + core_in[j, m, rows, :].astype(jnp.float32)).astype(jnp.bfloat16)
            if (j, m) in over_z_first:
                send_over_z(j, m, i)
            else:
                for copy in x_copies[j, m, i]:
                    copy.start()

    def add_up(first, rest):
        total = first.astype(jnp.float32)
        for term in rest:
            total = total + term.astype(jnp.float32)
        return total

    def over_x(j, i=0):
        rows = part_rows(j, i)
        for m in range(2):
            if (j, m) in over_z_first:
                continue
            for copy in x_copies[j, m, i]:
                copy.wait_recv()
            total = add_up(share[j, m, rows, lanes(x, width)], [x_in[j, n, m, rows, :] for n in range(3)])
            done[j, m, rows, :] = total.astype(jnp.bfloat16)
            send_over_z(j, m, i)

    for q in range(4):
        fown[pl.ds(q * edge, edge), :] = ftx[:, pl.ds((q + 1) * edge, edge)].T
    tile(0, (1,))
    for e in (0, 1, 3):
        for b in range(2):
            own_up[e, b].wait_recv()
            own_dn[e, b].wait_recv()
    fwd_up.start()
    fwd_dn.start()
    over_core(0, 0, (1,))
    apply(1)
    apply(2)
    for b in range(2):
        own_up[2, b].wait_recv()
        own_dn[2, b].wait_recv()
    for i in range(2):
        for copy in late[i]:
            copy.start()
    for e in (1, 3, 2):
        lo_copies[e].wait_recv()
        hi_copies[e].wait_recv()
    apply(0)
    apply(3)
    tile(0, (0,))
    tile(1)
    over_core(0, 0, (0,))
    tile(2)
    over_core(1)
    over_x(0)
    over_core(2)
    fwd_up.wait_recv()
    fwd_dn.wait_recv()
    half_tile(3, 0)

    @pl.when(x // 2 == k)
    def _():
        over_core(3, 0)
        over_core(3, 1)

    over_x(1)
    for i in range(2):
        for copy in late[i]:
            copy.wait_recv()
        late_quarter(i)

        @pl.when(x // 2 != k)
        def _():
            over_core(3, i)

    over_x(2)

    @pl.when(jnp.logical_not(far))
    def _():
        for d in (1, 2, 3):
            remote(share.at[0, 0], zin.at[d], zk_s.at[0], zk_r.at[d], on_z(d)).wait_recv()
        ksum[...] = add_up(zin[0], [zin[d] for d in (1, 2, 3)]).astype(jnp.bfloat16)
        for copy in kx_copies:
            copy.start()

    over_x(3, 0)
    over_x(3, 1)

    def owned(m):
        @pl.when(owner == 2)
        def _():
            for d in (1, 2, 3):
                for i in range(2):
                    rows = part_rows(3, i)
                    remote(done.at[3, m, rows], fin.at[d, m, rows], z_s.at[3, m, i], z_r.at[d, m, i], on_z(d)).wait_recv()

        @pl.when(owner != 2)
        def _():
            for d in (1, 2, 3):
                remote(done.at[0, m], fin.at[d, m], z_s.at[0, m, 0], z_r.at[d, m, 0], on_z(d)).wait_recv()

        return add_up(fin[0, m], [fin[d, m] for d in (1, 2, 3)])

    @pl.when(jnp.logical_not(far))
    def _():
        for copy in kx_copies:
            copy.wait_recv()
        sums[0] = add_up(ksum[:, lanes(x, width)], [kx_in[i] for i in range(3)])

    @pl.when(far)
    def _():
        sums[0] = owned(0)

    sums[1] = owned(1)

    for h in range(2):
        for copy in (*stage1[h], *(c for copies in stage2[h] for c in copies)):
            copy.wait_send()
        for p in range(out):
            tile_up(p + pairs - out, h).wait_send()
        for p in range(out - 1):
            tile_down(p, h).wait_send()
    for p in range(out):
        vector_up(p + pairs - out).wait_send()
        vector_down(p).wait_send()
    for copy in (*v_copies, *f_copies.values(), *lo_copies.values(), *hi_copies.values(), *own_up.values(),
                 *own_dn.values(), fwd_up, fwd_dn, *late[0], *late[1], *core_copies.values(),
                 *(c for cs in x_copies.values() for c in cs)):
        copy.wait_send()
    for j in range(4):
        for m, i in [(m, i) for m in range(2) for i in parts(j)]:
            d, copy = z_copy(j, m, i)

            @pl.when(d != 0)
            def _():
                copy.wait_send()

    @pl.when(jnp.logical_not(far))
    def _():
        for copy in kx_copies:
            copy.wait_send()


def body(vectors, block_count, block_cols, blocks):
    n_row = lax.axis_size("row")
    n_col = lax.axis_size("col")
    edge, columns = vectors.shape
    local_blocks, slots, blk, _ = blocks.shape
    width = columns // n_col
    scale = 1.0 / math.sqrt(edge * n_row * n_col)
    wide, half, part = 4 * width, 2 * width, 4 * edge
    reach = n_col + 2 * REACH_IN
    anywhere = pl.BlockSpec(memory_space=pl.ANY)
    vmem = pl.BlockSpec(memory_space=pltpu.VMEM)
    bf16 = jnp.bfloat16
    dma = pltpu.SemaphoreType.DMA
    sums = pl.pallas_call(
        functools.partial(kernel, n_row, local_blocks * n_row * n_col),
        out_shape=jax.ShapeDtypeStruct((2, half, width), jnp.float32),
        in_specs=[anywhere] * 4,
        out_specs=vmem,
        scratch_shapes=[
            pltpu.SMEM(block_cols.shape, jnp.int32),
            pltpu.SMEM(block_count.shape, jnp.int32),
            pltpu.VMEM(blocks.shape, bf16),
            pltpu.VMEM((reach - 1, 2, 3, blk, blk), bf16),
            pltpu.VMEM((reach, 6 * blk, edge), bf16),
            pltpu.VMEM((reach, edge, width), bf16),
            pltpu.VMEM((width, reach * edge), bf16),
            pltpu.VMEM((width, reach * edge), bf16),
            pltpu.VMEM((wide, part + 2 * edge), bf16),
            pltpu.VMEM((3, wide, part), bf16),
            pltpu.VMEM((part, wide), bf16),
            pltpu.VMEM((part, wide), bf16),
            pltpu.VMEM((4, 2, half, wide), bf16),
            pltpu.VMEM((4, 2, half, wide), jnp.float32),
            pltpu.VMEM((4, 2, half, wide), bf16),
            pltpu.VMEM((4, 2, half, wide), bf16),
            pltpu.VMEM((4, 3, 2, half, width), bf16),
            pltpu.VMEM((4, 2, half, width), bf16),
            pltpu.VMEM((4, 2, half, width), bf16),
            pltpu.VMEM((4, half, wide), bf16),
            pltpu.VMEM((half, wide), bf16),
            pltpu.VMEM((3, half, width), bf16),
            pltpu.VMEM((2, width, edge), bf16),
            dma((4,)),
            dma((16,)), dma((16,)), dma((2, REACH_IN)), dma((2, REACH_IN)),
            dma((2, 3)), dma((2, 3)), dma((2, 4, 3)), dma((2, 4, 3)),
            dma((REACH_IN, 2)), dma((REACH_IN, 2)), dma((REACH_IN - 1, 2)), dma((REACH_IN - 1, 2)),
            dma((2, 3)), dma((2, 3)), dma((3,)), dma((3,)), dma((3,)), dma((3,)),
            dma((11,)), dma((11,)), dma((11,)), dma((11,)),
            dma((4, 2, 2)), dma((4, 2, 2)), dma((4, 2, 2, 3)), dma((4, 2, 2, 3)), dma((4, 2, 2)), dma((4, 2, 2)),
            dma((2,)), dma((4,)), dma((3,)), dma((3,)), dma((2,)), dma((2,)),
        ],
        compiler_params=pltpu.CompilerParams(
            collective_id=0, has_side_effects=True, vmem_limit_bytes=58 * 1024 * 1024
        ),
    )(block_cols, block_count, blocks, vectors)
    return (sums[0] * scale, sums[1] * scale)


def solution(mesh):
    in_specs = (
        P(("row", "col"), None),
        P(("row", "col")),
        P(("row", "col"), None),
        P(("row", "col"), None, None, None),
    )
    out_specs = (P("row", "col"), P("row", "col"))
    return jax.shard_map(body, mesh=mesh, in_specs=in_specs, out_specs=out_specs, check_vma=False)
```

```python
import functools
import math

import jax
import jax.numpy as jnp
from jax import lax
from jax.experimental import pallas as pl
from jax.experimental.pallas import tpu as pltpu
from jax.sharding import PartitionSpec as P

DEGREE = 8
REACH_IN = DEGREE
MESH = pl.DeviceIdType.MESH

filter_center = 0.25
filter_half = 1.75


def kernel(n_row, total_blocks, cols_hbm, count_hbm, blocks_hbm, v_ref, sums,
           cols_ref, count_ref, blocks_ref, hg, band, vland, ext0, ext1, ftx, ft, aown, fown,
           away, keep, core_in, share, x_in, done, fin, zin, ksum, kx_in, fedge,
           in_sem, v_s, v_r, vh_s, vh_r, h1_s, h1_r, h2_s, h2_r, eu_s, eu_r, ed_s, ed_r,
           fx_s, fx_r, lo_s, lo_r, hi_s, hi_r, up_s, up_r, dn_s, dn_r, core_s, core_r, x_s, x_r, z_s, z_r,
           zk_s, zk_r, kx_s, kx_r, fe_s, fe_r):
    edge = v_ref.shape[0]
    blk = edge // 2
    pairs = 16
    out = REACH_IN
    row, col = lax.axis_index("row"), lax.axis_index("col")
    z, k, y, x = row // 2, row % 2, col // 4, col % 4
    up, down = {"row": (row + 1) % n_row}, {"row": (row + n_row - 1) % n_row}
    partner = {"row": z * 2 + 1 - k}
    across = {"row": (row + n_row - 1 + 2 * k) % n_row}

    def place(dy, dx):
        return ((y + dy) % 4) * 4 + (x + dx) % 4

    def on_x(d):
        return {"col": place(0, d)}

    def on_y(d):
        return {"col": place(d, 0)}

    def on_z(d):
        return {"row": ((z + d) % 4) * 2 + k}

    def remote(src, dst, send, recv, device):
        return pltpu.make_async_remote_copy(
            src_ref=src, dst_ref=dst, send_sem=send, recv_sem=recv, device_id=device, device_id_type=MESH
        )

    def lanes(i, size, count=1):
        return pl.ds(pl.multiple_of(i * size, size), count * size)

    others = [(dy, dx) for dy in range(4) for dx in range(4) if dy or dx]
    barrier = pltpu.get_barrier_semaphore()
    for device in [partner, across, on_z(1), on_z(2), on_z(3)] + [{"col": place(dy, dx)} for dy, dx in others]:
        pl.semaphore_signal(barrier, inc=1, device_id=device, device_id_type=MESH)

    fetch = [
        pltpu.make_async_copy(cols_hbm, cols_ref, in_sem.at[0]),
        pltpu.make_async_copy(count_hbm, count_ref, in_sem.at[1]),
        pltpu.make_async_copy(blocks_hbm, blocks_ref, in_sem.at[2]),
        pltpu.make_async_copy(v_ref.at[:, lanes(col, blk)], vland.at[col + out], in_sem.at[3]),
    ]
    for copy in fetch:
        copy.start()
    for copy in fetch[:3]:
        copy.wait()

    first = (row * pairs + col) * 2
    for i in range(2):
        for offset in range(3):
            tile = jnp.zeros((blk, blk), jnp.bfloat16)
            for slot in range(5):
                relative = lax.rem(cols_ref[i, slot] - first - i + total_blocks, total_blocks)
                hit = jnp.logical_and(relative == offset, slot < count_ref[i])
                tile = jnp.where(hit, blocks_ref[i, slot], tile)
            hg[col + out, i, offset] = tile

    pl.semaphore_wait(barrier, 20)

    def where(h, a, b):
        return place(b, a) if h == 0 else place(a, b)

    def tile_copy(h, a, b, to_a, to_b, send, recv):
        unit = hg.at[where(h, a, b) + out, h]
        return remote(unit, unit, send, recv, {"col": where(h, to_a, to_b)})

    stage1, stage2 = [], []
    for h in range(2):
        sign = 1 if h == 0 else 3
        moves = [(0, 1), (0, 3), (4 - sign, sign)]
        stage1.append([tile_copy(h, a, 0, to, 0, h1_s.at[h, n], h1_r.at[h, n]) for n, (a, to) in enumerate(moves)])
        lists = []
        for a in range(4):
            sign = 1 if a < 2 else 3
            moves = [(0, 1), (0, 3), (4 - sign, sign)]
            lists.append([
                tile_copy(h, a, b, 0, to, h2_s.at[h, a, n], h2_r.at[h, a, n]) for n, (b, to) in enumerate(moves)
            ])
        stage2.append(lists)

    v_copies = [
        remote(v_ref.at[:, lanes(place(dy, dx), blk)], vland.at[col + out], v_s.at[dy * 4 + dx],
               v_r.at[dy * 4 + dx], {"col": place(dy, dx)})
        for dy, dx in others
    ]

    def tile_up(p, h):
        return remote(hg.at[p + out, h], hg.at[p + out - pairs, h], eu_s.at[p + out - pairs, h],
                      eu_r.at[p + out - pairs, h], up)

    def tile_down(p, h):
        return remote(hg.at[p + out, h], hg.at[p + out + pairs, h], ed_s.at[p, h], ed_r.at[p, h], down)

    def pass_on(h, a, b):
        p = where(h, a, b)

        @pl.when(p >= pairs - out)
        def _():
            tile_up(p, h).start()

        @pl.when(p < out - 1)
        def _():
            tile_down(p, h).start()

    def vector_up(p):
        return remote(vland.at[p + out], vland.at[p + out - pairs], vh_s.at[0, p + out - pairs],
                      vh_r.at[0, p + out - pairs], up)

    def vector_down(p):
        return remote(vland.at[p + out], vland.at[p + out + pairs], vh_s.at[1, p], vh_r.at[1, p], down)

    def pass_vector(dy, dx):
        if dy or dx:
            v_copies[others.index((dy, dx))].wait_recv()
        else:
            fetch[3].wait()
        p = place(4 - dy, 4 - dx)

        @pl.when(p >= pairs - out)
        def _():
            vector_up(p).start()

        @pl.when(p < out)
        def _():
            vector_down(p).start()

    def scatter(slot, h):
        def put(s, r, c, value):
            band[s, pl.ds(r * blk, blk), pl.ds(c * blk, blk)] = value

        put(slot, 2 + h, h, hg[slot, h, 0])
        put(slot, 3 + h, h, hg[slot, h, 1].T)
        put(slot, 4 + h, h, hg[slot, h, 2].T)
        put(slot, 5 - 5 * h, h, jnp.zeros((blk, blk), jnp.bfloat16))
        if h == 0:
            put(slot, 2, 1, hg[slot, 0, 1])
            put(slot + 1, 0, 0, hg[slot, 0, 2])
        else:
            put(slot + 1, 1, 0, hg[slot, 1, 1])
            put(slot + 1, 1, 1, hg[slot, 1, 2])

    def scatter_unit(h, a, b):
        scatter(where(h, a, b) + out, h)

    def start_first():
        for h in range(2):
            stage1[h][0].start()
            stage1[h][1].start()

    def start_own():
        for h in range(2):
            stage2[h][0][0].start()
            stage2[h][0][1].start()

    def start_vectors(moves):
        for move in moves:
            v_copies[others.index(move)].start()

    def pass_vectors(moves):
        for dy, dx in moves:
            pass_vector(dy, dx)

    def pass_own():
        for h in range(2):
            pass_on(h, 0, 0)
            scatter_unit(h, 0, 0)

    def take_first():
        for h in range(2):
            for n, a in ((0, 3), (1, 1)):
                stage1[h][n].wait_recv()
                if n == h:
                    stage1[h][2].start()
                stage2[h][a][0].start()
                stage2[h][a][1].start()
                pass_on(h, a, 0)
        for h in range(2):
            scatter_unit(h, 3, 0)
            scatter_unit(h, 1, 0)

    def take_far():
        for h in range(2):
            stage1[h][2].wait_recv()
            stage2[h][2][0].start()
            stage2[h][2][1].start()
            pass_on(h, 2, 0)
        for h in range(2):
            scatter_unit(h, 2, 0)

    def receive(a):
        for h in range(2):
            for n, b in ((0, 3), (1, 1)):
                stage2[h][a][n].wait_recv()
                if n == (0 if a < 2 else 1):
                    stage2[h][a][2].start()
                pass_on(h, a, b)
        for h in range(2):
            scatter_unit(h, a, 3)
            scatter_unit(h, a, 1)

    def receive_far(a):
        for h in range(2):
            stage2[h][a][2].wait_recv()
            pass_on(h, a, 2)
        for h in range(2):
            scatter_unit(h, a, 2)

    def turn(slot):
        ext0[:, lanes(slot, edge)] = vland[slot].T

    near = [(0, 1), (0, 3), (1, 0), (3, 0)]
    middle = [(1, 1), (1, 3), (3, 1), (3, 3), (0, 2), (2, 0)]
    distant = [(1, 2), (3, 2), (2, 1), (2, 3), (2, 2)]

    start_first()
    start_own()
    start_vectors(near)
    pass_own()
    take_first()
    pass_vectors([(0, 0)] + near)
    start_vectors(middle)
    take_far()
    receive(0)
    pass_vectors(middle)
    start_vectors(distant)
    receive(3)
    receive_far(0)
    receive(1)
    receive_far(3)
    pass_vectors(distant)
    receive(2)
    receive_far(1)
    receive_far(2)

    def turn_all(low, high):
        def one(slot, carry):
            turn(slot)
            return carry

        lax.fori_loop(low, high, one, 0)

    turn_all(out, out + pairs)

    def update(step, j):
        source, target = (ext0, ext1) if step % 2 else (ext1, ext0)
        own = lanes(j + out, edge)
        product = jnp.dot(source[:, lanes(j + out - 1, edge, 3)], band[j + out], preferred_element_type=jnp.float32)
        shifted = product - filter_center * source[:, own].astype(jnp.float32)
        if step == 1:
            result = shifted / filter_half
        else:
            result = 2.0 * shifted / filter_half - target[:, own].astype(jnp.float32)
        target[:, own] = result.astype(jnp.bfloat16)

    for step in range(1, DEGREE):
        def inside(j, carry):
            update(step, j)
            return carry

        lax.fori_loop(step, pairs - step, inside, 0, unroll=pairs // 2 - step)

    for p in range(out):
        vector_up(p + pairs - out).wait_recv()
        turn(p)
        vector_down(p).wait_recv()
        turn(p + pairs + out)
    for p in range(out):
        for h in range(2):
            tile_up(p + pairs - out, h).wait_recv()
            scatter(p, h)
            if p < out - 1:
                tile_down(p, h).wait_recv()
                scatter(p + pairs + out, h)

    for step in range(1, DEGREE + 1):
        def outside(i, carry):
            update(step, step - out + i)
            update(step, pairs - step + i)
            return carry

        lax.fori_loop(0, out, outside, 0, unroll=out)

    f_up = remote(ext0.at[:, lanes(pairs - 1 + out, edge)], fedge.at[0], fe_s.at[0], fe_r.at[0], up)
    f_down = remote(ext0.at[:, lanes(out, edge)], fedge.at[1], fe_s.at[1], fe_r.at[1], down)

    part = 4 * edge
    width = blk
    half = 2 * width

    def mate(e):
        return (x, x + 1 - 2 * (x % 2), (x + 2) % 4, 3 - x)[e]

    def x_copy(e, first_pair, count, offset, sems):
        pair = 4 * mate(e) + first_pair + out
        return remote(ext0.at[:, lanes(pair, edge, count)], ftx.at[lanes(x, width), pl.ds(offset, count * edge)],
                      sems[0].at[e - 1], sems[1].at[e - 1], {"col": y * 4 + mate(e)})

    f_copies = {
        (e, b): x_copy(e, 2 * b, 2, edge + 2 * b * edge, (fx_s.at[b], fx_r.at[b])) for e in (1, 2, 3) for b in range(2)
    }
    lo_copies = {e: x_copy(e, -1, 1, 0, (lo_s, lo_r)) for e in (1, 2, 3)}
    hi_copies = {e: x_copy(e, 4, 1, 5 * edge, (hi_s, hi_r)) for e in (1, 2, 3)}
    inner = pl.ds(edge, part)

    def y_copy(from_slot, to_slot, e, b, count, index, is_up):
        piece = lanes(mate(e), width)
        sems = (up_s, up_r) if is_up else (dn_s, dn_r)
        depth = 2 * b * edge, 2 * count * edge
        if from_slot == 0:
            src = ftx.at[piece, pl.ds(edge + depth[0], depth[1])]
        else:
            src = ft.at[from_slot - 1, piece, pl.ds(*depth)]
        return remote(src, ft.at[to_slot - 1, piece, pl.ds(*depth)], sems[0].at[index], sems[1].at[index],
                      on_y(1 if is_up else 3))

    own_up = {(e, b): y_copy(0, 1, e, b, 1, 2 * e + b, True) for e in range(4) for b in range(2)}
    own_dn = {(e, b): y_copy(0, 2, e, b, 1, 2 * e + b, False) for e in range(4) for b in range(2)}
    fwd_up, fwd_dn = y_copy(1, 3, 0, 0, 2, 8, True), y_copy(2, 3, 1, 0, 2, 8, False)

    def late_rows(i):
        return lanes(2 * (1 - x // 2) + i, width)

    def late_copy(i, is_up):
        sems = (up_s, up_r) if is_up else (dn_s, dn_r)
        depth = pl.ds(0 if is_up else part // 2, part // 2)
        return remote(ft.at[0 if is_up else 1, late_rows(i), depth], ft.at[2, late_rows(i), depth],
                      sems[0].at[9 + i], sems[1].at[9 + i], on_y(1 if is_up else 3))

    late = [[late_copy(i, is_up) for is_up in (True, False)] for i in range(2)]

    def spread(e, b):
        own_up[e, b].start()
        own_dn[e, b].start()

    order = [(1, 0), (3, 0), (1, 1), (3, 1), (2, 0), (2, 1)]
    for key in order:
        f_copies[key].start()
    ftx[lanes(x, width), inner] = ext0[:, lanes(4 * x + out, edge, 4)]
    spread(0, 0)
    spread(0, 1)
    f_up.start()
    f_down.start()
    for key in order:
        f_copies[key].wait_recv()
        spread(*key)
    f_up.wait()
    f_down.wait()
    ext0[:, lanes(out - 1, edge)] = fedge[0]
    ext0[:, lanes(pairs + out, edge)] = fedge[1]
    for e in (1, 3, 2):
        lo_copies[e].start()
        hi_copies[e].start()
    ftx[lanes(x, width), pl.ds(0, edge)] = ext0[:, lanes(4 * x - 1 + out, edge)]
    ftx[lanes(x, width), pl.ds(5 * edge, edge)] = ext0[:, lanes(4 * x + 4 + out, edge)]

    def apply(q):
        rows = pl.ds(q * edge, edge)
        applied = jnp.dot(ftx[:, pl.ds(q * edge, 3 * edge)], band[4 * x + q + out], preferred_element_type=jnp.float32)
        aown[rows, :] = applied.astype(jnp.bfloat16).T

    def parts(j):
        return range(2 if j == 3 else 1)

    def part_rows(j, i):
        return pl.ds(i * width, width) if j == 3 else pl.ds(0, half)

    core_copies = {
        (j, m, i): remote(away.at[j, m, part_rows(j, i)], core_in.at[j, m, part_rows(j, i)], core_s.at[j, m, i],
                          core_r.at[j, m, i], partner)
        for j in range(4) for m in range(2) for i in parts(j)
    }
    owner = (y - z + 4) % 4
    far = owner >= 2

    over_z_first = [(0, 0), (1, 0)]
    x_copies = {
        (j, m, i): [
            remote(share.at[j, m, part_rows(j, i), lanes((x + d) % 4, width)], x_in.at[j, d - 1, m, part_rows(j, i)],
                   x_s.at[j, m, i, d - 1], x_r.at[j, m, i, d - 1], on_x(d))
            for d in (1, 2, 3)
        ]
        for j in range(4) for m in range(2) for i in parts(j) if (j, m) not in over_z_first
    }
    kx_copies = [
        remote(ksum.at[:, lanes((x + d) % 4, width)], kx_in.at[d - 1], kx_s.at[d - 1], kx_r.at[d - 1], on_x(d))
        for d in (1, 2, 3)
    ]

    def to_owner(j):
        return (y + (0, 3, 1, 2)[j] - z + 4) % 4

    def z_copy(j, m, i):
        d = to_owner(j)
        if (j, m) in over_z_first:
            return d, remote(share.at[j, 0], zin.at[d], zk_s.at[j], zk_r.at[d], on_z(d))
        rows = part_rows(j, i)
        return d, remote(done.at[j, m, rows], fin.at[d, m, rows], z_s.at[j, m, i], z_r.at[d, m, i], on_z(d))

    def send_over_z(j, m, i):
        d, copy = z_copy(j, m, i)

        @pl.when(d != 0)
        def _():
            copy.start()

        @pl.when(d == 0)
        def _():
            if (j, m) in over_z_first:
                zin[0] = share[j, 0]
            else:
                fin[0, m, part_rows(j, i), :] = done[j, m, part_rows(j, i), :]

    def place_product(j, m, target_k, product, rows, sent):
        @pl.when(target_k == k)
        def _():
            keep[j, m, rows, :] = product

        @pl.when(target_k != k)
        def _():
            away[j, m, rows, :] = product.astype(jnp.bfloat16)
            for i in sent:
                core_copies[j, m, i].start()

    def half_tile(j, g, products=(0, 1)):
        target_k = x // 2 if g == 0 else 1 - x // 2
        rows = lanes(target_k, half)
        lhs = ftx[rows, inner] if j == 0 else ft[j - 1, rows, :]
        for m in products:
            product = jnp.dot(lhs, (aown, fown)[m][...], preferred_element_type=jnp.float32)
            place_product(j, m, target_k, product, pl.ds(0, half), parts(j))

    def late_quarter(i):
        lhs = ft[2, late_rows(i), :]
        for m, rhs in enumerate((aown, fown)):
            product = jnp.dot(lhs, rhs[...], preferred_element_type=jnp.float32)
            place_product(3, m, 1 - x // 2, product, part_rows(3, i), [i])

    def tile(j, products=(0, 1)):
        half_tile(j, 0, products)
        half_tile(j, 1, products)

    def over_core(j, i=0, products=(0, 1)):
        rows = part_rows(j, i)
        for m in products:
            core_copies[j, m, i].wait_recv()
            share[j, m, rows, :] = (keep[j, m, rows, :] + core_in[j, m, rows, :].astype(jnp.float32)).astype(jnp.bfloat16)
            if (j, m) in over_z_first:
                send_over_z(j, m, i)
            else:
                for copy in x_copies[j, m, i]:
                    copy.start()

    def add_up(first, rest):
        total = first.astype(jnp.float32)
        for term in rest:
            total = total + term.astype(jnp.float32)
        return total

    def over_x(j, i=0):
        rows = part_rows(j, i)
        for m in range(2):
            if (j, m) in over_z_first:
                continue
            for copy in x_copies[j, m, i]:
                copy.wait_recv()
            total = add_up(share[j, m, rows, lanes(x, width)], [x_in[j, n, m, rows, :] for n in range(3)])
            done[j, m, rows, :] = total.astype(jnp.bfloat16)
            send_over_z(j, m, i)

    for q in range(4):
        fown[pl.ds(q * edge, edge), :] = ftx[:, pl.ds((q + 1) * edge, edge)].T
    tile(0, (1,))
    for e in (0, 1, 3):
        for b in range(2):
            own_up[e, b].wait_recv()
            own_dn[e, b].wait_recv()
    fwd_up.start()
    fwd_dn.start()
    over_core(0, 0, (1,))
    apply(1)
    apply(2)
    for e in (1, 3, 2):
        lo_copies[e].wait_recv()
        hi_copies[e].wait_recv()
    apply(0)
    apply(3)
    for b in range(2):
        own_up[2, b].wait_recv()
        own_dn[2, b].wait_recv()
    for i in range(2):
        for copy in late[i]:
            copy.start()
    tile(0, (0,))
    tile(1)
    over_core(0, 0, (0,))
    tile(2)
    over_core(1)
    over_x(0)
    over_core(2)
    fwd_up.wait_recv()
    fwd_dn.wait_recv()
    half_tile(3, 0)

    @pl.when(x // 2 == k)
    def _():
        over_core(3, 0)
        over_core(3, 1)

    over_x(1)
    for i in range(2):
        for copy in late[i]:
            copy.wait_recv()
        late_quarter(i)

        @pl.when(x // 2 != k)
        def _():
            over_core(3, i)

    over_x(2)

    @pl.when(jnp.logical_not(far))
    def _():
        for d in (1, 2, 3):
            remote(share.at[0, 0], zin.at[d], zk_s.at[0], zk_r.at[d], on_z(d)).wait_recv()
        ksum[...] = add_up(zin[0], [zin[d] for d in (1, 2, 3)]).astype(jnp.bfloat16)
        for copy in kx_copies:
            copy.start()

    over_x(3, 0)
    over_x(3, 1)

    def owned(m):
        @pl.when(owner == 2)
        def _():
            for d in (1, 2, 3):
                for i in range(2):
                    rows = part_rows(3, i)
                    remote(done.at[3, m, rows], fin.at[d, m, rows], z_s.at[3, m, i], z_r.at[d, m, i], on_z(d)).wait_recv()

        @pl.when(owner != 2)
        def _():
            for d in (1, 2, 3):
                remote(done.at[0, m], fin.at[d, m], z_s.at[0, m, 0], z_r.at[d, m, 0], on_z(d)).wait_recv()

        return add_up(fin[0, m], [fin[d, m] for d in (1, 2, 3)])

    @pl.when(jnp.logical_not(far))
    def _():
        for copy in kx_copies:
            copy.wait_recv()
        sums[0] = add_up(ksum[:, lanes(x, width)], [kx_in[i] for i in range(3)])

    @pl.when(far)
    def _():
        sums[0] = owned(0)

    sums[1] = owned(1)

    for h in range(2):
        for copy in (*stage1[h], *(c for copies in stage2[h] for c in copies)):
            copy.wait_send()
        for p in range(out):
            tile_up(p + pairs - out, h).wait_send()
        for p in range(out - 1):
            tile_down(p, h).wait_send()
    for p in range(out):
        vector_up(p + pairs - out).wait_send()
        vector_down(p).wait_send()
    for copy in (*v_copies, *f_copies.values(), *lo_copies.values(), *hi_copies.values(), *own_up.values(),
                 *own_dn.values(), fwd_up, fwd_dn, *late[0], *late[1], *core_copies.values(),
                 *(c for cs in x_copies.values() for c in cs)):
        copy.wait_send()
    for j in range(4):
        for m, i in [(m, i) for m in range(2) for i in parts(j)]:
            d, copy = z_copy(j, m, i)

            @pl.when(d != 0)
            def _():
                copy.wait_send()

    @pl.when(jnp.logical_not(far))
    def _():
        for copy in kx_copies:
            copy.wait_send()


def body(vectors, block_count, block_cols, blocks):
    n_row = lax.axis_size("row")
    n_col = lax.axis_size("col")
    edge, columns = vectors.shape
    local_blocks, slots, blk, _ = blocks.shape
    width = columns // n_col
    scale = 1.0 / math.sqrt(edge * n_row * n_col)
    wide, half, part = 4 * width, 2 * width, 4 * edge
    reach = n_col + 2 * REACH_IN
    anywhere = pl.BlockSpec(memory_space=pl.ANY)
    vmem = pl.BlockSpec(memory_space=pltpu.VMEM)
    bf16 = jnp.bfloat16
    dma = pltpu.SemaphoreType.DMA
    sums = pl.pallas_call(
        functools.partial(kernel, n_row, local_blocks * n_row * n_col),
        out_shape=jax.ShapeDtypeStruct((2, half, width), jnp.float32),
        in_specs=[anywhere] * 4,
        out_specs=vmem,
        scratch_shapes=[
            pltpu.SMEM(block_cols.shape, jnp.int32),
            pltpu.SMEM(block_count.shape, jnp.int32),
            pltpu.VMEM(blocks.shape, bf16),
            pltpu.VMEM((reach - 1, 2, 3, blk, blk), bf16),
            pltpu.VMEM((reach, 6 * blk, edge), bf16),
            pltpu.VMEM((reach, edge, width), bf16),
            pltpu.VMEM((width, reach * edge), bf16),
            pltpu.VMEM((width, reach * edge), bf16),
            pltpu.VMEM((wide, part + 2 * edge), bf16),
            pltpu.VMEM((3, wide, part), bf16),
            pltpu.VMEM((part, wide), bf16),
            pltpu.VMEM((part, wide), bf16),
            pltpu.VMEM((4, 2, half, wide), bf16),
            pltpu.VMEM((4, 2, half, wide), jnp.float32),
            pltpu.VMEM((4, 2, half, wide), bf16),
            pltpu.VMEM((4, 2, half, wide), bf16),
            pltpu.VMEM((4, 3, 2, half, width), bf16),
            pltpu.VMEM((4, 2, half, width), bf16),
            pltpu.VMEM((4, 2, half, width), bf16),
            pltpu.VMEM((4, half, wide), bf16),
            pltpu.VMEM((half, wide), bf16),
            pltpu.VMEM((3, half, width), bf16),
            pltpu.VMEM((2, width, edge), bf16),
            dma((4,)),
            dma((16,)), dma((16,)), dma((2, REACH_IN)), dma((2, REACH_IN)),
            dma((2, 3)), dma((2, 3)), dma((2, 4, 3)), dma((2, 4, 3)),
            dma((REACH_IN, 2)), dma((REACH_IN, 2)), dma((REACH_IN - 1, 2)), dma((REACH_IN - 1, 2)),
            dma((2, 3)), dma((2, 3)), dma((3,)), dma((3,)), dma((3,)), dma((3,)),
            dma((11,)), dma((11,)), dma((11,)), dma((11,)),
            dma((4, 2, 2)), dma((4, 2, 2)), dma((4, 2, 2, 3)), dma((4, 2, 2, 3)), dma((4, 2, 2)), dma((4, 2, 2)),
            dma((2,)), dma((4,)), dma((3,)), dma((3,)), dma((2,)), dma((2,)),
        ],
        compiler_params=pltpu.CompilerParams(
            collective_id=0, has_side_effects=True, vmem_limit_bytes=58 * 1024 * 1024
        ),
    )(block_cols, block_count, blocks, vectors)
    return (sums[0] * scale, sums[1] * scale)


def solution(mesh):
    in_specs = (
        P(("row", "col"), None),
        P(("row", "col")),
        P(("row", "col"), None),
        P(("row", "col"), None, None, None),
    )
    out_specs = (P("row", "col"), P("row", "col"))
    return jax.shard_map(body, mesh=mesh, in_specs=in_specs, out_specs=out_specs, check_vma=False)
```
